32 devices in a mesh: dp: 8 (over z, y), fsdp: 4 (over x, core).
Axes of the slice: x: 2, y: 2, z: 4, core: 2. Of those that a mesh axis runs over, the one named last changes fastest.
Arguments:
- inputs: bfloat16 [32768, 512], P(('dp', 'fsdp')), may hold values from -8.5 to 8.5
- embedding: bfloat16 [32768, 512], P(('dp', 'fsdp')), may hold values from -6 to 6
- segments: int32 [32, 1024], P(('dp', 'fsdp')), may hold values from 0 to 5, never falling along the last dimension, each value on 1 to 512 neighbouring positions
- routes_first: int32 [32768, 1], P(('dp', 'fsdp')), may hold values from 0 to 3; in each aligned block of 1024 rows (0 to 1023, 1024 to 2047, ...) at most 512 rows name the same one
- routes_second: int32 [32768, 1], P(('dp', 'fsdp')), may hold values from 0 to 3; in each aligned block of 1024 rows (0 to 1023, 1024 to 2047, ...) at most 512 rows name the same one
- cotangent: bfloat16 [32768, 512], P(('dp', 'fsdp')), may hold values from -8.5 to 8.5
- first_gain: bfloat16 [512], P(('dp', 'fsdp')), may hold values from 0.5 to 1.5
- first_bias: bfloat16 [512], P(('dp', 'fsdp')), may hold values from -1.75 to 1.75
- first_router: bfloat16 [1024, 4], P(('dp', 'fsdp')), may hold values from -0.09375 to 0.09375
- first_up: bfloat16 [4, 512, 2048], P(None, ('dp', 'fsdp')), may hold values from -0.25 to 0.25
- first_down: bfloat16 [4, 2048, 512], P(None, ('dp', 'fsdp')), may hold values from -1.5 to 1.5
- attend_gain: bfloat16 [512], P(('dp', 'fsdp')), may hold values from 0.5 to 1.5
- attend_bias: bfloat16 [512], P(('dp', 'fsdp')), may hold values from -1.75 to 1.75
- project_in: bfloat16 [512, 1536], P(('dp', 'fsdp')), may hold values from -0.25 to 0.25
- relative_weight: bfloat16 [512, 512], P(('dp', 'fsdp')), may hold values from -0.25 to 0.25
- content_bias: bfloat16 [512], P(('dp', 'fsdp')), may hold values from -3 to 3
- position_bias: bfloat16 [512], P(('dp', 'fsdp')), may hold values from -3 to 3
- attend_out: bfloat16 [512, 512], P(('dp', 'fsdp')), may hold values from -1.5 to 1.5
- depth_gain: bfloat16 [512], P(('dp', 'fsdp')), may hold values from 0.5 to 1.5
- depth_bias: bfloat16 [512], P(('dp', 'fsdp')), may hold values from -1.75 to 1.75
- gated_in: bfloat16 [512, 1024], P(('dp', 'fsdp')), may hold values from -0.25 to 0.25
- depth_kernel: bfloat16 [15, 512], P(None, ('dp', 'fsdp')), may hold values from -1.5 to 1.5
- batch_gain: bfloat16 [512], P(('dp', 'fsdp')), may hold values from 0.5 to 1.5
- batch_bias: bfloat16 [512], P(('dp', 'fsdp')), may hold values from -1.75 to 1.75
- point_out: bfloat16 [512, 512], P(('dp', 'fsdp')), may hold values from -0.25 to 0.25
- second_gain: bfloat16 [512], P(('dp', 'fsdp')), may hold values from 0.5 to 1.5
- second_bias: bfloat16 [512], P(('dp', 'fsdp')), may hold values from -1.75 to 1.75
- second_router: bfloat16 [1024, 4], P(('dp', 'fsdp')), may hold values from -0.09375 to 0.09375
- second_up: bfloat16 [4, 512, 2048], P(None, ('dp', 'fsdp')), may hold values from -0.25 to 0.25
- second_down: bfloat16 [4, 2048, 512], P(None, ('dp', 'fsdp')), may hold values from -1.5 to 1.5
- final_gain: bfloat16 [512], P(('dp', 'fsdp')), may hold values from 0.5 to 1.5
- final_bias: bfloat16 [512], P(('dp', 'fsdp')), may hold values from -1.75 to 1.75
Outputs:
- result: bfloat16 [32768, 512], P(('dp', 'fsdp'))
- input_gradient: float32 [32768, 512], P(('dp', 'fsdp'))
- first_gain_gradient: float32 [512], P(('dp', 'fsdp'))
- first_bias_gradient: float32 [512], P(('dp', 'fsdp'))
- first_router_gradient: float32 [1024, 4], P(('dp', 'fsdp'))
- first_up_gradient: float32 [4, 512, 2048], P(None, ('dp', 'fsdp'))
- first_down_gradient: float32 [4, 2048, 512], P(None, ('dp', 'fsdp'))
- attend_gain_gradient: float32 [512], P(('dp', 'fsdp'))
- attend_bias_gradient: float32 [512], P(('dp', 'fsdp'))
- project_in_gradient: float32 [512, 1536], P(('dp', 'fsdp'))
- relative_weight_gradient: float32 [512, 512], P(('dp', 'fsdp'))
- content_bias_gradient: float32 [512], P(('dp', 'fsdp'))
- position_bias_gradient: float32 [512], P(('dp', 'fsdp'))
- attend_out_gradient: float32 [512, 512], P(('dp', 'fsdp'))
- depth_gain_gradient: float32 [512], P(('dp', 'fsdp'))
- depth_bias_gradient: float32 [512], P(('dp', 'fsdp'))
- gated_in_gradient: float32 [512, 1024], P(('dp', 'fsdp'))
- depth_kernel_gradient: float32 [15, 512], P(None, ('dp', 'fsdp'))
- batch_gain_gradient: float32 [512], P(('dp', 'fsdp'))
- batch_bias_gradient: float32 [512], P(('dp', 'fsdp'))
- point_out_gradient: float32 [512, 512], P(('dp', 'fsdp'))
- second_gain_gradient: float32 [512], P(('dp', 'fsdp'))
- second_bias_gradient: float32 [512], P(('dp', 'fsdp'))
- second_router_gradient: float32 [1024, 4], P(('dp', 'fsdp'))
- second_up_gradient: float32 [4, 512, 2048], P(None, ('dp', 'fsdp'))
- second_down_gradient: float32 [4, 2048, 512], P(None, ('dp', 'fsdp'))
- final_gain_gradient: float32 [512], P(('dp', 'fsdp'))
- final_bias_gradient: float32 [512], P(('dp', 'fsdp'))
The draws below stay inside these ranges and needn't reach their ends.
Inputs may be any that keep to these rules, and one draw needn't show every extreme that they name: `segments`: in each row the numbers never fall and each utterance holds 1 to 512 frames. `routes_first`: at most 512 of one device's frames name the same expert, and this bound is reached. `routes_second`: at most 512 of one device's frames name the same expert, and this bound is reached.
All inputs are finite; a program needn't handle non-finite values.
Results may differ from the reference program's by a relative error of at most 0.039.
Values may be sent and summed in bfloat16 or wider, within the bound.
No kernel may reach another device: no remote copies, remote signals or barrier semaphores. Data moves between devices by JAX's collectives and lax.ppermute only.
A program may use at most 384 MiB of HBM per device.

```python
import math
import jax
import jax.numpy as jnp
import numpy as np
from jax import lax

D = 512
HEADS = 8
FF = 2048
EXPERTS = 4
KERNEL = 15
TOK_DEV = 1024
HEAD_DIM = 64
CAPACITY = 512
FRAMES = 32768
N_DP = 8
N_FSDP = 4


def add_line(key, noise, lift):
    count = noise.shape[0]
    width = noise.shape[1]
    direction = jnp.clip(jax.random.normal(key, (width,), jnp.float32), -3.0, 3.0)
    place = jnp.arange(count).astype(jnp.float32) / count
    return noise + lift * place[:, None] * direction[None, :]


def draw_inputs(key, part):
    key = jax.random.fold_in(key, 7)
    noise_key, line_key = jax.random.split(key)
    noise = jnp.clip(jax.random.normal(noise_key, (FRAMES, D), jnp.float32), -4.0, 4.0)
    lift = 1.5
    return add_line(line_key, noise, lift).astype(jnp.bfloat16)


def draw_cotangent(key, part):
    key = jax.random.fold_in(key, 13)
    noise_key, line_key = jax.random.split(key)
    noise = jnp.clip(jax.random.normal(noise_key, (FRAMES, D), jnp.float32), -4.0, 4.0)
    lift = 1.5
    return add_line(line_key, noise, lift).astype(jnp.bfloat16)


def levels(stream_key, extent, cuts, smallest, high):
    level, own = 1.0, jax.random.fold_in(stream_key, 6)
    for axis_at, parts in cuts:
        heights = jnp.exp(jax.random.uniform(jax.random.fold_in(own, axis_at), (parts,), jnp.float32, smallest / len(cuts), high / len(cuts)))
        level = level * jnp.repeat(heights, extent[axis_at] // parts).reshape([-1 if axis == axis_at else 1 for axis in range(len(extent))])
    return level


def profile(amount, total, most, lean):
    portions = [(1 << 20) // math.isqrt(standing ** lean) + 1 for standing in range(2, amount + 1)]
    rest, given = total - most - (amount - 1), [1] * (amount - 1)
    while rest > 0:
        free = [i for i in range(amount - 1) if given[i] < most]
        whole, budget = sum([portions[i] for i in free]), rest
        for i in free:
            extra = min(most - given[i], max(1, budget * portions[i] // whole), rest)
            given[i] = given[i] + extra
            rest = rest - extra
    return np.array([most] + given)


def uneven(rng, count, total, most, skew):
    if count == 2:
        one = jax.random.randint(rng, (), max(1, total - most), min(most, total - 1) + 1)
        return jnp.stack([one, total - one])
    tallies = jnp.asarray(profile(count, total, most, skew), jnp.int32)
    pairs = (count - 1) // 2
    giver, taker = tallies[1:1 + 2 * pairs:2], tallies[2:2 + 2 * pairs:2]
    room = jnp.minimum(giver - 1, most - taker)
    moved = jax.random.randint(jax.random.fold_in(rng, 1), (pairs,), 0, 1 << 20) % (room + 1)
    tallies = tallies.at[1:1 + 2 * pairs:2].set(giver - moved).at[2:2 + 2 * pairs:2].set(taker + moved)
    return tallies[jax.random.permutation(jax.random.fold_in(rng, 2), count)]


def assign_block(rng, own, number, rows, number_of, top, bound, lean):
    ranking = jax.random.permutation(rng, number_of)
    crowded, ordinary = load_shares(number_of, rows * top, bound, lean, True), load_shares(number_of, rows * top, bound, lean, False)
    places = jnp.arange(number_of)

    def named(sizes, turn):
        used = int((sizes > 0).sum())
        fixed = max(1, used // 4)
        moved = fixed + (places - fixed + turn * (used - fixed)) % max(1, number_of - fixed)
        return jnp.zeros((number_of,), jnp.int32).at[ranking[jnp.where(places < fixed, places, moved)]].set(jnp.asarray(sizes, jnp.int32))

    sizes = jnp.where(number % 4 == 0, named(crowded, number // 4), named(ordinary, number - number // 4 - 1))
    mixed = jax.random.permutation(jax.random.fold_in(own, 3), number_of)
    giver, receiver = mixed[0:number_of // 2 * 2:2], mixed[1:number_of // 2 * 2:2]
    room = jnp.minimum(sizes[giver] - 1, bound - sizes[receiver]) // 2
    room = jnp.where((giver == ranking[0]) | (receiver == ranking[0]) | (sizes[receiver] == 0), 0, jnp.maximum(room, 0))
    moved = jax.random.randint(jax.random.fold_in(own, 4), (number_of // 2,), 0, 1 << 20) % (room + 1)
    sizes = sizes.at[giver].add(-moved).at[receiver].add(moved)
    items = jnp.searchsorted(jnp.cumsum(sizes), jnp.arange(rows * top), side="right").astype(jnp.int32)
    listing = items.reshape(top, rows).T
    listing = listing[jax.random.permutation(jax.random.fold_in(own, 1), rows)]
    turn = jax.random.randint(jax.random.fold_in(own, 2), (rows, 1), 0, top)
    return jnp.take_along_axis(listing, (jnp.arange(top)[None, :] + turn) % top, axis=1)


def load_shares(count, total, limit, slope, full):
    loads = [(1 << 20) // math.isqrt(rank ** slope) + 1 for rank in range(1, count + 1)]
    largest = limit if full else min(limit, max(-(-total // count), total * loads[0] // sum(loads)))
    least = 1 if total - largest >= count - 1 else 0
    counts, spare = [largest] + [least] * (count - 1), total - largest - least * (count - 1)
    while spare > 0:
        candidates = [i for i in range(1, count) if counts[i] < largest] or [i for i in range(1, count) if counts[i] < limit]
        mass, remaining = sum([loads[i] for i in candidates]), spare
        for i in candidates:
            extra = min(limit - counts[i], max(1, remaining * loads[i] // mass), spare)
            counts[i] = counts[i] + extra
            spare = spare - extra
    return np.array(counts)


def centred(rng, dims, scale, limit, cuts=(), held_as=jnp.bfloat16):
    loudness = levels(rng, dims, cuts, -0.22, 0.18) if cuts else 1.0
    result = jax.random.normal(rng, dims, jnp.float32) * scale * loudness
    return jnp.minimum(jnp.maximum(result, -limit), limit).astype(held_as)


def setup_inputs(seed: int = 0) -> dict:
    key_of = jax.random.split(jax.random.key(seed), 33)
    inputs = draw_inputs(jax.random.fold_in(key_of[32], 71), 0)
    embedding = centred(key_of[1], (FRAMES, D), 1.0, 6.0, ((0, 32),))
    segments = jax.vmap(lambda own: jnp.searchsorted(jnp.cumsum(uneven(own, 6, TOK_DEV, TOK_DEV // 2, 1)), jnp.arange(TOK_DEV), side="right"))(jax.random.split(key_of[2], (N_DP * N_FSDP))).reshape((N_DP * N_FSDP, TOK_DEV)).astype(jnp.int32)
    routes_first_keys = jax.random.split(jax.random.fold_in(key_of[3], 1), FRAMES // TOK_DEV)
    routes_first_turns = jax.random.permutation(jax.random.fold_in(key_of[3], 3), FRAMES // TOK_DEV)
    routes_first = jax.vmap(lambda own, number: assign_block(jax.random.fold_in(key_of[3], 2), own, number, TOK_DEV, EXPERTS, 1, CAPACITY, 1))(routes_first_keys, routes_first_turns).reshape((FRAMES, 1))
    routes_second_keys = jax.random.split(jax.random.fold_in(key_of[4], 1), FRAMES // TOK_DEV)
    routes_second_turns = jax.random.permutation(jax.random.fold_in(key_of[4], 3), FRAMES // TOK_DEV)
    routes_second = jax.vmap(lambda own, number: assign_block(jax.random.fold_in(key_of[4], 2), own, number, TOK_DEV, EXPERTS, 1, CAPACITY, 1))(routes_second_keys, routes_second_turns).reshape((FRAMES, 1))
    cotangent = draw_cotangent(jax.random.fold_in(key_of[32], 71), 0)
    first_gain = jnp.clip(1.0 + 0.1 * jax.random.normal(key_of[6], (D,), jnp.float32), 0.5, 1.5).astype(jnp.bfloat16)
    first_bias = centred(key_of[7], (D,), 0.3, 1.75, ((0, 32),))
    first_router = centred(key_of[8], (2 * D, EXPERTS), (8 * D) ** -0.5, 0.09375, ((0, 32),))
    first_up = centred(key_of[9], (EXPERTS, D, FF), D ** -0.5, 0.25, ((1, 32),))
    first_down = centred(key_of[10], (EXPERTS, FF, D), (FF // 128) ** -0.5, 1.5, ((1, 32),))
    attend_gain = jnp.clip(1.0 + 0.1 * jax.random.normal(key_of[11], (D,), jnp.float32), 0.5, 1.5).astype(jnp.bfloat16)
    attend_bias = centred(key_of[12], (D,), 0.3, 1.75, ((0, 32),))
    project_in = centred(key_of[13], (D, 3 * D), D ** -0.5, 0.25, ((0, 32),))
    relative_weight = centred(key_of[14], (D, D), D ** -0.5, 0.25, ((0, 32),))
    content_bias = centred(key_of[15], (D,), 0.5, 3.0, ((0, 32),))
    position_bias = centred(key_of[16], (D,), 0.5, 3.0, ((0, 32),))
    attend_out = centred(key_of[17], (D, D), (D // 32) ** -0.5, 1.5, ((0, 32),))
    depth_gain = jnp.clip(1.0 + 0.1 * jax.random.normal(key_of[18], (D,), jnp.float32), 0.5, 1.5).astype(jnp.bfloat16)
    depth_bias = centred(key_of[19], (D,), 0.3, 1.75, ((0, 32),))
    gated_in = centred(key_of[20], (D, 2 * D), D ** -0.5, 0.25, ((0, 32),))
    depth_kernel = centred(key_of[21], (KERNEL, D), KERNEL ** -0.5, 1.5, ((1, 32),))
    batch_gain = jnp.clip(1.0 + 0.1 * jax.random.normal(key_of[22], (D,), jnp.float32), 0.5, 1.5).astype(jnp.bfloat16)
    batch_bias = centred(key_of[23], (D,), 0.3, 1.75, ((0, 32),))
    point_out = centred(key_of[24], (D, D), D ** -0.5, 0.25, ((0, 32),))
    second_gain = jnp.clip(1.0 + 0.1 * jax.random.normal(key_of[25], (D,), jnp.float32), 0.5, 1.5).astype(jnp.bfloat16)
    second_bias = centred(key_of[26], (D,), 0.3, 1.75, ((0, 32),))
    second_router = centred(key_of[27], (2 * D, EXPERTS), (8 * D) ** -0.5, 0.09375, ((0, 32),))
    second_up = centred(key_of[28], (EXPERTS, D, FF), D ** -0.5, 0.25, ((1, 32),))
    second_down = centred(key_of[29], (EXPERTS, FF, D), (FF // 128) ** -0.5, 1.5, ((1, 32),))
    final_gain = jnp.clip(1.0 + 0.1 * jax.random.normal(key_of[30], (D,), jnp.float32), 0.5, 1.5).astype(jnp.bfloat16)
    final_bias = centred(key_of[31], (D,), 0.3, 1.75, ((0, 32),))
    return dict(inputs=inputs, embedding=embedding, segments=segments, routes_first=routes_first, routes_second=routes_second, cotangent=cotangent, first_gain=first_gain, first_bias=first_bias, first_router=first_router, first_up=first_up, first_down=first_down, attend_gain=attend_gain, attend_bias=attend_bias, project_in=project_in, relative_weight=relative_weight, content_bias=content_bias, position_bias=position_bias, attend_out=attend_out, depth_gain=depth_gain, depth_bias=depth_bias, gated_in=gated_in, depth_kernel=depth_kernel, batch_gain=batch_gain, batch_bias=batch_bias, point_out=point_out, second_gain=second_gain, second_bias=second_bias, second_router=second_router, second_up=second_up, second_down=second_down, final_gain=final_gain, final_bias=final_bias)


@jax.custom_vjp
def low(v):
    return lax.optimization_barrier(v.astype(jnp.bfloat16)).astype(jnp.float32)

@jax.custom_vjp
def low_back(v):
    return v

def low_keep(v):
    return (low(v), None)

def low_pass(kept, grad):
    return (grad,)

def back_keep(v):
    return (v, None)

def back_low(kept, grad):
    return (low(grad),)
low.defvjp(low_keep, low_pass)
low_back.defvjp(back_keep, back_low)
eps = 1e-05

def product(left, right):
    return jnp.dot(left, right, precision=lax.Precision.HIGHEST)

def layer_norm(value, gain, bias):
    average = lax.optimization_barrier(jnp.mean(value, -1, keepdims=True))
    centered = value - average
    spread = lax.optimization_barrier(jnp.mean(centered * centered, -1, keepdims=True))
    return centered * lax.rsqrt(spread + eps) * gain + bias

def swish(value):
    return value * jax.nn.sigmoid(value)

def position_table(length, width):
    steps = jnp.arange(2 * length - 1).astype(jnp.float32)
    distance = length - 1 - steps
    freqs = jnp.exp(jnp.arange(0, width, 2).astype(jnp.float32) * (-jnp.log(10000.0) / width))
    angle = distance[:, None] * freqs[None, :]
    return jnp.stack([jnp.sin(angle), jnp.cos(angle)], -1).reshape(2 * length - 1, width)

def shift_rows(wide, count, keys):
    heads = wide.shape[0]
    span = wide.shape[2]
    flat = wide.reshape(heads, count * span)
    flat = lax.slice_in_dim(flat, count - 1, count - 1 + count * (span - 1), axis=1)
    return flat.reshape(heads, count, span - 1)[:, :, :keys]

def expert_row(resid, embed_row, route, gain, bias, router, up_weight, down_weight):
    normed = low(layer_norm(resid, gain, bias))
    logits = product(jnp.concatenate([normed, embed_row], 1), router)
    chances = jax.nn.softmax(logits, -1)
    chosen = (route[:, None] == jnp.arange(EXPERTS)[None, :]).astype(jnp.float32)
    gate = lax.optimization_barrier(jnp.sum(chances * chosen, 1))
    total = jnp.zeros_like(resid)
    for expert in range(EXPERTS):
        inner = low_back(product(normed, up_weight[expert]))
        active = low(swish(inner))
        total = total + chosen[:, expert:expert + 1] * product(active, down_weight[expert])
    return resid + 0.5 * gate[:, None] * low_back(total)

def attention_row(resid, segment, gain, bias, project_in, relative_weight, content_bias, position_bias, attend_out):
    length = resid.shape[0]
    normed = low(layer_norm(resid, gain, bias))
    mixed = low_back(product(normed, project_in))
    query = mixed[:, :D].reshape(length, HEADS, HEAD_DIM)
    keys = low(mixed[:, D:2 * D].reshape(length, HEADS, HEAD_DIM))
    values = low(mixed[:, 2 * D:].reshape(length, HEADS, HEAD_DIM))
    query_u = low(query + content_bias.reshape(HEADS, HEAD_DIM))
    query_v = low(query + position_bias.reshape(HEADS, HEAD_DIM))
    table = low(position_table(length, D))
    relpos = low(low_back(product(table, relative_weight))).reshape(2 * length - 1, HEADS, HEAD_DIM)
    content = jnp.einsum('ihe,jhe->hij', query_u, keys, precision=lax.Precision.HIGHEST)
    wide = jnp.einsum('ihe,mhe->him', query_v, relpos, precision=lax.Precision.HIGHEST)
    scores = low_back(content + shift_rows(wide, length, length)) * HEAD_DIM ** (-0.5)
    same = segment[:, None] == segment[None, :]
    scores = jnp.where(same[None], scores, -1000000000.0)
    chances = low(jax.nn.softmax(scores, -1))
    context = jnp.einsum('hij,jhe->ihe', chances, values, precision=lax.Precision.HIGHEST).reshape(length, D)
    context = low(low_back(context))
    return resid + low_back(product(context, attend_out))

def depthwise(glu, segment, kernel):
    half = KERNEL // 2
    length = glu.shape[0]
    padded = jnp.pad(glu, ((half, half), (0, 0)))
    padded_seg = jnp.pad(segment, (half, half), constant_values=-1)
    total = jnp.zeros_like(glu)
    for index_tap in range(KERNEL):
        same = padded_seg[index_tap:index_tap + length] == segment
        total = total + kernel[index_tap] * jnp.where(same[:, None], padded[index_tap:index_tap + length], 0.0)
    return total

def conv_front(resid, segment, gain, bias, gated_in, kernel):
    normed = low(layer_norm(resid, gain, bias))
    joined = low_back(product(normed, gated_in))
    glu = joined[:, :D] * jax.nn.sigmoid(joined[:, D:])
    return depthwise(glu, segment, kernel)

def conv_tail(resid, depth, average, spread, batch_gain, batch_bias, point_out):
    shifted = (depth - average) * lax.rsqrt(spread + eps) * batch_gain + batch_bias
    return resid + low_back(product(low(swish(shifted)), point_out))

def layer_forward(flat_inputs, embed_rows, segments, first_routes, second_routes, params):
    first_gain, first_bias, first_router, first_up, first_down, attend_gain, attend_bias, project_in, relative_weight, content_bias, position_bias, attend_out, depth_gain, depth_bias, gated_in, depth_kernel, batch_gain, batch_bias, point_out, second_gain, second_bias, second_router, second_up, second_down, final_gain, final_bias = params
    frame_rows = flat_inputs.reshape(-1, TOK_DEV, D)

    def first_block(item):
        return expert_row(item[0], item[1], item[2], first_gain, first_bias, first_router, first_up, first_down)

    def attend_block(item):
        return attention_row(item[0], item[1], attend_gain, attend_bias, project_in, relative_weight, content_bias, position_bias, attend_out)

    def front_block(item):
        return conv_front(item[0], item[1], depth_gain, depth_bias, gated_in, depth_kernel)

    def second_block(item):
        return expert_row(item[0], item[1], item[2], second_gain, second_bias, second_router, second_up, second_down)
    frame_rows = lax.map(jax.checkpoint(first_block), (frame_rows, embed_rows, first_routes))
    frame_rows = lax.map(jax.checkpoint(attend_block), (frame_rows, segments))
    depth = lax.map(jax.checkpoint(front_block), (frame_rows, segments))
    average = lax.optimization_barrier(jnp.mean(depth, (0, 1)))
    spread = lax.optimization_barrier(jnp.mean(jnp.square(depth - average), (0, 1)))

    def tail_block(item):
        return conv_tail(item[0], item[1], average, spread, batch_gain, batch_bias, point_out)
    frame_rows = lax.map(jax.checkpoint(tail_block), (frame_rows, depth))
    frame_rows = lax.map(jax.checkpoint(second_block), (frame_rows, embed_rows, second_routes))
    return layer_norm(frame_rows, final_gain, final_bias).reshape(-1, D)

def reference(inputs, embedding, segments, routes_first, routes_second, cotangent, first_gain, first_bias, first_router, first_up, first_down, attend_gain, attend_bias, project_in, relative_weight, content_bias, position_bias, attend_out, depth_gain, depth_bias, gated_in, depth_kernel, batch_gain, batch_bias, point_out, second_gain, second_bias, second_router, second_up, second_down, final_gain, final_bias):
    weights = (first_gain, first_bias, first_router, first_up, first_down, attend_gain, attend_bias, project_in, relative_weight, content_bias, position_bias, attend_out, depth_gain, depth_bias, gated_in, depth_kernel, batch_gain, batch_bias, point_out, second_gain, second_bias, second_router, second_up, second_down, final_gain, final_bias)
    floats = tuple((weight.astype(jnp.float32) for weight in weights))
    embed_rows = embedding.astype(jnp.float32).reshape(-1, TOK_DEV, D)
    first_routes = routes_first.reshape(-1, TOK_DEV)
    second_routes = routes_second.reshape(-1, TOK_DEV)

    def forward(flat_inputs, params):
        return layer_forward(flat_inputs, embed_rows, segments, first_routes, second_routes, params)
    value, backward = jax.vjp(forward, inputs.astype(jnp.float32), floats)
    input_slope, grads = backward(cotangent.astype(jnp.float32))
    return (value.astype(jnp.bfloat16), input_slope, grads[0], grads[1], grads[2], grads[3], grads[4], grads[5], grads[6], grads[7], grads[8], grads[9], grads[10], grads[11], grads[12], grads[13], grads[14], grads[15], grads[16], grads[17], grads[18], grads[19], grads[20], grads[21], grads[22], grads[23], grads[24], grads[25])
```

```python
import functools

import jax
import jax.numpy as jnp
from jax import lax
from jax.experimental import pallas as pl
from jax.experimental.pallas import tpu as pltpu
from jax.sharding import PartitionSpec as P

HEADS = 8
EXPERTS = 4
KERNEL = 15
HEAD_DIM = 64
CAPACITY = 512
AXES = ("dp", "fsdp")

eps = 1e-05
blocked = -1000000000.0


def product(left, right):
    return jnp.dot(left, right, preferred_element_type=jnp.float32)


NN = (((1,), (0,)), ((), ()))
NT = (((1,), (1,)), ((), ()))
TN = (((0,), (0,)), ((), ()))


def mul(left, right, dims=NN):
    return lax.dot_general(left, right, dims, preferred_element_type=jnp.float32)


def norm_parts(value):
    average = jnp.mean(value, -1, keepdims=True)
    centered = value - average
    spread = jnp.mean(centered * centered, -1, keepdims=True)
    inverse = lax.rsqrt(spread + eps)
    return centered * inverse, inverse


def norm_slope(unit, inverse, slope, gain):
    scaled = slope * gain
    first = jnp.mean(scaled, -1, keepdims=True)
    second = jnp.mean(scaled * unit, -1, keepdims=True)
    return (scaled - first - unit * second) * inverse


def head_mask(rows, head):
    lane = lax.broadcasted_iota(jnp.int32, (rows, 2 * HEAD_DIM), 1)
    return (lane >= head * HEAD_DIM) & (lane < (head + 1) * HEAD_DIM)


def angles(length, width):
    freqs = jnp.exp(jnp.arange(0, width, 2).astype(jnp.float32) * (-jnp.log(10000.0) / width))
    coarse = (jnp.arange(length // 32) * 32).astype(jnp.float32)[:, None] * freqs[None, :]
    fine = jnp.arange(32).astype(jnp.float32)[:, None] * freqs[None, :]
    cos_a, sin_a = jnp.cos(coarse)[:, None], jnp.sin(coarse)[:, None]
    cos_b, sin_b = jnp.cos(fine)[None], jnp.sin(fine)[None]
    cosine = (cos_a * cos_b - sin_a * sin_b).reshape(length, width // 2)
    sine = (sin_a * cos_b + cos_a * sin_b).reshape(length, width // 2)
    return cosine, sine


def attend_forward_kernel(
    resid_ref,
    gain_ref,
    bias_ref,
    pq_ref,
    pk_ref,
    pv_ref,
    rel_ref,
    cb_ref,
    pb_ref,
    segr_ref,
    segc_ref,
    tab_ref,
    cos_ref,
    sin_ref,
    ha_ref,
    qu_ref,
    qv_ref,
    k_ref,
    v_ref,
    p_ref,
    ctx_ref,
    kt_ref,
):
    length = resid_ref.shape[0]
    half = cos_ref.shape[1]
    pair = 2 * HEAD_DIM
    rows = 256

    @pl.when(pl.program_id(0) == 0)
    def first():
        unit, inverse = norm_parts(resid_ref[...])
        ha_ref[...] = (unit * gain_ref[...] + bias_ref[...]).astype(jnp.bfloat16)
        kt_ref[:, pair:] = tab_ref[...]

    normed = ha_ref[...]
    query = mul(normed, pq_ref[...])
    keys = mul(normed, pk_ref[...]).astype(jnp.bfloat16)
    k_ref[...] = keys
    kt_ref[:, :pair] = keys
    v_ref[...] = mul(normed, pv_ref[...]).astype(jnp.bfloat16)
    qu_ref[...] = (query + cb_ref[...]).astype(jnp.bfloat16)
    qv_ref[...] = (query + pb_ref[...]).astype(jnp.bfloat16)

    def block(index, carry):
        at = pl.ds(pl.multiple_of(index * rows, rows), rows)
        same = segc_ref[at, :] == segr_ref[...]
        cosine, sine = cos_ref[at, :], sin_ref[at, :]
        contexts = []
        for head in range(2):
            own = head_mask(rows, head)
            part_u = jnp.where(own, qu_ref[at, :], 0) * 0.125
            part_v = jnp.where(own, qv_ref[at, :], 0)
            coef = mul(part_v, rel_ref[...], NT) * 0.125
            left, right = coef[:, :half], coef[:, half:]
            turned_a = (left * sine + right * cosine).astype(jnp.bfloat16)
            turned_b = (right * sine - left * cosine).astype(jnp.bfloat16)
            scores = mul(
                jnp.concatenate([part_u.astype(jnp.bfloat16), turned_a, turned_b], 1), kt_ref[...], NT
            )
            scores = jnp.where(same, scores, blocked)
            peak = jnp.max(scores, -1, keepdims=True)
            raised = jnp.exp(scores - peak)
            summed = jnp.sum(raised, -1, keepdims=True)
            chances = (raised * (1.0 / summed)).astype(jnp.bfloat16)
            p_ref[head, at, :] = chances
            contexts.append(mul(chances, v_ref[...]))
        ctx_ref[at, :] = jnp.where(head_mask(rows, 0), contexts[0], contexts[1]).astype(jnp.bfloat16)
        return carry

    lax.fori_loop(0, length // rows, block, 0)


def attend_backward_kernel(
    p_ref,
    tab_ref,
    cos_ref,
    sin_ref,
    resid_ref,
    slope_ref,
    ha_ref,
    qu_ref,
    qv_ref,
    k_ref,
    v_ref,
    ctx_ref,
    ao_ref,
    pq_ref,
    pk_ref,
    pv_ref,
    rel_ref,
    gain_ref,
    g1_ref,
    dao_ref,
    dpq_ref,
    dpk_ref,
    dpv_ref,
    drel_ref,
    dcb_ref,
    dpb_ref,
    dgain_ref,
    dbias_ref,
    kt_ref,
    dout_ref,
    dctx_ref,
    dn_ref,
    dq_ref,
    dkt_ref,
    dvt_ref,
    drt_ref,
):
    length = resid_ref.shape[0]
    half = cos_ref.shape[1]
    pair = 2 * HEAD_DIM
    rows = 256
    step = pl.program_id(0)

    @pl.when(step == 0)
    def first():
        dout_ref[...] = slope_ref[...].astype(jnp.bfloat16)
        kt_ref[:, pair:] = tab_ref[...]
        dn_ref[...] = jnp.zeros_like(dn_ref)

    kt_ref[:, :pair] = k_ref[...]
    dao_ref[...] = mul(ctx_ref[...], dout_ref[...], TN)
    dctx_ref[...] = mul(dout_ref[...], ao_ref[...], NT).astype(jnp.bfloat16)
    dkt_ref[...] = jnp.zeros_like(dkt_ref)
    dvt_ref[...] = jnp.zeros_like(dvt_ref)
    drt_ref[...] = jnp.zeros_like(drt_ref)
    dcb_ref[...] = jnp.zeros_like(dcb_ref)
    dpb_ref[...] = jnp.zeros_like(dpb_ref)

    def block(index, carry):
        at = pl.ds(pl.multiple_of(index * rows, rows), rows)
        cosine, sine = cos_ref[at, :], sin_ref[at, :]
        total = jnp.zeros((rows, pair), jnp.float32)
        sum_u = jnp.zeros((1, pair), jnp.float32)
        sum_v = jnp.zeros((1, pair), jnp.float32)
        for head in range(2):
            own = head_mask(rows, head)
            part = jnp.where(own, dctx_ref[at, :], 0)
            low = p_ref[head, at, :]
            chances = low.astype(jnp.float32)
            raw = mul(part, v_ref[...], NT)
            weighted = chances * raw
            delta = jnp.sum(weighted, -1, keepdims=True)
            slope = ((weighted - chances * delta) * 0.125).astype(jnp.bfloat16)
            dvt_ref[...] += mul(part, low, TN)
            dkt_ref[...] += mul(jnp.where(own, qu_ref[at, :], 0), slope, TN)
            wide = mul(slope, kt_ref[...])
            slope_u = jnp.where(own, wide[:, :pair], 0.0)
            first, second = wide[:, pair : pair + half], wide[:, pair + half :]
            coef = jnp.concatenate(
                [
                    (first * sine - second * cosine).astype(jnp.bfloat16),
                    (first * cosine + second * sine).astype(jnp.bfloat16),
                ],
                1,
            )
            slope_v = jnp.where(own, mul(coef, rel_ref[...]), 0.0)
            drt_ref[...] += mul(jnp.where(own, qv_ref[at, :], 0), coef, TN)
            total = total + slope_u + slope_v
            sum_u = sum_u + jnp.sum(slope_u, 0, keepdims=True)
            sum_v = sum_v + jnp.sum(slope_v, 0, keepdims=True)
        dq_ref[at, :] = total
        dcb_ref[...] += sum_u
        dpb_ref[...] += sum_v
        return carry

    lax.fori_loop(0, length // rows, block, 0)
    low_q = dq_ref[...].astype(jnp.bfloat16)
    low_k = dkt_ref[...].T.astype(jnp.bfloat16)
    low_v = dvt_ref[...].T.astype(jnp.bfloat16)
    drel_ref[...] = drt_ref[...].T
    normed = ha_ref[...]
    dpq_ref[...] = mul(normed, low_q, TN)
    dpk_ref[...] = mul(normed, low_k, TN)
    dpv_ref[...] = mul(normed, low_v, TN)
    dn_ref[...] += (
        mul(low_q, pq_ref[...], NT) + mul(low_k, pk_ref[...], NT) + mul(low_v, pv_ref[...], NT)
    )

    @pl.when(step == pl.num_programs(0) - 1)
    def last():
        unit, inverse = norm_parts(resid_ref[...])
        slope = dn_ref[...]
        dgain_ref[...] = jnp.sum(slope * unit, 0, keepdims=True)
        dbias_ref[...] = jnp.sum(slope, 0, keepdims=True)
        g1_ref[...] = slope_ref[...] + norm_slope(unit, inverse, slope, gain_ref[...])


def whole(shape):
    return pl.BlockSpec(shape, lambda p: (0,) * len(shape))


def columns(rows, width, shift=0):
    return pl.BlockSpec((rows, width), lambda p: (0, p + shift))


def attention_forward(resid, segments, weights, tables):
    gain, bias, project_in, relative, content_bias, position_bias, attend_out = weights
    table, cosine, sine = tables
    length, width = resid.shape
    pair = 2 * HEAD_DIM
    pairs = HEADS // 2
    low = jnp.bfloat16
    shape = jax.ShapeDtypeStruct
    return pl.pallas_call(
        attend_forward_kernel,
        grid=(pairs,),
        in_specs=[
            whole((length, width)),
            whole((1, width)),
            whole((1, width)),
            columns(width, pair),
            columns(width, pair, pairs),
            columns(width, pair, 2 * pairs),
            columns(width, pair),
            columns(1, pair),
            columns(1, pair),
            whole((1, length)),
            whole((length, 1)),
            whole((length, width)),
            whole((length, width // 2)),
            whole((length, width // 2)),
        ],
        out_specs=[whole((length, width))]
        + [columns(length, pair)] * 4
        + [pl.BlockSpec((2, length, length), lambda p: (p, 0, 0)), columns(length, pair)],
        out_shape=[shape((length, width), low)] * 5
        + [shape((HEADS, length, length), low), shape((length, width), low)],
        scratch_shapes=[pltpu.VMEM((length, pair + width), low)],
        compiler_params=pltpu.CompilerParams(vmem_limit_bytes=56 * 1024 * 1024),
        cost_estimate=pl.CostEstimate(flops=24 * 10**9, bytes_accessed=30 * 10**6, transcendentals=8 * 10**6),
        name="attend_forward",
    )(
        resid,
        gain,
        bias,
        project_in,
        project_in,
        project_in,
        relative,
        content_bias,
        position_bias,
        segments,
        segments.reshape(length, 1),
        table,
        cosine,
        sine,
    )


def attention_backward(resid, slope, weights, tables, kept):
    gain, bias, project_in, relative, content_bias, position_bias, attend_out = weights
    table, cosine, sine = tables
    normed, query_u, query_v, keys, values, chances, context = kept
    length, width = resid.shape
    pair = 2 * HEAD_DIM
    pairs = HEADS // 2
    low, full = jnp.bfloat16, jnp.float32
    shape = jax.ShapeDtypeStruct
    return pl.pallas_call(
        attend_backward_kernel,
        grid=(pairs,),
        in_specs=[
            pl.BlockSpec((2, length, length), lambda p: (p, 0, 0)),
            whole((length, width)),
            whole((length, width // 2)),
            whole((length, width // 2)),
            whole((length, width)),
            whole((length, width)),
            whole((length, width)),
        ]
        + [columns(length, pair)] * 5
        + [
            pl.BlockSpec((pair, width), lambda p: (p, 0)),
            columns(width, pair),
            columns(width, pair, pairs),
            columns(width, pair, 2 * pairs),
            columns(width, pair),
            whole((1, width)),
        ],
        out_specs=[
            whole((length, width)),
            pl.BlockSpec((pair, width), lambda p: (p, 0)),
            columns(width, pair),
            columns(width, pair),
            columns(width, pair),
            columns(width, pair),
            columns(1, pair),
            columns(1, pair),
            whole((1, width)),
            whole((1, width)),
        ],
        out_shape=[shape((length, width), full)]
        + [shape((width, width), full)] * 5
        + [shape((1, width), full)] * 4,
        scratch_shapes=[
            pltpu.VMEM((length, pair + width), low),
            pltpu.VMEM((length, width), low),
            pltpu.VMEM((length, pair), low),
            pltpu.VMEM((length, width), full),
            pltpu.VMEM((length, pair), full),
            pltpu.VMEM((pair, length), full),
            pltpu.VMEM((pair, length), full),
            pltpu.VMEM((pair, width), full),
        ],
        compiler_params=pltpu.CompilerParams(vmem_limit_bytes=60 * 1024 * 1024),
        cost_estimate=pl.CostEstimate(flops=40 * 10**9, bytes_accessed=40 * 10**6, transcendentals=0),
        name="attend_backward",
    )(
        chances,
        table,
        cosine,
        sine,
        resid,
        slope,
        normed,
        query_u,
        query_v,
        keys,
        values,
        context,
        attend_out,
        project_in,
        project_in,
        project_in,
        relative,
        gain,
    )


TILE = 256


def one_hot_rows(pos_row, base):
    slot = lax.broadcasted_iota(jnp.int32, (TILE, pos_row.shape[1]), 0) + base
    return (slot == pos_row).astype(jnp.float32).astype(jnp.bfloat16)


def one_hot_columns(pos_col, base):
    slot = lax.broadcasted_iota(jnp.int32, (pos_col.shape[0], TILE), 1) + base
    return (slot == pos_col).astype(jnp.float32).astype(jnp.bfloat16)


def routed(route_col):
    lane = lax.broadcasted_iota(jnp.int32, (route_col.shape[0], 128), 1)
    return (lane == route_col).astype(jnp.float32)


def sigmoid(value):
    return 1.0 / (1.0 + jnp.exp(-value))


def split_mul(wide, narrow, dims):
    high = wide.astype(jnp.bfloat16)
    rest = (wide - high.astype(jnp.float32)).astype(jnp.bfloat16)
    return mul(high, narrow, dims) + mul(rest, narrow, dims)


def route_probs(normed, embed, router_ref):
    width = normed.shape[1]
    logits = mul(normed, router_ref[:width, :]) + mul(embed, router_ref[width:, :])
    lane = lax.broadcasted_iota(jnp.int32, logits.shape, 1)
    logits = jnp.where(lane < EXPERTS, logits, -jnp.inf)
    raised = jnp.exp(logits - jnp.max(logits, -1, keepdims=True))
    return raised / jnp.sum(raised, -1, keepdims=True)


def expert_tile(index, normed, pos_row, up, down):
    base = index * TILE
    picked = mul(one_hot_rows(pos_row, base), normed).astype(jnp.bfloat16)
    total = None
    chunk = 512
    for start in range(0, up.shape[1], chunk):
        inner = mul(picked, up[:, start : start + chunk])
        active = (inner * sigmoid(inner)).astype(jnp.bfloat16)
        part = mul(active, down[start : start + chunk, :])
        total = part if total is None else total + part
    return total.astype(jnp.bfloat16)


def expert_forward_steps(counts_ref, normed_ref, posr_ref, posc_ref, up_ref, down_ref, branch_ref):
    expert = pl.program_id(0)
    width = normed_ref.shape[1]
    up = up_ref[...].reshape(width, -1)
    down = down_ref[...].reshape(-1, width)

    @pl.when(expert == 0)
    def clear():
        branch_ref[...] = jnp.zeros_like(branch_ref)

    for part in range(CAPACITY // TILE):

        @pl.when(counts_ref[expert] > part * TILE)
        def run():
            index = expert * (CAPACITY // TILE) + part
            outgoing = expert_tile(index, normed_ref[...], posr_ref[...], up, down)
            branch_ref[...] += mul(one_hot_columns(posc_ref[...], index * TILE), outgoing)


def first_forward_kernel(
    counts_ref, normed_ref, posr_ref, posc_ref, up_ref, down_ref, resid_ref, probs_ref, route_ref,
    out_ref, branch_ref,
):
    expert_forward_steps(counts_ref, normed_ref, posr_ref, posc_ref, up_ref, down_ref, branch_ref)

    @pl.when(pl.program_id(0) == pl.num_programs(0) - 1)
    def last():
        gate = jnp.sum(probs_ref[...] * routed(route_ref[...]), -1, keepdims=True)
        out_ref[...] = resid_ref[...].astype(jnp.float32) + 0.5 * gate * branch_ref[...]


def second_forward_kernel(
    counts_ref, normed_ref, posr_ref, posc_ref, up_ref, down_ref, resid_ref, probs_ref, route_ref,
    cot_ref, gain_ref, bias_ref,
    result_ref, g4_ref, dgain_ref, dbias_ref, branch_ref,
):
    expert_forward_steps(counts_ref, normed_ref, posr_ref, posc_ref, up_ref, down_ref, branch_ref)

    @pl.when(pl.program_id(0) == pl.num_programs(0) - 1)
    def last():
        gate = jnp.sum(probs_ref[...] * routed(route_ref[...]), -1, keepdims=True)
        unit, inverse = norm_parts(resid_ref[...] + 0.5 * gate * branch_ref[...])
        gain = gain_ref[...]
        cot = cot_ref[...].astype(jnp.float32)
        result_ref[...] = (unit * gain + bias_ref[...]).astype(jnp.bfloat16)
        dgain_ref[...] = jnp.sum(cot * unit, 0, keepdims=True)
        dbias_ref[...] = jnp.sum(cot, 0, keepdims=True)
        g4_ref[...] = norm_slope(unit, inverse, cot, gain)


def expert_backward_kernel(
    counts_ref, normed_ref, posr_ref, posc_ref, up_ref, down_ref, resid_ref, probs_ref, route_ref,
    branch_ref, slope_ref, embed_ref, router_ref, gain_ref,
    dup_ref, ddown_ref, out_ref, dgain_ref, dbias_ref, drouter_ref,
    low_ref, dlogits_ref, dnorm_ref, picked_ref, dpicked_ref, active_ref, dinner_ref,
):
    expert = pl.program_id(0)
    width = normed_ref.shape[1]
    up = up_ref[...].reshape(width, -1)
    down = down_ref[...].reshape(-1, width)
    hidden = up.shape[1]
    chunk = 512

    @pl.when(expert == 0)
    def first():
        chosen = routed(route_ref[...])
        probs = probs_ref[...]
        gate = jnp.sum(probs * chosen, -1, keepdims=True)
        slope = slope_ref[...]
        low_ref[...] = (0.5 * gate * slope).astype(jnp.bfloat16)
        dgate = 0.5 * jnp.sum(slope * branch_ref[...], -1, keepdims=True)
        dlogits = probs * (chosen - gate) * dgate
        dlogits_ref[...] = dlogits
        dnorm_ref[...] = split_mul(dlogits, router_ref[:width, :], NT)

    def tile(part):
        index = expert * (CAPACITY // TILE) + part
        at = slice(part * TILE, (part + 1) * TILE)
        hot = one_hot_rows(posr_ref[...], index * TILE)
        picked = mul(hot, normed_ref[...]).astype(jnp.bfloat16)
        dpicked = mul(hot, low_ref[...]).astype(jnp.bfloat16)
        picked_ref[at, :] = picked
        dpicked_ref[at, :] = dpicked
        total = None
        for start in range(0, hidden, chunk):
            span = slice(start, start + chunk)
            inner = mul(picked, up[:, span])
            sigma = sigmoid(inner)
            active_ref[at, span] = (inner * sigma).astype(jnp.bfloat16)
            dactive = mul(dpicked, down[span, :], NT)
            dinner = (dactive * (sigma * (1.0 + inner * (1.0 - sigma)))).astype(jnp.bfloat16)
            dinner_ref[at, span] = dinner
            part_sum = mul(dinner, up[:, span], NT)
            total = part_sum if total is None else total + part_sum
        dnorm_ref[...] += mul(one_hot_columns(posc_ref[...], index * TILE), total.astype(jnp.bfloat16))

    def weight_grads(rows):
        for start in range(0, hidden, chunk):
            span = slice(start, start + chunk)
            dup_ref[..., span] = (
                mul(picked_ref[:rows, :], dinner_ref[:rows, span], TN)
                .astype(jnp.bfloat16)
                .reshape(dup_ref.shape[:-1] + (chunk,))
            )
            grads = mul(active_ref[:rows, span], dpicked_ref[:rows, :], TN).astype(jnp.bfloat16)
            owned = ddown_ref.shape[2]
            if owned > chunk:
                ddown_ref[0, 0, span, :] = grads
            else:
                groups = slice(start // owned, (start + chunk) // owned)
                ddown_ref[groups] = grads.reshape((chunk // owned,) + ddown_ref.shape[1:])

    tile(0)
    count = counts_ref[expert]

    @pl.when(count <= TILE)
    def small():
        weight_grads(TILE)

    @pl.when(count > TILE)
    def large():
        tile(1)
        weight_grads(2 * TILE)

    @pl.when(expert == pl.num_programs(0) - 1)
    def last():
        unit, inverse = norm_parts(resid_ref[...].astype(jnp.float32))
        slope = dnorm_ref[...]
        dgain_ref[...] = jnp.sum(slope * unit, 0, keepdims=True)
        dbias_ref[...] = jnp.sum(slope, 0, keepdims=True)
        out_ref[...] = slope_ref[...] + norm_slope(unit, inverse, slope, gain_ref[...])
        dlogits = dlogits_ref[...]
        drouter_ref[:, :width] = split_mul(dlogits, normed_ref[...], TN)
        drouter_ref[:, width:] = split_mul(dlogits, embed_ref[...], TN)


def fixed(shape):
    return pl.BlockSpec(shape, lambda e, counts: (0,) * len(shape))


def expert_specs(length, width, up, down):
    return [
        fixed((length, width)),
        fixed((1, length)),
        fixed((length, 1)),
        pl.BlockSpec((up.shape[0], 1) + up.shape[2:], lambda e, counts: (0, e, 0, 0)),
        pl.BlockSpec((down.shape[0], 1) + down.shape[2:], lambda e, counts: (0, e, 0, 0)),
        fixed((length, width)),
        fixed((length, 128)),
        fixed((length, 1)),
    ]


def expert_call(kernel, name, extra_specs, out_specs, out_shape, scratch, flops, args):
    counts, normed, pos_row, pos_col, up, down = args[:6]
    length, width = normed.shape
    return pl.pallas_call(
        kernel,
        grid_spec=pltpu.PrefetchScalarGridSpec(
            num_scalar_prefetch=1,
            grid=(EXPERTS,),
            in_specs=expert_specs(length, width, up, down) + extra_specs,
            out_specs=out_specs,
            scratch_shapes=scratch,
        ),
        out_shape=out_shape,
        compiler_params=pltpu.CompilerParams(vmem_limit_bytes=60 * 1024 * 1024),
        cost_estimate=pl.CostEstimate(flops=flops, bytes_accessed=30 * 10**6, transcendentals=4 * 10**6),
        name=name,
    )(*args)


def first_forward(args):
    length, width = args[1].shape
    full = jnp.float32
    out = jax.ShapeDtypeStruct((length, width), full)
    return expert_call(
        first_forward_kernel,
        "first_forward",
        [],
        [fixed((length, width))] * 2,
        [out, out],
        [],
        10 * 10**9,
        args,
    )


def second_forward(args):
    length, width = args[1].shape
    full = jnp.float32
    wide = jax.ShapeDtypeStruct((length, width), full)
    thin = jax.ShapeDtypeStruct((1, width), full)
    return expert_call(
        second_forward_kernel,
        "second_forward",
        [fixed((length, width)), fixed((1, width)), fixed((1, width))],
        [fixed((length, width))] * 2 + [fixed((1, width))] * 2 + [fixed((length, width))],
        [jax.ShapeDtypeStruct((length, width), jnp.bfloat16), wide, thin, thin, wide],
        [],
        10 * 10**9,
        args,
    )


def expert_backward(args):
    length, width = args[1].shape
    up, down = args[4:6]
    hidden = up.shape[3]
    low, full = jnp.bfloat16, jnp.float32
    shape = jax.ShapeDtypeStruct
    thin = shape((1, width), full)
    return expert_call(
        expert_backward_kernel,
        "expert_backward",
        [
            fixed((length, width)),
            fixed((length, width)),
            fixed((length, width)),
            fixed((2 * width, 128)),
            fixed((1, width)),
        ],
        [
            pl.BlockSpec((up.shape[0], 1) + up.shape[2:], lambda e, counts: (0, e, 0, 0)),
            pl.BlockSpec((down.shape[0], 1) + down.shape[2:], lambda e, counts: (0, e, 0, 0)),
            fixed((length, width)),
            fixed((1, width)),
            fixed((1, width)),
            fixed((128, 2 * width)),
        ],
        [
            shape(up.shape, low),
            shape(down.shape, low),
            shape((length, width), full),
            thin,
            thin,
            shape((128, 2 * width), full),
        ],
        [
            pltpu.VMEM((length, width), low),
            pltpu.VMEM((length, 128), full),
            pltpu.VMEM((length, width), full),
            pltpu.VMEM((CAPACITY, width), low),
            pltpu.VMEM((CAPACITY, width), low),
            pltpu.VMEM((CAPACITY, hidden), low),
            pltpu.VMEM((CAPACITY, hidden), low),
        ],
        28 * 10**9,
        args,
    )


def enter_kernel(resid_ref, embed_ref, router_ref, gain_ref, bias_ref, normed_ref, probs_ref):
    unit, inverse = norm_parts(resid_ref[...].astype(jnp.float32))
    normed = (unit * gain_ref[...] + bias_ref[...]).astype(jnp.bfloat16)
    normed_ref[...] = normed
    probs_ref[...] = route_probs(normed, embed_ref[...], router_ref)


def expert_enter(resid, embedding, router, gain, bias):
    length, width = resid.shape
    return pl.pallas_call(
        enter_kernel,
        out_shape=[
            jax.ShapeDtypeStruct((length, width), jnp.bfloat16),
            jax.ShapeDtypeStruct((length, 128), jnp.float32),
        ],
        compiler_params=pltpu.CompilerParams(vmem_limit_bytes=40 * 1024 * 1024),
        name="expert_enter",
    )(resid, embedding, router, gain, bias)


def places(routes):
    length = routes.shape[0]
    chosen = (routes == jnp.arange(EXPERTS, dtype=jnp.int32)[None, :]).astype(jnp.float32)
    row = lax.broadcasted_iota(jnp.int32, (length, length), 0)
    before = (lax.broadcasted_iota(jnp.int32, (length, length), 1) < row).astype(jnp.bfloat16)
    earlier = product(before, chosen.astype(jnp.bfloat16))
    slot = jnp.sum(earlier * chosen, 1).astype(jnp.int32) + routes[:, 0] * CAPACITY
    counts = jnp.sum(chosen, 0).astype(jnp.int32)
    return counts, slot[None, :], slot[:, None]


CHUNK = 64
EDGE = 8


def tap_masks(segments):
    half = KERNEL // 2
    segment = segments[0]
    length = segment.shape[0]
    padded = jnp.pad(segment, (half, half), constant_values=-1)
    same = [padded[k : k + length] == segment for k in range(KERNEL)]
    masks = jnp.stack(same, 1).astype(jnp.float32)
    return jnp.pad(masks, ((0, 0), (0, 128 - KERNEL)))


def conv_front_kernel(
    resid_ref, ctx_ref, ao_ref, gain_ref, bias_ref, gated_ref, taps_ref, mask_ref,
    out_ref, normed_ref, joined_ref, depth_ref, sums_ref,
    pad_ref,
):
    length, width = resid_ref.shape
    resid = resid_ref[...] + mul(ctx_ref[...], ao_ref[...])
    out_ref[...] = resid
    unit, inverse = norm_parts(resid)
    normed = (unit * gain_ref[...] + bias_ref[...]).astype(jnp.bfloat16)
    normed_ref[...] = normed
    joined = mul(normed, gated_ref[...])
    joined_ref[...] = joined
    pad_ref[:EDGE, :] = jnp.zeros((EDGE, width), jnp.float32)
    pad_ref[EDGE + length :, :] = jnp.zeros((EDGE, width), jnp.float32)
    pad_ref[EDGE : EDGE + length, :] = joined[:, :width] * sigmoid(joined[:, width:])
    sums_ref[...] = jnp.zeros_like(sums_ref)

    def chunk(index, carry):
        at = pl.ds(pl.multiple_of(index * CHUNK, CHUNK), CHUNK)
        window = pad_ref[pl.ds(pl.multiple_of(index * CHUNK, CHUNK), CHUNK + 2 * EDGE), :]
        masks = mask_ref[at, :]
        total = jnp.zeros((CHUNK, width), jnp.float32)
        for k in range(KERNEL):
            total = total + window[k + 1 : k + 1 + CHUNK] * masks[:, k : k + 1] * taps_ref[k : k + 1, :]
        depth_ref[at, :] = total
        sums_ref[0:1, :] += jnp.sum(total, 0, keepdims=True)
        sums_ref[1:2, :] += jnp.sum(total * total, 0, keepdims=True)
        return carry

    lax.fori_loop(0, length // CHUNK, chunk, 0)


def conv_front(resid, context, attend_out, gain, bias, gated_in, taps, masks):
    length, width = resid.shape
    low, full = jnp.bfloat16, jnp.float32
    shape = jax.ShapeDtypeStruct
    return pl.pallas_call(
        conv_front_kernel,
        out_shape=[
            shape((length, width), full),
            shape((length, width), low),
            shape((length, 2 * width), full),
            shape((length, width), full),
            shape((2, width), full),
        ],
        scratch_shapes=[pltpu.VMEM((length + 2 * EDGE, width), full)],
        compiler_params=pltpu.CompilerParams(vmem_limit_bytes=56 * 1024 * 1024),
        cost_estimate=pl.CostEstimate(flops=4 * 10**9, bytes_accessed=16 * 10**6, transcendentals=10**6),
        name="conv_front",
    )(resid, context, attend_out, gain, bias, gated_in, taps, masks)


def batch_stats(stats, frames):
    average = stats[0:1, :] * (1.0 / frames)
    spread = stats[1:2, :] * (1.0 / frames) - average * average
    return average, lax.rsqrt(spread + eps)


def conv_tail_kernel(
    frames, depth_ref, stats_ref, bgain_ref, bbias_ref, point_ref, resid_ref,
    embed_ref, router_ref, gain_ref, bias_ref,
    out_ref, normed_ref, probs_ref,
):
    average, inverse = batch_stats(stats_ref[...], frames)
    shifted = (depth_ref[...] - average) * inverse * bgain_ref[...] + bbias_ref[...]
    tail = (shifted * sigmoid(shifted)).astype(jnp.bfloat16)
    resid = resid_ref[...] + mul(tail, point_ref[...])
    out_ref[...] = resid
    unit, spread = norm_parts(resid)
    normed = (unit * gain_ref[...] + bias_ref[...]).astype(jnp.bfloat16)
    normed_ref[...] = normed
    probs_ref[...] = route_probs(normed, embed_ref[...], router_ref)


def conv_tail(frames, depth, stats, bgain, bbias, point_out, resid, embedding, router, gain, bias):
    length, width = resid.shape
    shape = jax.ShapeDtypeStruct
    return pl.pallas_call(
        functools.partial(conv_tail_kernel, frames),
        out_shape=[
            shape((length, width), jnp.float32),
            shape((length, width), jnp.bfloat16),
            shape((length, 128), jnp.float32),
        ],
        compiler_params=pltpu.CompilerParams(vmem_limit_bytes=56 * 1024 * 1024),
        cost_estimate=pl.CostEstimate(flops=10**9, bytes_accessed=8 * 10**6, transcendentals=10**6),
        name="conv_tail",
    )(depth, stats, bgain, bbias, point_out, resid, embedding, router, gain, bias)


def conv_turn_kernel(
    frames, slope_ref, depth_ref, stats_ref, bgain_ref, bbias_ref, point_ref,
    dshift_ref, dpoint_ref, sums_ref,
):
    average, inverse = batch_stats(stats_ref[...], frames)
    centered = (depth_ref[...] - average) * inverse
    shifted = centered * bgain_ref[...] + bbias_ref[...]
    sigma = sigmoid(shifted)
    low = slope_ref[...].astype(jnp.bfloat16)
    dpoint_ref[...] = mul((shifted * sigma).astype(jnp.bfloat16), low, TN)
    dshift = mul(low, point_ref[...], NT) * (sigma * (1.0 + shifted * (1.0 - sigma)))
    dshift_ref[...] = dshift
    sums_ref[0:1, :] = jnp.sum(dshift * centered, 0, keepdims=True)
    sums_ref[1:2, :] = jnp.sum(dshift, 0, keepdims=True)


def conv_turn(frames, slope, depth, stats, bgain, bbias, point_out):
    length, width = slope.shape
    shape = jax.ShapeDtypeStruct
    return pl.pallas_call(
        functools.partial(conv_turn_kernel, frames),
        out_shape=[
            shape((length, width), jnp.float32),
            shape((width, width), jnp.float32),
            shape((2, width), jnp.float32),
        ],
        compiler_params=pltpu.CompilerParams(vmem_limit_bytes=56 * 1024 * 1024),
        cost_estimate=pl.CostEstimate(flops=10**9, bytes_accessed=8 * 10**6, transcendentals=10**6),
        name="conv_turn",
    )(slope, depth, stats, bgain, bbias, point_out)


def conv_back_kernel(
    frames, slope_ref, dshift_ref, depth_ref, stats_ref, sums_ref, bgain_ref, joined_ref, normed_ref,
    resid_ref, gain_ref, gated_ref, taps_ref, mask_ref,
    out_ref, dgated_ref, dtaps_ref, dgain_ref, dbias_ref,
    pad_ref, dpad_ref, dtap_ref, dglu_ref,
):
    length, width = resid_ref.shape
    average, inverse = batch_stats(stats_ref[...], frames)
    bgain = bgain_ref[...]
    sums = sums_ref[...] * (1.0 / frames) * bgain
    centered = (depth_ref[...] - average) * inverse
    edge = jnp.zeros((EDGE, width), jnp.float32)
    left = joined_ref[:, :width]
    sigma = sigmoid(joined_ref[:, width:])
    for ref, value in (
        (pad_ref, left * sigma),
        (dpad_ref, inverse * (dshift_ref[...] * bgain - sums[1:2, :] - centered * sums[0:1, :])),
    ):
        ref[:EDGE, :] = edge
        ref[EDGE + length :, :] = edge
        ref[EDGE : EDGE + length, :] = value
    dtap_ref[...] = jnp.zeros_like(dtap_ref)

    def chunk(index, carry):
        at = pl.ds(pl.multiple_of(index * CHUNK, CHUNK), CHUNK)
        around = pl.ds(pl.multiple_of(index * CHUNK, CHUNK), CHUNK + 2 * EDGE)
        window = pad_ref[around, :]
        dwindow = dpad_ref[around, :]
        masks = mask_ref[at, :]
        middle = dwindow[EDGE : EDGE + CHUNK]
        total = jnp.zeros((CHUNK, width), jnp.float32)
        for k in range(KERNEL):
            mask = masks[:, k : k + 1]
            back = KERNEL - 1 - k
            total = total + dwindow[k + 1 : k + 1 + CHUNK] * mask * taps_ref[back : back + 1, :]
            term = window[k + 1 : k + 1 + CHUNK] * mask * middle
            dtap_ref[8 * k : 8 * k + 8, :] += jnp.sum(term.reshape(CHUNK // 8, 8, width), 0)
        dglu_ref[at, :] = total
        return carry

    lax.fori_loop(0, length // CHUNK, chunk, 0)
    for k in range(KERNEL):
        dtaps_ref[k : k + 1, :] = jnp.sum(dtap_ref[8 * k : 8 * k + 8, :], 0, keepdims=True)
    dglu = dglu_ref[...]
    low = jnp.concatenate(
        [
            (dglu * sigma).astype(jnp.bfloat16),
            (dglu * left * sigma * (1.0 - sigma)).astype(jnp.bfloat16),
        ],
        1,
    )
    dgated_ref[...] = mul(normed_ref[...], low, TN)
    slope = mul(low, gated_ref[...], NT)
    unit, spread = norm_parts(resid_ref[...])
    dgain_ref[...] = jnp.sum(slope * unit, 0, keepdims=True)
    dbias_ref[...] = jnp.sum(slope, 0, keepdims=True)
    out_ref[...] = slope_ref[...] + norm_slope(unit, spread, slope, gain_ref[...])


def conv_back(
    frames, slope, dshift, depth, stats, sums, bgain, joined, normed, resid, gain, gated_in, taps, masks
):
    length, width = resid.shape
    full = jnp.float32
    shape = jax.ShapeDtypeStruct
    padded = pltpu.VMEM((length + 2 * EDGE, width), full)
    return pl.pallas_call(
        functools.partial(conv_back_kernel, frames),
        out_shape=[
            shape((length, width), full),
            shape((width, 2 * width), full),
            shape((KERNEL, width), full),
            shape((1, width), full),
            shape((1, width), full),
        ],
        scratch_shapes=[
            padded,
            padded,
            pltpu.VMEM((8 * KERNEL, width), full),
            pltpu.VMEM((length, width), full),
        ],
        compiler_params=pltpu.CompilerParams(vmem_limit_bytes=60 * 1024 * 1024),
        cost_estimate=pl.CostEstimate(flops=6 * 10**9, bytes_accessed=20 * 10**6, transcendentals=10**6),
        name="conv_back",
    )(slope, dshift, depth, stats, sums, bgain, joined, normed, resid, gain, gated_in, taps, masks)


def total_of(value):
    count = lax.axis_size(AXES)
    bit = 1
    while bit < count:
        value = value + lax.ppermute(value, AXES, [(d, d ^ bit) for d in range(count)])
        bit *= 2
    return value


def gather_experts(value):
    blocks = lax.all_gather(value, AXES, axis=0, tiled=False)
    if value.shape[1] % 16:
        blocks = blocks.transpose(1, 0, 2, 3).reshape((1, EXPERTS, -1, value.shape[2]))
    return blocks


def scatter_experts(value):
    devices = lax.axis_size(AXES)
    if value.shape[0] == 1:
        value = value.reshape((EXPERTS, devices, -1, value.shape[3])).transpose(1, 0, 2, 3)
    return lax.psum_scatter(value, AXES, scatter_dimension=0, tiled=False).astype(jnp.float32)


def gather_rows(value):
    return lax.all_gather(value, AXES, axis=0, tiled=True)


def scatter_rows(value):
    return lax.psum_scatter(value, AXES, scatter_dimension=0, tiled=True)


def router_columns(router):
    count = router.shape[0] // 2
    return router.reshape(2, count, EXPERTS).transpose(1, 0, 2).reshape(count, 2 * EXPERTS)


def router_rows(packed, devices):
    count = packed.shape[0] // devices
    return (
        packed.reshape(devices, count, 2, EXPERTS).transpose(0, 2, 1, 3).reshape(-1, EXPERTS)
    )


def on_device(
    inputs,
    embedding,
    segments,
    routes_first,
    routes_second,
    cotangent,
    first_gain,
    first_bias,
    first_router,
    first_up,
    first_down,
    attend_gain,
    attend_bias,
    project_in,
    relative_weight,
    content_bias,
    position_bias,
    attend_out,
    depth_gain,
    depth_bias,
    gated_in,
    depth_kernel,
    batch_gain,
    batch_bias,
    point_out,
    second_gain,
    second_bias,
    second_router,
    second_up,
    second_down,
    final_gain,
    final_bias,
):
    segment = segments[0]
    devices = lax.axis_size(AXES)
    length, width = inputs.shape
    frames = length * devices
    vectors = jnp.stack(
        [
            first_gain,
            first_bias,
            second_gain,
            second_bias,
            attend_gain,
            attend_bias,
            content_bias,
            position_bias,
            depth_gain,
            depth_bias,
            batch_gain,
            batch_bias,
            final_gain,
            final_bias,
        ],
        1,
    )
    n_vec = vectors.shape[1]
    small = jnp.concatenate(
        [
            vectors,
            depth_kernel.T,
            router_columns(first_router),
            router_columns(second_router),
        ],
        1,
    )
    n_small = small.shape[1]
    small = jnp.pad(small, ((0, 0), (0, 128 - n_small)))
    packed = gather_rows(
        jnp.concatenate(
            [small, project_in, relative_weight, attend_out, gated_in, point_out], 1
        )
    )
    small = packed[:, :n_small]
    rows = small[:, : n_vec + KERNEL].T
    col = n_vec + KERNEL
    first_router_full = router_rows(small[:, col : col + 2 * EXPERTS], devices)
    second_router_full = router_rows(small[:, col + 2 * EXPERTS : col + 4 * EXPERTS], devices)
    at = 128
    project_full = packed[:, at : at + 3 * width]
    at = at + 3 * width
    relative_full = packed[:, at : at + width]
    at = at + width
    attend_out_full = packed[:, at : at + width]
    at = at + width
    gated_full = packed[:, at : at + 2 * width]
    at = at + 2 * width
    point_full = packed[:, at : at + width]
    relative_full = relative_full.reshape(width // 2, 2, width).transpose(1, 0, 2).reshape(width, width)
    floats = rows.astype(jnp.float32)

    def vec(index):
        return floats[index : index + 1]

    def router_wide(router):
        return jnp.pad(router, ((0, 0), (0, 128 - EXPERTS)))

    first_router_full = router_wide(first_router_full)
    second_router_full = router_wide(second_router_full)
    taps = floats[n_vec : n_vec + KERNEL]
    masks = tap_masks(segments)
    first_places = places(routes_first)
    second_places = places(routes_second)
    first_ups, first_downs = gather_experts(first_up), gather_experts(first_down)
    second_ups, second_downs = gather_experts(second_up), gather_experts(second_down)
    attend_full = (
        vec(4),
        vec(5),
        project_full,
        relative_full,
        vec(6),
        vec(7),
        attend_out_full,
    )
    cosine, sine = angles(length, width)
    tables = (jnp.concatenate([cosine, sine], 1).astype(jnp.bfloat16), cosine, sine)

    first_normed, first_probs = expert_enter(inputs, embedding, first_router_full, vec(0), vec(1))
    first_common = (
        first_places[0],
        first_normed,
        first_places[1],
        first_places[2],
        first_ups,
        first_downs,
        inputs,
        first_probs,
        routes_first,
    )
    first_resid, first_branch = first_forward(first_common)
    attend_kept = attention_forward(first_resid, segments, attend_full, tables)
    attend_resid, conv_normed, joined, depth, stats = conv_front(
        first_resid, attend_kept[6], attend_out_full, vec(8), vec(9), gated_full, taps, masks
    )
    stats = total_of(stats)
    conv_resid, second_normed, second_probs = conv_tail(
        frames, depth, stats, vec(10), vec(11), point_full, attend_resid,
        embedding, second_router_full, vec(2), vec(3),
    )
    second_common = (
        second_places[0],
        second_normed,
        second_places[1],
        second_places[2],
        second_ups,
        second_downs,
        conv_resid,
        second_probs,
        routes_second,
    )
    result, slope, final_gain_grad, final_bias_grad, second_branch = second_forward(
        second_common + (cotangent, vec(12), vec(13))
    )
    second_dup, second_ddown, slope, dgain_second, dbias_second, drouter_second = expert_backward(
        second_common + (second_branch, slope, embedding, second_router_full, vec(2))
    )
    second_up_grad, second_down_grad = scatter_experts(second_dup), scatter_experts(second_ddown)
    dshift, dpoint, sums = conv_turn(frames, slope, depth, stats, vec(10), vec(11), point_full)
    sums = total_of(sums)
    slope, dgated, dtaps, dgain_depth, dbias_depth = conv_back(
        frames, slope, dshift, depth, stats, sums, vec(10), joined, conv_normed,
        attend_resid, vec(8), gated_full, taps, masks,
    )
    slope, dao, dpq, dpk, dpv, drel, dcb, dpb, dgain_attend, dbias_attend = attention_backward(
        first_resid, slope, attend_full, tables, attend_kept
    )
    drel = drel.reshape(2, width // 2, width).transpose(1, 0, 2).reshape(width, width)
    matrices = jnp.concatenate([dpq, dpk, dpv, drel, dao, dgated, dpoint], 1).astype(jnp.bfloat16)
    matrices = scatter_rows(matrices).astype(jnp.float32)
    first_dup, first_ddown, slope, dgain_first, dbias_first, drouter_first = expert_backward(
        first_common + (first_branch, slope, embedding, first_router_full, vec(0))
    )
    first_up_grad, first_down_grad = scatter_experts(first_dup), scatter_experts(first_ddown)

    def columns_of(grad):
        return (
            grad[:EXPERTS]
            .reshape(EXPERTS, devices, 2, -1)
            .transpose(1, 3, 2, 0)
            .reshape(width, 2 * EXPERTS)
        )

    small_grad = scatter_rows(
        jnp.concatenate(
            [
                jnp.concatenate(
                    [
                        dgain_first,
                        dbias_first,
                        dgain_second,
                        dbias_second,
                        dgain_attend,
                        dbias_attend,
                        dcb,
                        dpb,
                        dgain_depth,
                        dbias_depth,
                        final_gain_grad,
                        final_bias_grad,
                        dtaps,
                    ],
                    0,
                ).T,
                columns_of(drouter_first),
                columns_of(drouter_second),
            ],
            1,
        )
    )
    own = small_grad.shape[0]
    start = own * lax.axis_index(AXES)
    own_sums = lax.dynamic_slice_in_dim(sums, start, own, 1)

    def vector(index):
        return small_grad[:, index]

    def router_of(start):
        block = small_grad[:, start : start + 2 * EXPERTS]
        return block.reshape(own, 2, EXPERTS).transpose(1, 0, 2).reshape(2 * own, EXPERTS)

    return (
        result,
        slope,
        vector(0),
        vector(1),
        router_of(12 + KERNEL),
        first_up_grad,
        first_down_grad,
        vector(4),
        vector(5),
        matrices[:, : 3 * width],
        matrices[:, 3 * width : 4 * width],
        vector(6),
        vector(7),
        matrices[:, 4 * width : 5 * width],
        vector(8),
        vector(9),
        matrices[:, 5 * width : 7 * width],
        small_grad[:, 12 : 12 + KERNEL].T,
        own_sums[0],
        own_sums[1],
        matrices[:, 7 * width : 8 * width],
        vector(2),
        vector(3),
        router_of(12 + KERNEL + 2 * EXPERTS),
        second_up_grad,
        second_down_grad,
        vector(10),
        vector(11),
    )


def solution(mesh):
    placed = (
        P(("dp", "fsdp"), None),
        P(("dp", "fsdp"), None),
        P(("dp", "fsdp"), None),
        P(("dp", "fsdp"), None),
        P(("dp", "fsdp"), None),
        P(("dp", "fsdp"), None),
        P(("dp", "fsdp")),
        P(("dp", "fsdp")),
        P(("dp", "fsdp"), None),
        P(None, ("dp", "fsdp"), None),
        P(None, ("dp", "fsdp"), None),
        P(("dp", "fsdp")),
        P(("dp", "fsdp")),
        P(("dp", "fsdp"), None),
        P(("dp", "fsdp"), None),
        P(("dp", "fsdp")),
        P(("dp", "fsdp")),
        P(("dp", "fsdp"), None),
        P(("dp", "fsdp")),
        P(("dp", "fsdp")),
        P(("dp", "fsdp"), None),
        P(None, ("dp", "fsdp")),
        P(("dp", "fsdp")),
        P(("dp", "fsdp")),
        P(("dp", "fsdp"), None),
        P(("dp", "fsdp")),
        P(("dp", "fsdp")),
        P(("dp", "fsdp"), None),
        P(None, ("dp", "fsdp"), None),
        P(None, ("dp", "fsdp"), None),
        P(("dp", "fsdp")),
        P(("dp", "fsdp")),
    )
    return jax.shard_map(
        on_device,
        mesh=mesh,
        in_specs=placed,
        out_specs=(
            P(("dp", "fsdp"), None),
            P(("dp", "fsdp"), None),
            P(("dp", "fsdp")),
            P(("dp", "fsdp")),
            P(("dp", "fsdp"), None),
            P(None, ("dp", "fsdp"), None),
            P(None, ("dp", "fsdp"), None),
            P(("dp", "fsdp")),
            P(("dp", "fsdp")),
            P(("dp", "fsdp"), None),
            P(("dp", "fsdp"), None),
            P(("dp", "fsdp")),
            P(("dp", "fsdp")),
            P(("dp", "fsdp"), None),
            P(("dp", "fsdp")),
            P(("dp", "fsdp")),
            P(("dp", "fsdp"), None),
            P(None, ("dp", "fsdp")),
            P(("dp", "fsdp")),
            P(("dp", "fsdp")),
            P(("dp", "fsdp"), None),
            P(("dp", "fsdp")),
            P(("dp", "fsdp")),
            P(("dp", "fsdp"), None),
            P(None, ("dp", "fsdp"), None),
            P(None, ("dp", "fsdp"), None),
            P(("dp", "fsdp")),
            P(("dp", "fsdp")),
        ),
        check_vma=False,
    )
```

```python
import functools

import jax
import jax.numpy as jnp
from jax import lax
from jax.experimental import pallas as pl
from jax.experimental.pallas import tpu as pltpu
from jax.sharding import PartitionSpec as P

HEADS = 8
EXPERTS = 4
KERNEL = 15
HEAD_DIM = 64
CAPACITY = 512
AXES = ("dp", "fsdp")

eps = 1e-05
blocked = -1000000000.0


def product(left, right):
    return jnp.dot(left, right, preferred_element_type=jnp.float32)


NN = (((1,), (0,)), ((), ()))
NT = (((1,), (1,)), ((), ()))
TN = (((0,), (0,)), ((), ()))


def mul(left, right, dims=NN):
    return lax.dot_general(left, right, dims, preferred_element_type=jnp.float32)


def norm_parts(value):
    average = jnp.mean(value, -1, keepdims=True)
    centered = value - average
    spread = jnp.mean(centered * centered, -1, keepdims=True)
    inverse = lax.rsqrt(spread + eps)
    return centered * inverse, inverse


def norm_slope(unit, inverse, slope, gain):
    scaled = slope * gain
    first = jnp.mean(scaled, -1, keepdims=True)
    second = jnp.mean(scaled * unit, -1, keepdims=True)
    return (scaled - first - unit * second) * inverse


def head_mask(rows, head):
    lane = lax.broadcasted_iota(jnp.int32, (rows, 2 * HEAD_DIM), 1)
    return (lane >= head * HEAD_DIM) & (lane < (head + 1) * HEAD_DIM)


def angles(length, width):
    freqs = jnp.exp(jnp.arange(0, width, 2).astype(jnp.float32) * (-jnp.log(10000.0) / width))
    coarse = (jnp.arange(length // 32) * 32).astype(jnp.float32)[:, None] * freqs[None, :]
    fine = jnp.arange(32).astype(jnp.float32)[:, None] * freqs[None, :]
    cos_a, sin_a = jnp.cos(coarse)[:, None], jnp.sin(coarse)[:, None]
    cos_b, sin_b = jnp.cos(fine)[None], jnp.sin(fine)[None]
    cosine = (cos_a * cos_b - sin_a * sin_b).reshape(length, width // 2)
    sine = (sin_a * cos_b + cos_a * sin_b).reshape(length, width // 2)
    return cosine, sine


def attend_forward_kernel(
    resid_ref,
    gain_ref,
    bias_ref,
    pq_ref,
    pk_ref,
    pv_ref,
    rel_ref,
    cb_ref,
    pb_ref,
    segr_ref,
    segc_ref,
    tab_ref,
    cos_ref,
    sin_ref,
    ha_ref,
    qu_ref,
    qv_ref,
    k_ref,
    v_ref,
    p_ref,
    ctx_ref,
    kt_ref,
):
    length = resid_ref.shape[0]
    half = cos_ref.shape[1]
    pair = 2 * HEAD_DIM
    rows = 256

    @pl.when(pl.program_id(0) == 0)
    def first():
        unit, inverse = norm_parts(resid_ref[...])
        ha_ref[...] = (unit * gain_ref[...] + bias_ref[...]).astype(jnp.bfloat16)
        kt_ref[:, pair:] = tab_ref[...]

    normed = ha_ref[...]
    query = mul(normed, pq_ref[...])
    keys = mul(normed, pk_ref[...]).astype(jnp.bfloat16)
    k_ref[...] = keys
    kt_ref[:, :pair] = keys
    v_ref[...] = mul(normed, pv_ref[...]).astype(jnp.bfloat16)
    qu_ref[...] = (query + cb_ref[...]).astype(jnp.bfloat16)
    qv_ref[...] = (query + pb_ref[...]).astype(jnp.bfloat16)

    def block(index, carry):
        at = pl.ds(pl.multiple_of(index * rows, rows), rows)
        same = segc_ref[at, :] == segr_ref[...]
        cosine, sine = cos_ref[at, :], sin_ref[at, :]
        contexts = []
        for head in range(2):
            own = head_mask(rows, head)
            part_u = jnp.where(own, qu_ref[at, :], 0) * 0.125
            part_v = jnp.where(own, qv_ref[at, :], 0)
            coef = mul(part_v, rel_ref[...], NT) * 0.125
            left, right = coef[:, :half], coef[:, half:]
            turned_a = (left * sine + right * cosine).astype(jnp.bfloat16)
            turned_b = (right * sine - left * cosine).astype(jnp.bfloat16)
            scores = mul(
                jnp.concatenate([part_u.astype(jnp.bfloat16), turned_a, turned_b], 1), kt_ref[...], NT
            )
            scores = jnp.where(same, scores, blocked)
            peak = jnp.max(scores, -1, keepdims=True)
            raised = jnp.exp(scores - peak)
            summed = jnp.sum(raised, -1, keepdims=True)
            chances = (raised * (1.0 / summed)).astype(jnp.bfloat16)
            p_ref[head, at, :] = chances
            contexts.append(mul(chances, v_ref[...]))
        ctx_ref[at, :] = jnp.where(head_mask(rows, 0), contexts[0], contexts[1]).astype(jnp.bfloat16)
        return carry

    lax.fori_loop(0, length // rows, block, 0)


def attend_backward_kernel(
    p_ref,
    tab_ref,
    cos_ref,
    sin_ref,
    resid_ref,
    slope_ref,
    ha_ref,
    qu_ref,
    qv_ref,
    k_ref,
    v_ref,
    ctx_ref,
    ao_ref,
    pq_ref,
    pk_ref,
    pv_ref,
    rel_ref,
    gain_ref,
    g1_ref,
    dao_ref,
    dpq_ref,
    dpk_ref,
    dpv_ref,
    drel_ref,
    dcb_ref,
    dpb_ref,
    dgain_ref,
    dbias_ref,
    kt_ref,
    dout_ref,
    dctx_ref,
    dn_ref,
    dq_ref,
    dkt_ref,
    dvt_ref,
    drt_ref,
):
    length = resid_ref.shape[0]
    half = cos_ref.shape[1]
    pair = 2 * HEAD_DIM
    rows = 256
    step = pl.program_id(0)

    @pl.when(step == 0)
    def first():
        dout_ref[...] = slope_ref[...].astype(jnp.bfloat16)
        kt_ref[:, pair:] = tab_ref[...]
        dn_ref[...] = jnp.zeros_like(dn_ref)

    kt_ref[:, :pair] = k_ref[...]
    dao_ref[...] = mul(ctx_ref[...], dout_ref[...], TN)
    dctx_ref[...] = mul(dout_ref[...], ao_ref[...], NT).astype(jnp.bfloat16)
    dkt_ref[...] = jnp.zeros_like(dkt_ref)
    dvt_ref[...] = jnp.zeros_like(dvt_ref)
    drt_ref[...] = jnp.zeros_like(drt_ref)
    dcb_ref[...] = jnp.zeros_like(dcb_ref)
    dpb_ref[...] = jnp.zeros_like(dpb_ref)

    def block(index, carry):
        at = pl.ds(pl.multiple_of(index * rows, rows), rows)
        cosine, sine = cos_ref[at, :], sin_ref[at, :]
        total = jnp.zeros((rows, pair), jnp.float32)
        sum_u = jnp.zeros((1, pair), jnp.float32)
        sum_v = jnp.zeros((1, pair), jnp.float32)
        for head in range(2):
            own = head_mask(rows, head)
            part = jnp.where(own, dctx_ref[at, :], 0)
            low = p_ref[head, at, :]
            chances = low.astype(jnp.float32)
            raw = mul(part, v_ref[...], NT)
            weighted = chances * raw
            delta = jnp.sum(weighted, -1, keepdims=True)
            slope = ((weighted - chances * delta) * 0.125).astype(jnp.bfloat16)
            dvt_ref[...] += mul(part, low, TN)
            dkt_ref[...] += mul(jnp.where(own, qu_ref[at, :], 0), slope, TN)
            wide = mul(slope, kt_ref[...])
            slope_u = jnp.where(own, wide[:, :pair], 0.0)
            first, second = wide[:, pair : pair + half], wide[:, pair + half :]
            coef = jnp.concatenate(
                [
                    (first * sine - second * cosine).astype(jnp.bfloat16),
                    (first * cosine + second * sine).astype(jnp.bfloat16),
                ],
                1,
            )
            slope_v = jnp.where(own, mul(coef, rel_ref[...]), 0.0)
            drt_ref[...] += mul(jnp.where(own, qv_ref[at, :], 0), coef, TN)
            total = total + slope_u + slope_v
            sum_u = sum_u + jnp.sum(slope_u, 0, keepdims=True)
            sum_v = sum_v + jnp.sum(slope_v, 0, keepdims=True)
        dq_ref[at, :] = total
        dcb_ref[...] += sum_u
        dpb_ref[...] += sum_v
        return carry

    lax.fori_loop(0, length // rows, block, 0)
    low_q = dq_ref[...].astype(jnp.bfloat16)
    low_k = dkt_ref[...].T.astype(jnp.bfloat16)
    low_v = dvt_ref[...].T.astype(jnp.bfloat16)
    drel_ref[...] = drt_ref[...].T
    normed = ha_ref[...]
    dpq_ref[...] = mul(normed, low_q, TN)
    dpk_ref[...] = mul(normed, low_k, TN)
    dpv_ref[...] = mul(normed, low_v, TN)
    dn_ref[...] += (
        mul(low_q, pq_ref[...], NT) + mul(low_k, pk_ref[...], NT) + mul(low_v, pv_ref[...], NT)
    )

    @pl.when(step == pl.num_programs(0) - 1)
    def last():
        unit, inverse = norm_parts(resid_ref[...])
        slope = dn_ref[...]
        dgain_ref[...] = jnp.sum(slope * unit, 0, keepdims=True)
        dbias_ref[...] = jnp.sum(slope, 0, keepdims=True)
        g1_ref[...] = slope_ref[...] + norm_slope(unit, inverse, slope, gain_ref[...])


def whole(shape):
    return pl.BlockSpec(shape, lambda p: (0,) * len(shape))


def columns(rows, width, shift=0):
    return pl.BlockSpec((rows, width), lambda p: (0, p + shift))


def attention_forward(resid, segments, weights, tables):
    gain, bias, project_in, relative, content_bias, position_bias, attend_out = weights
    table, cosine, sine = tables
    length, width = resid.shape
    pair = 2 * HEAD_DIM
    pairs = HEADS // 2
    low = jnp.bfloat16
    shape = jax.ShapeDtypeStruct
    return pl.pallas_call(
        attend_forward_kernel,
        grid=(pairs,),
        in_specs=[
            whole((length, width)),
            whole((1, width)),
            whole((1, width)),
            columns(width, pair),
            columns(width, pair, pairs),
            columns(width, pair, 2 * pairs),
            columns(width, pair),
            columns(1, pair),
            columns(1, pair),
            whole((1, length)),
            whole((length, 1)),
            whole((length, width)),
            whole((length, width // 2)),
            whole((length, width // 2)),
        ],
        out_specs=[whole((length, width))]
        + [columns(length, pair)] * 4
        + [pl.BlockSpec((2, length, length), lambda p: (p, 0, 0)), columns(length, pair)],
        out_shape=[shape((length, width), low)] * 5
        + [shape((HEADS, length, length), low), shape((length, width), low)],
        scratch_shapes=[pltpu.VMEM((length, pair + width), low)],
        compiler_params=pltpu.CompilerParams(vmem_limit_bytes=56 * 1024 * 1024),
        cost_estimate=pl.CostEstimate(flops=24 * 10**9, bytes_accessed=30 * 10**6, transcendentals=8 * 10**6),
        name="attend_forward",
    )(
        resid,
        gain,
        bias,
        project_in,
        project_in,
        project_in,
        relative,
        content_bias,
        position_bias,
        segments,
        segments.reshape(length, 1),
        table,
        cosine,
        sine,
    )


def attention_backward(resid, slope, weights, tables, kept):
    gain, bias, project_in, relative, content_bias, position_bias, attend_out = weights
    table, cosine, sine = tables
    normed, query_u, query_v, keys, values, chances, context = kept
    length, width = resid.shape
    pair = 2 * HEAD_DIM
    pairs = HEADS // 2
    low, full = jnp.bfloat16, jnp.float32
    shape = jax.ShapeDtypeStruct
    return pl.pallas_call(
        attend_backward_kernel,
        grid=(pairs,),
        in_specs=[
            pl.BlockSpec((2, length, length), lambda p: (p, 0, 0)),
            whole((length, width)),
            whole((length, width // 2)),
            whole((length, width // 2)),
            whole((length, width)),
            whole((length, width)),
            whole((length, width)),
        ]
        + [columns(length, pair)] * 5
        + [
            pl.BlockSpec((pair, width), lambda p: (p, 0)),
            columns(width, pair),
            columns(width, pair, pairs),
            columns(width, pair, 2 * pairs),
            columns(width, pair),
            whole((1, width)),
        ],
        out_specs=[
            whole((length, width)),
            pl.BlockSpec((pair, width), lambda p: (p, 0)),
            columns(width, pair),
            columns(width, pair),
            columns(width, pair),
            columns(width, pair),
            columns(1, pair),
            columns(1, pair),
            whole((1, width)),
            whole((1, width)),
        ],
        out_shape=[shape((length, width), full)]
        + [shape((width, width), full)] * 5
        + [shape((1, width), full)] * 4,
        scratch_shapes=[
            pltpu.VMEM((length, pair + width), low),
            pltpu.VMEM((length, width), low),
            pltpu.VMEM((length, pair), low),
            pltpu.VMEM((length, width), full),
            pltpu.VMEM((length, pair), full),
            pltpu.VMEM((pair, length), full),
            pltpu.VMEM((pair, length), full),
            pltpu.VMEM((pair, width), full),
        ],
        compiler_params=pltpu.CompilerParams(vmem_limit_bytes=60 * 1024 * 1024),
        cost_estimate=pl.CostEstimate(flops=40 * 10**9, bytes_accessed=40 * 10**6, transcendentals=0),
        name="attend_backward",
    )(
        chances,
        table,
        cosine,
        sine,
        resid,
        slope,
        normed,
        query_u,
        query_v,
        keys,
        values,
        context,
        attend_out,
        project_in,
        project_in,
        project_in,
        relative,
        gain,
    )


def grid_of(count_dp, count_fsdp):
    depth = 4 if count_dp % 4 == 0 else count_dp
    cores = 2 if count_fsdp % 2 == 0 else 1
    return {"z": depth, "y": count_dp // depth, "x": count_fsdp // cores, "c": cores}


def sizes():
    return grid_of(lax.axis_size("dp"), lax.axis_size("fsdp"))


def place(grid, axis):
    index = lax.axis_index(AXES)
    for name in ("c", "x", "y", "z"):
        if name == axis:
            return index % grid[name]
        index = index // grid[name]


def number(grid, at):
    return ((at["z"] * grid["y"] + at["y"]) * grid["x"] + at["x"]) * grid["c"] + at["c"]


def move(value, grid, **steps):
    pairs = []
    for z in range(grid["z"]):
        for y in range(grid["y"]):
            for x in range(grid["x"]):
                for c in range(grid["c"]):
                    at = {"z": z, "y": y, "x": x, "c": c}
                    to = {name: (at[name] + steps.get(name, 0)) % grid[name] for name in at}
                    pairs.append((number(grid, at), number(grid, to)))
    return lax.ppermute(value, AXES, pairs)


def total_of(value):
    count = lax.axis_size(AXES)
    bit = 1
    while bit < count:
        value = value + lax.ppermute(value, AXES, [(d, d ^ bit) for d in range(count)])
        bit *= 2
    return value


def gather_small(value):
    count = lax.axis_size(AXES)
    index = lax.axis_index(AXES)
    value = value[None]
    bit = 1
    while bit < count:
        other = lax.ppermute(value, AXES, [(d, d ^ bit) for d in range(count)])
        upper = (index // bit) % 2 == 1
        value = jnp.where(
            upper, jnp.concatenate([other, value], 0), jnp.concatenate([value, other], 0)
        )
        bit *= 2
    return value


PLANE = ((0, 1), (1, 0), (1, 1))


def joined(pieces):
    return (
        jnp.concatenate([value for value, _ in pieces], 0),
        [offset for _, offsets in pieces for offset in offsets],
    )


def along_depth(piece, grid):
    value, offsets = piece
    steps = [piece]
    for step in range(1, grid["z"]):
        value = move(value, grid, z=1)
        steps.append((value, [dict(o, z=(o["z"] - step) % grid["z"]) for o in offsets]))
    return steps


def over_plane(piece, grid):
    value, offsets = piece
    return [piece] + [
        (move(value, grid, y=dy, x=dx), [dict(o, y=o["y"] ^ dy, x=o["x"] ^ dx) for o in offsets])
        for dy, dx in PLANE
    ]


def over_cores(pieces, grid):
    return pieces + [
        (move(value, grid, c=1), [dict(o, c=1 - o["c"]) for o in offsets])
        for value, offsets in pieces
    ]


def gather_pieces(block, grid, depth_first):
    piece = (block[None], [{"z": 0, "y": 0, "x": 0, "c": 0}])
    if depth_first:
        pieces = over_plane(joined(along_depth(piece, grid)), grid)
    else:
        pieces = along_depth(joined(over_plane(piece, grid)), grid)
    return over_cores(pieces, grid)


def owners(pieces, grid):
    own = {axis: place(grid, axis) for axis in grid}
    found = []
    for _, offsets in pieces:
        for offset in offsets:
            at = {axis: (own[axis] + offset[axis]) % grid[axis] for axis in grid}
            found.append(number(grid, at))
    return jnp.stack(found)


FAST = {"z": 4, "y": 2, "x": 2, "c": 2}


def gather_experts(value, depth_first):
    grid = sizes()
    if grid == FAST:
        pieces = gather_pieces(value, grid, depth_first)
        return [piece for piece, _ in pieces], owners(pieces, grid)
    return gather_whole(value)


def gather_whole(value):
    grid = sizes()
    if grid == FAST:
        blocks = lax.all_gather(value, AXES, axis=0, tiled=False)
        return [blocks], jnp.arange(blocks.shape[0], dtype=jnp.int32)
    blocks = lax.all_gather(value, AXES, axis=1, tiled=True)
    return [blocks[None]], jnp.zeros((1,), jnp.int32)


def block_at(value, index, at):
    return lax.dynamic_index_in_dim(value, index % value.shape[at], at, keepdims=False)


def wide(value):
    return value.astype(jnp.float32)


def sum_cores(value, grid, at):
    own = place(grid, "c")
    other = move(block_at(value, own + 1, at), grid, c=1)
    return (wide(block_at(value, own, at)) + wide(other)).astype(value.dtype)


def sum_plane(value, grid, at, dtype):
    y, x = place(grid, "y"), place(grid, "x")

    def block(dy, dx):
        return block_at(block_at(value, y + dy, at), x + dx, at)

    total = wide(block(0, 0))
    for dy, dx in PLANE:
        total = total + wide(move(block(dy, dx), grid, y=dy, x=dx))
    return total.astype(dtype)


def sum_depth(value, grid, dtype):
    length = grid["z"]
    own = place(grid, "z")
    part = block_at(value, own + length - 1, 0)
    for step in range(1, length):
        total = wide(block_at(value, own + 2 * length - 1 - step, 0)) + wide(move(part, grid, z=1))
        part = total.astype(dtype if step == length - 1 else value.dtype)
    return part


def scatter_blocks(value, depth_first):
    grid = sizes()
    if grid != FAST:
        return wide(lax.psum_scatter(value, AXES, scatter_dimension=0, tiled=False))
    value = value.reshape((4, 2, 2, 2) + value.shape[1:])
    value = sum_cores(value, grid, 3)
    if depth_first:
        return sum_plane(sum_depth(value, grid, value.dtype), grid, 0, jnp.float32)
    return sum_depth(sum_plane(value, grid, 1, value.dtype), grid, jnp.float32)


def by_devices(value):
    if value.shape[0] > 1:
        return value
    devices = lax.axis_size(AXES)
    return value.reshape((EXPERTS, devices, -1, value.shape[3])).transpose(1, 0, 2, 3)


ROWS = (256, 384, 512)


def one_hot_rows(pos_row, base, rows):
    slot = lax.broadcasted_iota(jnp.int32, (rows, pos_row.shape[1]), 0) + base
    return (slot == pos_row).astype(jnp.float32).astype(jnp.bfloat16)


def one_hot_columns(pos_col, base, rows):
    slot = lax.broadcasted_iota(jnp.int32, (pos_col.shape[0], rows), 1) + base
    return (slot == pos_col).astype(jnp.float32).astype(jnp.bfloat16)


def routed(route_col):
    lane = lax.broadcasted_iota(jnp.int32, (route_col.shape[0], 128), 1)
    return (lane == route_col).astype(jnp.float32)


def sigmoid(value):
    return 1.0 / (1.0 + jnp.exp(-value))


def split_mul(wide, narrow, dims):
    high = wide.astype(jnp.bfloat16)
    rest = (wide - high.astype(jnp.float32)).astype(jnp.bfloat16)
    return mul(high, narrow, dims) + mul(rest, narrow, dims)


def route_probs(normed, embed, router_ref):
    width = normed.shape[1]
    logits = mul(normed, router_ref[:width, :]) + mul(embed, router_ref[width:, :])
    lane = lax.broadcasted_iota(jnp.int32, logits.shape, 1)
    logits = jnp.where(lane < EXPERTS, logits, -jnp.inf)
    raised = jnp.exp(logits - jnp.max(logits, -1, keepdims=True))
    return raised / jnp.sum(raised, -1, keepdims=True)


def sized(count, body):
    lower = -1
    for rows in ROWS:
        pl.when((count > lower) & (count <= rows))(functools.partial(body, rows))
        lower = rows


def assemble(refs, ids_ref, whole_ref):
    at = 0
    for ref in refs:
        rows = ref.shape[2]
        for block in range(ref.shape[0]):
            start = pl.multiple_of(ids_ref[at] * rows, rows)
            whole_ref[pl.ds(start, rows), :] = ref[block, 0]
            at += 1


class Weights:
    def __init__(self, gathered):
        self.arrays, self.ids = gathered
        rows = sum(piece.shape[0] * piece.shape[2] for piece in self.arrays)
        self.shape = (rows, self.arrays[0].shape[3])
        self.rows = self.arrays[0].shape[2]

    def specs(self):
        return [by_owner(piece.shape) for piece in self.arrays]


def fixed(shape):
    return pl.BlockSpec(shape, lambda e, *_: (0,) * len(shape))


def by_expert(shape):
    return pl.BlockSpec((1,) + shape, lambda e, *_: (e,) + (0,) * len(shape))


def by_owner(shape):
    return pl.BlockSpec((shape[0], 1) + shape[2:], lambda e, *_: (0, e, 0, 0))


def grads_shape(weights):
    count = weights.shape[0] // weights.rows
    return (count, EXPERTS, weights.rows, weights.shape[1])


def expert_call(kernel, name, counts, weights, inputs, outputs, scratch, flops):
    scalars = [counts] + [weight.ids for weight in weights]
    arrays = [piece for weight in weights for piece in weight.arrays]
    n_in, n_out = len(inputs), len(outputs)

    def body(*refs):
        count_ref, *ids = refs[: len(scalars)]
        refs = refs[len(scalars) :]
        pieces, refs = refs[: len(arrays)], refs[len(arrays) :]
        operands, results, rest = refs[:n_in], refs[n_in : n_in + n_out], refs[n_in + n_out :]
        expert = pl.program_id(0)
        for at, weight in enumerate(weights):
            own = pieces[: len(weight.arrays)]
            pieces = pieces[len(weight.arrays) :]
            assemble(own, ids[at], rest[at])
        kernel(expert, count_ref[expert], *rest[: len(weights)], *operands, *results, *rest[len(weights) :])

    return pl.pallas_call(
        body,
        grid_spec=pltpu.PrefetchScalarGridSpec(
            num_scalar_prefetch=len(scalars),
            grid=(EXPERTS,),
            in_specs=[spec for weight in weights for spec in weight.specs()]
            + [spec for _, spec in inputs],
            out_specs=[spec for _, spec in outputs],
            scratch_shapes=[pltpu.VMEM(weight.shape, jnp.bfloat16) for weight in weights] + scratch,
        ),
        out_shape=[shape for shape, _ in outputs],
        compiler_params=pltpu.CompilerParams(vmem_limit_bytes=60 * 1024 * 1024),
        cost_estimate=pl.CostEstimate(
            flops=flops, bytes_accessed=20 * 10**6, transcendentals=4 * 10**6
        ),
        name=name,
    )(*scalars, *arrays, *[value for value, _ in inputs])


def struct(shape, dtype=jnp.float32):
    return jax.ShapeDtypeStruct(shape, dtype)


def whole_in(value):
    return (value, fixed(value.shape))


def whole_out(shape, dtype=jnp.float32):
    return (struct(shape, dtype), fixed(shape))


def expert_in(value):
    return (value, by_expert(value.shape[1:]))


def expert_out(shape, dtype=jnp.bfloat16):
    return (struct((EXPERTS,) + shape, dtype), by_expert(shape))


def spans(hidden):
    chunk = 512
    return [slice(start, start + chunk) for start in range(0, hidden, chunk)]


def up_part(expert, rows, up_ref, normed_ref, posr_ref, picked_ref, inner_ref, then=None):
    hot = one_hot_rows(posr_ref[...], expert * CAPACITY, rows)
    picked = mul(hot, normed_ref[...]).astype(jnp.bfloat16)
    picked_ref[0, :rows, :] = picked
    total = None
    for span in spans(up_ref.shape[1]):
        inner = mul(picked, up_ref[:, span])
        inner_ref[0, :rows, span] = inner.astype(jnp.bfloat16)
        if then is not None:
            part = then(inner, span)
            total = part if total is None else total + part
    return total


def first_up_kernel(expert, count, up_ref, normed_ref, posr_ref, picked_ref, inner_ref):
    def run(rows):
        up_part(expert, rows, up_ref, normed_ref, posr_ref, picked_ref, inner_ref)

    sized(count, run)


def first_up_call(counts, pos_row, normed, up):
    length, width = normed.shape
    return expert_call(
        first_up_kernel,
        "first_up",
        counts,
        [up],
        [whole_in(normed), whole_in(pos_row)],
        [expert_out((CAPACITY, width)), expert_out((CAPACITY, up.shape[1]))],
        [],
        5 * 10**9,
    )


def first_down_kernel(
    expert, count, down_ref, inner_ref, posc_ref, resid_ref, probs_ref, route_ref, out_ref, branch_ref
):
    @pl.when(expert == 0)
    def clear():
        branch_ref[...] = jnp.zeros_like(branch_ref)

    def run(rows):
        total = None
        for span in spans(down_ref.shape[0]):
            inner = inner_ref[0, :rows, span].astype(jnp.float32)
            part = mul((inner * sigmoid(inner)).astype(jnp.bfloat16), down_ref[span, :])
            total = part if total is None else total + part
        hot = one_hot_columns(posc_ref[...], expert * CAPACITY, rows)
        branch_ref[...] += mul(hot, total.astype(jnp.bfloat16))

    sized(count, run)

    @pl.when(expert == EXPERTS - 1)
    def last():
        gate = jnp.sum(probs_ref[...] * routed(route_ref[...]), -1, keepdims=True)
        out_ref[...] = resid_ref[...].astype(jnp.float32) + 0.5 * gate * branch_ref[...]


def first_down_call(counts, pos_col, inner, resid, probs, routes, down):
    shape = resid.shape
    return expert_call(
        first_down_kernel,
        "first_down",
        counts,
        [down],
        [expert_in(inner)] + [whole_in(v) for v in (pos_col, resid, probs, routes)],
        [whole_out(shape), whole_out(shape)],
        [],
        5 * 10**9,
    )


def second_forward_kernel(
    expert, count, up_ref, down_ref,
    normed_ref, posr_ref, posc_ref, resid_ref, probs_ref, route_ref, cot_ref, gain_ref, bias_ref,
    picked_ref, inner_ref, branch_ref, result_ref, g4_ref, dgain_ref, dbias_ref,
):
    @pl.when(expert == 0)
    def clear():
        branch_ref[...] = jnp.zeros_like(branch_ref)

    def run(rows):
        def then(inner, span):
            return mul((inner * sigmoid(inner)).astype(jnp.bfloat16), down_ref[span, :])

        total = up_part(expert, rows, up_ref, normed_ref, posr_ref, picked_ref, inner_ref, then)
        hot = one_hot_columns(posc_ref[...], expert * CAPACITY, rows)
        branch_ref[...] += mul(hot, total.astype(jnp.bfloat16))

    sized(count, run)

    @pl.when(expert == EXPERTS - 1)
    def last():
        gate = jnp.sum(probs_ref[...] * routed(route_ref[...]), -1, keepdims=True)
        unit, inverse = norm_parts(resid_ref[...] + 0.5 * gate * branch_ref[...])
        gain = gain_ref[...]
        cot = cot_ref[...].astype(jnp.float32)
        result_ref[...] = (unit * gain + bias_ref[...]).astype(jnp.bfloat16)
        dgain_ref[...] = jnp.sum(cot * unit, 0, keepdims=True)
        dbias_ref[...] = jnp.sum(cot, 0, keepdims=True)
        g4_ref[...] = norm_slope(unit, inverse, cot, gain)


def second_forward_call(counts, pos_row, pos_col, normed, resid, probs, routes, cot, gain, bias, up, down):
    length, width = normed.shape
    return expert_call(
        second_forward_kernel,
        "second_forward",
        counts,
        [up, down],
        [whole_in(v) for v in (normed, pos_row, pos_col, resid, probs, routes, cot, gain, bias)],
        [
            expert_out((CAPACITY, width)),
            expert_out((CAPACITY, up.shape[1])),
            whole_out((length, width)),
            whole_out((length, width), jnp.bfloat16),
            whole_out((length, width)),
            whole_out((1, width)),
            whole_out((1, width)),
        ],
        [],
        10 * 10**9,
    )


def enter_slope(slope_ref, probs_ref, route_ref, branch_ref, low_ref, dlogits_ref):
    chosen = routed(route_ref[...])
    probs = probs_ref[...]
    gate = jnp.sum(probs * chosen, -1, keepdims=True)
    slope = slope_ref[...]
    low_ref[...] = (0.5 * gate * slope).astype(jnp.bfloat16)
    dgate = 0.5 * jnp.sum(slope * branch_ref[...], -1, keepdims=True)
    dlogits_ref[...] = probs * (chosen - gate) * dgate


def leave_slope(
    dnorm, dlogits, slope_ref, resid_ref, normed_ref, embed_ref, gain_ref,
    out_ref, dgain_ref, dbias_ref, drouter_ref,
):
    width = resid_ref.shape[1]
    unit, inverse = norm_parts(resid_ref[...].astype(jnp.float32))
    dgain_ref[...] = jnp.sum(dnorm * unit, 0, keepdims=True)
    dbias_ref[...] = jnp.sum(dnorm, 0, keepdims=True)
    out_ref[...] = slope_ref[...] + norm_slope(unit, inverse, dnorm, gain_ref[...])
    drouter_ref[:, :width] = split_mul(dlogits, normed_ref[...], TN)
    drouter_ref[:, width:] = split_mul(dlogits, embed_ref[...], TN)


def active_of(inner):
    inner = inner.astype(jnp.float32)
    return (inner * sigmoid(inner)).astype(jnp.bfloat16)


def slope_of(inner):
    inner = inner.astype(jnp.float32)
    sigma = sigmoid(inner)
    return sigma * (1.0 + inner * (1.0 - sigma))


def store_rows(ref, span, value):
    owned = ref.shape[2]
    count = span.stop - span.start
    if owned > count:
        ref[0, 0, span, :] = value
    else:
        ref[span.start // owned : span.stop // owned] = value.reshape((count // owned,) + ref.shape[1:])


def down_grads(rows, inner_ref, dpicked, ddown_ref):
    for span in spans(inner_ref.shape[2]):
        grads = mul(active_of(inner_ref[0, :rows, span]), dpicked, TN)
        store_rows(ddown_ref, span, grads.astype(jnp.bfloat16))


def up_grads(picked, dinner, span, dup_ref):
    grads = mul(picked, dinner, TN).astype(jnp.bfloat16)
    dup_ref[:, :, :, span] = grads.reshape(dup_ref.shape[:3] + (grads.shape[1],))


def first_back_kernel(
    expert, count, slope_ref, probs_ref, route_ref, branch_ref, posr_ref, inner_ref,
    ddown_ref, dpicked_ref, dlogits_ref,
    low_ref,
):
    @pl.when(expert == 0)
    def first():
        enter_slope(slope_ref, probs_ref, route_ref, branch_ref, low_ref, dlogits_ref)

    def run(rows):
        hot = one_hot_rows(posr_ref[...], expert * CAPACITY, rows)
        dpicked = mul(hot, low_ref[...]).astype(jnp.bfloat16)
        dpicked_ref[0, :rows, :] = dpicked
        down_grads(rows, inner_ref, dpicked, ddown_ref)

    sized(count, run)


def first_back_call(counts, pos_row, slope, probs, routes, branch, inner, down):
    length, width = slope.shape
    shape = grads_shape(down)
    return expert_call(
        first_back_kernel,
        "first_down_grads",
        counts,
        [],
        [whole_in(v) for v in (slope, probs, routes, branch, pos_row)] + [expert_in(inner)],
        [
            (struct(shape, jnp.bfloat16), by_owner(shape)),
            expert_out((CAPACITY, width)),
            whole_out((length, 128)),
        ],
        [pltpu.VMEM((length, width), jnp.bfloat16)],
        5 * 10**9,
    )


def first_middle_kernel(expert, count, down_ref, dpicked_ref, picked_ref, inner_ref, dup_ref, dinner_ref):
    def run(rows):
        dpicked = dpicked_ref[0, :rows, :]
        picked = picked_ref[0, :rows, :]
        for span in spans(inner_ref.shape[2]):
            dactive = mul(dpicked, down_ref[span, :], NT)
            dinner = (dactive * slope_of(inner_ref[0, :rows, span])).astype(jnp.bfloat16)
            dinner_ref[0, :rows, span] = dinner
            up_grads(picked, dinner, span, dup_ref)

    sized(count, run)


def first_middle_call(counts, dpicked, picked, inner, up, down):
    shape = grads_shape(up)
    return expert_call(
        first_middle_kernel,
        "first_up_grads",
        counts,
        [down],
        [expert_in(v) for v in (dpicked, picked, inner)],
        [(struct(shape, jnp.bfloat16), by_owner(shape)), expert_out(inner.shape[1:])],
        [],
        9 * 10**9,
    )


def first_leave_kernel(
    expert, count, up_ref, dinner_ref, posc_ref, dlogits_ref, router_ref, slope_ref, resid_ref, normed_ref,
    embed_ref, gain_ref,
    out_ref, dgain_ref, dbias_ref, drouter_ref,
    dnorm_ref,
):
    width = up_ref.shape[0]

    @pl.when(expert == 0)
    def first():
        dnorm_ref[...] = split_mul(dlogits_ref[...], router_ref[:width, :], NT)

    def run(rows):
        total = mul(dinner_ref[0, :rows, :], up_ref[...], NT).astype(jnp.bfloat16)
        dnorm_ref[...] += mul(one_hot_columns(posc_ref[...], expert * CAPACITY, rows), total)

    sized(count, run)

    @pl.when(expert == EXPERTS - 1)
    def last():
        leave_slope(
            dnorm_ref[...], dlogits_ref[...], slope_ref, resid_ref, normed_ref, embed_ref, gain_ref,
            out_ref, dgain_ref, dbias_ref, drouter_ref,
        )


def first_leave_call(counts, pos_col, dinner, dlogits, router, slope, resid, normed, embedding, gain, up):
    length, width = slope.shape
    return expert_call(
        first_leave_kernel,
        "first_leave",
        counts,
        [up],
        [expert_in(dinner)]
        + [whole_in(v) for v in (pos_col, dlogits, router, slope, resid, normed, embedding, gain)],
        [
            whole_out((length, width)),
            whole_out((1, width)),
            whole_out((1, width)),
            whole_out((128, 2 * width)),
        ],
        [pltpu.VMEM((length, width), jnp.float32)],
        5 * 10**9,
    )


def second_back_kernel(
    expert, count, up_ref, down_ref, slope_ref, probs_ref, route_ref, branch_ref, posr_ref, posc_ref, inner_ref,
    router_ref, resid_ref, normed_ref, embed_ref, gain_ref,
    out_ref, dgain_ref, dbias_ref, drouter_ref, dpicked_ref, dinner_ref,
    low_ref, dlogits_ref, dnorm_ref,
):
    width = up_ref.shape[0]

    @pl.when(expert == 0)
    def first():
        enter_slope(slope_ref, probs_ref, route_ref, branch_ref, low_ref, dlogits_ref)
        dnorm_ref[...] = split_mul(dlogits_ref[...], router_ref[:width, :], NT)

    def run(rows):
        hot = one_hot_rows(posr_ref[...], expert * CAPACITY, rows)
        dpicked = mul(hot, low_ref[...]).astype(jnp.bfloat16)
        dpicked_ref[0, :rows, :] = dpicked
        total = None
        for span in spans(up_ref.shape[1]):
            dactive = mul(dpicked, down_ref[span, :], NT)
            dinner = (dactive * slope_of(inner_ref[0, :rows, span])).astype(jnp.bfloat16)
            dinner_ref[0, :rows, span] = dinner
            part = mul(dinner, up_ref[:, span], NT)
            total = part if total is None else total + part
        hot = one_hot_columns(posc_ref[...], expert * CAPACITY, rows)
        dnorm_ref[...] += mul(hot, total.astype(jnp.bfloat16))

    sized(count, run)

    @pl.when(expert == EXPERTS - 1)
    def last():
        leave_slope(
            dnorm_ref[...], dlogits_ref[...], slope_ref, resid_ref, normed_ref, embed_ref, gain_ref,
            out_ref, dgain_ref, dbias_ref, drouter_ref,
        )


def second_back_call(
    counts, pos_row, pos_col, slope, probs, routes, branch, inner, router, resid, normed, embedding, gain, up, down
):
    length, width = slope.shape
    return expert_call(
        second_back_kernel,
        "second_back",
        counts,
        [up, down],
        [whole_in(v) for v in (slope, probs, routes, branch, pos_row, pos_col)]
        + [expert_in(inner)]
        + [whole_in(v) for v in (router, resid, normed, embedding, gain)],
        [
            whole_out((length, width)),
            whole_out((1, width)),
            whole_out((1, width)),
            whole_out((128, 2 * width)),
            expert_out((CAPACITY, width)),
            expert_out(inner.shape[1:]),
        ],
        [
            pltpu.VMEM((length, width), jnp.bfloat16),
            pltpu.VMEM((length, 128), jnp.float32),
            pltpu.VMEM((length, width), jnp.float32),
        ],
        10 * 10**9,
    )


def second_grads_kernel(expert, count, picked_ref, inner_ref, dpicked_ref, dinner_ref, out_ref):
    def run(rows):
        picked = picked_ref[0, :rows, :]
        dpicked = dpicked_ref[0, :rows, :]
        owned = out_ref.shape[2] // 2
        width = dpicked.shape[1]
        for span in spans(inner_ref.shape[2]):
            chunk = span.stop - span.start
            grads = mul(picked, dinner_ref[0, :rows, span], TN).astype(jnp.bfloat16)
            out_ref[:, :, :owned, span] = grads.reshape((-1, 1, owned, chunk))
            grads = mul(active_of(inner_ref[0, :rows, span]), dpicked, TN).astype(jnp.bfloat16)
            across = inner_ref.shape[2] // width
            if owned >= chunk:
                at = span.start // owned * width
                out_ref[0, 0, owned:, at : at + width] = grads
                continue
            first = span.start // (across * owned)
            count = chunk // (across * owned)
            grads = grads.reshape((count, 1, across, owned, width))
            for at in range(across):
                out_ref[first : first + count, :, owned:, at * width : (at + 1) * width] = grads[:, :, at]

    sized(count, run)


def second_grads_call(counts, picked, inner, dpicked, dinner, devices):
    hidden, width = inner.shape[2], picked.shape[2]
    shape = (devices, EXPERTS, 2 * width // devices, hidden)
    return expert_call(
        second_grads_kernel,
        "second_grads",
        counts,
        [],
        [expert_in(v) for v in (picked, inner, dpicked, dinner)],
        [(struct(shape, jnp.bfloat16), by_owner(shape))],
        [],
        10 * 10**9,
    )[0]


def enter_kernel(resid_ref, embed_ref, router_ref, gain_ref, bias_ref, normed_ref, probs_ref):
    unit, inverse = norm_parts(resid_ref[...].astype(jnp.float32))
    normed = (unit * gain_ref[...] + bias_ref[...]).astype(jnp.bfloat16)
    normed_ref[...] = normed
    probs_ref[...] = route_probs(normed, embed_ref[...], router_ref)


def expert_enter(resid, embedding, router, gain, bias):
    length, width = resid.shape
    return pl.pallas_call(
        enter_kernel,
        out_shape=[
            jax.ShapeDtypeStruct((length, width), jnp.bfloat16),
            jax.ShapeDtypeStruct((length, 128), jnp.float32),
        ],
        compiler_params=pltpu.CompilerParams(vmem_limit_bytes=40 * 1024 * 1024),
        cost_estimate=pl.CostEstimate(flops=10**9, bytes_accessed=4 * 10**6, transcendentals=10**5),
        name="expert_enter",
    )(resid, embedding, router, gain, bias)


def places(routes):
    length = routes.shape[0]
    chosen = (routes == jnp.arange(EXPERTS, dtype=jnp.int32)[None, :]).astype(jnp.float32)
    row = lax.broadcasted_iota(jnp.int32, (length, length), 0)
    before = (lax.broadcasted_iota(jnp.int32, (length, length), 1) < row).astype(jnp.bfloat16)
    earlier = product(before, chosen.astype(jnp.bfloat16))
    slot = jnp.sum(earlier * chosen, 1).astype(jnp.int32) + routes[:, 0] * CAPACITY
    counts = jnp.sum(chosen, 0).astype(jnp.int32)
    return counts, slot[None, :], slot[:, None]


CHUNK = 64
EDGE = 8


def tap_masks(segments):
    half = KERNEL // 2
    segment = segments[0]
    length = segment.shape[0]
    padded = jnp.pad(segment, (half, half), constant_values=-1)
    same = [padded[k : k + length] == segment for k in range(KERNEL)]
    masks = jnp.stack(same, 1).astype(jnp.float32)
    return jnp.pad(masks, ((0, 0), (0, 128 - KERNEL)))


def conv_front_kernel(
    resid_ref, ctx_ref, ao_ref, gain_ref, bias_ref, gated_ref, taps_ref, mask_ref,
    out_ref, normed_ref, joined_ref, depth_ref, sums_ref,
    pad_ref,
):
    length, width = resid_ref.shape
    resid = resid_ref[...] + mul(ctx_ref[...], ao_ref[...])
    out_ref[...] = resid
    unit, inverse = norm_parts(resid)
    normed = (unit * gain_ref[...] + bias_ref[...]).astype(jnp.bfloat16)
    normed_ref[...] = normed
    joined = mul(normed, gated_ref[...])
    joined_ref[...] = joined
    pad_ref[:EDGE, :] = jnp.zeros((EDGE, width), jnp.float32)
    pad_ref[EDGE + length :, :] = jnp.zeros((EDGE, width), jnp.float32)
    pad_ref[EDGE : EDGE + length, :] = joined[:, :width] * sigmoid(joined[:, width:])
    sums_ref[...] = jnp.zeros_like(sums_ref)

    def chunk(index, carry):
        at = pl.ds(pl.multiple_of(index * CHUNK, CHUNK), CHUNK)
        window = pad_ref[pl.ds(pl.multiple_of(index * CHUNK, CHUNK), CHUNK + 2 * EDGE), :]
        masks = mask_ref[at, :]
        total = jnp.zeros((CHUNK, width), jnp.float32)
        for k in range(KERNEL):
            total = total + window[k + 1 : k + 1 + CHUNK] * masks[:, k : k + 1] * taps_ref[k : k + 1, :]
        depth_ref[at, :] = total
        sums_ref[0:1, :] += jnp.sum(total, 0, keepdims=True)
        sums_ref[1:2, :] += jnp.sum(total * total, 0, keepdims=True)
        return carry

    lax.fori_loop(0, length // CHUNK, chunk, 0)


def conv_front(resid, context, attend_out, gain, bias, gated_in, taps, masks):
    length, width = resid.shape
    low, full = jnp.bfloat16, jnp.float32
    shape = jax.ShapeDtypeStruct
    return pl.pallas_call(
        conv_front_kernel,
        out_shape=[
            shape((length, width), full),
            shape((length, width), low),
            shape((length, 2 * width), full),
            shape((length, width), full),
            shape((2, width), full),
        ],
        scratch_shapes=[pltpu.VMEM((length + 2 * EDGE, width), full)],
        compiler_params=pltpu.CompilerParams(vmem_limit_bytes=56 * 1024 * 1024),
        cost_estimate=pl.CostEstimate(flops=4 * 10**9, bytes_accessed=16 * 10**6, transcendentals=10**6),
        name="conv_front",
    )(resid, context, attend_out, gain, bias, gated_in, taps, masks)


def batch_stats(stats, frames):
    average = stats[0:1, :] * (1.0 / frames)
    spread = stats[1:2, :] * (1.0 / frames) - average * average
    return average, lax.rsqrt(spread + eps)


def conv_tail_kernel(
    frames, depth_ref, stats_ref, bgain_ref, bbias_ref, point_ref, resid_ref,
    embed_ref, router_ref, gain_ref, bias_ref,
    out_ref, normed_ref, probs_ref,
):
    average, inverse = batch_stats(stats_ref[...], frames)
    shifted = (depth_ref[...] - average) * inverse * bgain_ref[...] + bbias_ref[...]
    tail = (shifted * sigmoid(shifted)).astype(jnp.bfloat16)
    resid = resid_ref[...] + mul(tail, point_ref[...])
    out_ref[...] = resid
    unit, spread = norm_parts(resid)
    normed = (unit * gain_ref[...] + bias_ref[...]).astype(jnp.bfloat16)
    normed_ref[...] = normed
    probs_ref[...] = route_probs(normed, embed_ref[...], router_ref)


def conv_tail(frames, depth, stats, bgain, bbias, point_out, resid, embedding, router, gain, bias):
    length, width = resid.shape
    shape = jax.ShapeDtypeStruct
    return pl.pallas_call(
        functools.partial(conv_tail_kernel, frames),
        out_shape=[
            shape((length, width), jnp.float32),
            shape((length, width), jnp.bfloat16),
            shape((length, 128), jnp.float32),
        ],
        compiler_params=pltpu.CompilerParams(vmem_limit_bytes=56 * 1024 * 1024),
        cost_estimate=pl.CostEstimate(flops=10**9, bytes_accessed=8 * 10**6, transcendentals=10**6),
        name="conv_tail",
    )(depth, stats, bgain, bbias, point_out, resid, embedding, router, gain, bias)


def conv_turn_kernel(
    frames, slope_ref, depth_ref, stats_ref, bgain_ref, bbias_ref, point_ref,
    dshift_ref, dpoint_ref, sums_ref,
):
    average, inverse = batch_stats(stats_ref[...], frames)
    centered = (depth_ref[...] - average) * inverse
    shifted = centered * bgain_ref[...] + bbias_ref[...]
    sigma = sigmoid(shifted)
    low = slope_ref[...].astype(jnp.bfloat16)
    dpoint_ref[...] = mul((shifted * sigma).astype(jnp.bfloat16), low, TN)
    dshift = mul(low, point_ref[...], NT) * (sigma * (1.0 + shifted * (1.0 - sigma)))
    dshift_ref[...] = dshift
    sums_ref[0:1, :] = jnp.sum(dshift * centered, 0, keepdims=True)
    sums_ref[1:2, :] = jnp.sum(dshift, 0, keepdims=True)


def conv_turn(frames, slope, depth, stats, bgain, bbias, point_out):
    length, width = slope.shape
    shape = jax.ShapeDtypeStruct
    return pl.pallas_call(
        functools.partial(conv_turn_kernel, frames),
        out_shape=[
            shape((length, width), jnp.float32),
            shape((width, width), jnp.float32),
            shape((2, width), jnp.float32),
        ],
        compiler_params=pltpu.CompilerParams(vmem_limit_bytes=56 * 1024 * 1024),
        cost_estimate=pl.CostEstimate(flops=10**9, bytes_accessed=8 * 10**6, transcendentals=10**6),
        name="conv_turn",
    )(slope, depth, stats, bgain, bbias, point_out)


def conv_back_kernel(
    frames, slope_ref, dshift_ref, depth_ref, stats_ref, sums_ref, bgain_ref, joined_ref, normed_ref,
    resid_ref, gain_ref, gated_ref, taps_ref, mask_ref,
    out_ref, dgated_ref, dtaps_ref, dgain_ref, dbias_ref,
    pad_ref, dpad_ref, dtap_ref, dglu_ref,
):
    length, width = resid_ref.shape
    average, inverse = batch_stats(stats_ref[...], frames)
    bgain = bgain_ref[...]
    sums = sums_ref[...] * (1.0 / frames) * bgain
    centered = (depth_ref[...] - average) * inverse
    edge = jnp.zeros((EDGE, width), jnp.float32)
    left = joined_ref[:, :width]
    sigma = sigmoid(joined_ref[:, width:])
    for ref, value in (
        (pad_ref, left * sigma),
        (dpad_ref, inverse * (dshift_ref[...] * bgain - sums[1:2, :] - centered * sums[0:1, :])),
    ):
        ref[:EDGE, :] = edge
        ref[EDGE + length :, :] = edge
        ref[EDGE : EDGE + length, :] = value
    dtap_ref[...] = jnp.zeros_like(dtap_ref)

    def chunk(index, carry):
        at = pl.ds(pl.multiple_of(index * CHUNK, CHUNK), CHUNK)
        around = pl.ds(pl.multiple_of(index * CHUNK, CHUNK), CHUNK + 2 * EDGE)
        window = pad_ref[around, :]
        dwindow = dpad_ref[around, :]
        masks = mask_ref[at, :]
        middle = dwindow[EDGE : EDGE + CHUNK]
        total = jnp.zeros((CHUNK, width), jnp.float32)
        for k in range(KERNEL):
            mask = masks[:, k : k + 1]
            back = KERNEL - 1 - k
            total = total + dwindow[k + 1 : k + 1 + CHUNK] * mask * taps_ref[back : back + 1, :]
            term = window[k + 1 : k + 1 + CHUNK] * mask * middle
            dtap_ref[8 * k : 8 * k + 8, :] += jnp.sum(term.reshape(CHUNK // 8, 8, width), 0)
        dglu_ref[at, :] = total
        return carry

    lax.fori_loop(0, length // CHUNK, chunk, 0)
    for k in range(KERNEL):
        dtaps_ref[k : k + 1, :] = jnp.sum(dtap_ref[8 * k : 8 * k + 8, :], 0, keepdims=True)
    dglu = dglu_ref[...]
    low = jnp.concatenate(
        [
            (dglu * sigma).astype(jnp.bfloat16),
            (dglu * left * sigma * (1.0 - sigma)).astype(jnp.bfloat16),
        ],
        1,
    )
    dgated_ref[...] = mul(normed_ref[...], low, TN)
    slope = mul(low, gated_ref[...], NT)
    unit, spread = norm_parts(resid_ref[...])
    dgain_ref[...] = jnp.sum(slope * unit, 0, keepdims=True)
    dbias_ref[...] = jnp.sum(slope, 0, keepdims=True)
    out_ref[...] = slope_ref[...] + norm_slope(unit, spread, slope, gain_ref[...])


def conv_back(
    frames, slope, dshift, depth, stats, sums, bgain, joined, normed, resid, gain, gated_in, taps, masks
):
    length, width = resid.shape
    full = jnp.float32
    shape = jax.ShapeDtypeStruct
    padded = pltpu.VMEM((length + 2 * EDGE, width), full)
    return pl.pallas_call(
        functools.partial(conv_back_kernel, frames),
        out_shape=[
            shape((length, width), full),
            shape((width, 2 * width), full),
            shape((KERNEL, width), full),
            shape((1, width), full),
            shape((1, width), full),
        ],
        scratch_shapes=[
            padded,
            padded,
            pltpu.VMEM((8 * KERNEL, width), full),
            pltpu.VMEM((length, width), full),
        ],
        compiler_params=pltpu.CompilerParams(vmem_limit_bytes=60 * 1024 * 1024),
        cost_estimate=pl.CostEstimate(flops=6 * 10**9, bytes_accessed=20 * 10**6, transcendentals=10**6),
        name="conv_back",
    )(slope, dshift, depth, stats, sums, bgain, joined, normed, resid, gain, gated_in, taps, masks)


def gather_rows(value):
    return lax.all_gather(value, AXES, axis=0, tiled=True)


def scatter_small(value):
    return scatter_blocks(value.reshape((lax.axis_size(AXES), -1) + value.shape[1:]), False)


def gathered_count(devices):
    return devices if sizes() == FAST else 1


def scatter_second(value, devices, width):
    if value.shape[0] == 1:
        up = by_devices(value[:, :, :width])
        down = value[0, :, width:].reshape(EXPERTS, width, -1, width).transpose(0, 2, 1, 3)
        down = by_devices(down.reshape(1, EXPERTS, -1, width))
        return [wide(lax.psum_scatter(part, AXES, scatter_dimension=0)) for part in (up, down)]
    total = wide(lax.psum_scatter(value, AXES, scatter_dimension=0, tiled=False))
    owned = width // devices
    down = total[:, owned:].reshape(EXPERTS, owned, -1, width).transpose(0, 2, 1, 3)
    return [total[:, :owned], down.reshape(EXPERTS, -1, width)]


def router_columns(router):
    count = router.shape[0] // 2
    return router.reshape(2, count, EXPERTS).transpose(1, 0, 2).reshape(count, 2 * EXPERTS)


def router_rows(packed, devices):
    count = packed.shape[0] // devices
    return (
        packed.reshape(devices, count, 2, EXPERTS).transpose(0, 2, 1, 3).reshape(-1, EXPERTS)
    )


def on_device(
    inputs,
    embedding,
    segments,
    routes_first,
    routes_second,
    cotangent,
    first_gain,
    first_bias,
    first_router,
    first_up,
    first_down,
    attend_gain,
    attend_bias,
    project_in,
    relative_weight,
    content_bias,
    position_bias,
    attend_out,
    depth_gain,
    depth_bias,
    gated_in,
    depth_kernel,
    batch_gain,
    batch_bias,
    point_out,
    second_gain,
    second_bias,
    second_router,
    second_up,
    second_down,
    final_gain,
    final_bias,
):
    segment = segments[0]
    devices = lax.axis_size(AXES)
    length, width = inputs.shape
    frames = length * devices
    vectors = jnp.stack(
        [
            first_gain,
            first_bias,
            second_gain,
            second_bias,
            attend_gain,
            attend_bias,
            content_bias,
            position_bias,
            depth_gain,
            depth_bias,
            batch_gain,
            batch_bias,
            final_gain,
            final_bias,
        ],
        1,
    )
    n_vec = vectors.shape[1]
    small = jnp.concatenate(
        [
            vectors,
            depth_kernel.T,
            router_columns(first_router),
            router_columns(second_router),
        ],
        1,
    )
    n_small = small.shape[1]
    small = jnp.pad(small, ((0, 0), (0, 128 - n_small)))
    first_ups = Weights(gather_experts(first_up, True))
    first_downs = Weights(gather_experts(first_down, False))
    small = gather_small(small).reshape(width, 128)[:, :n_small]
    packed = gather_rows(
        jnp.concatenate([project_in, relative_weight, attend_out, gated_in, point_out], 1)
    )
    rows = small[:, : n_vec + KERNEL].T
    col = n_vec + KERNEL
    first_router_full = router_rows(small[:, col : col + 2 * EXPERTS], devices)
    second_router_full = router_rows(small[:, col + 2 * EXPERTS : col + 4 * EXPERTS], devices)
    at = 0
    project_full = packed[:, at : at + 3 * width]
    at = at + 3 * width
    relative_full = packed[:, at : at + width]
    at = at + width
    attend_out_full = packed[:, at : at + width]
    at = at + width
    gated_full = packed[:, at : at + 2 * width]
    at = at + 2 * width
    point_full = packed[:, at : at + width]
    relative_full = relative_full.reshape(width // 2, 2, width).transpose(1, 0, 2).reshape(width, width)
    floats = rows.astype(jnp.float32)

    def vec(index):
        return floats[index : index + 1]

    def router_wide(router):
        return jnp.pad(router, ((0, 0), (0, 128 - EXPERTS)))

    first_router_full = router_wide(first_router_full)
    second_router_full = router_wide(second_router_full)
    taps = floats[n_vec : n_vec + KERNEL]
    masks = tap_masks(segments)
    first_places = places(routes_first)
    second_places = places(routes_second)
    second_ups = Weights(gather_whole(second_up))
    second_downs = Weights(gather_whole(second_down))
    attend_full = (
        vec(4),
        vec(5),
        project_full,
        relative_full,
        vec(6),
        vec(7),
        attend_out_full,
    )
    cosine, sine = angles(length, width)
    tables = (jnp.concatenate([cosine, sine], 1).astype(jnp.bfloat16), cosine, sine)

    first_normed, first_probs = expert_enter(inputs, embedding, first_router_full, vec(0), vec(1))
    counts, pos_row, pos_col = first_places
    first_picked, first_inner = first_up_call(counts, pos_row, first_normed, first_ups)
    first_resid, first_branch = first_down_call(
        counts, pos_col, first_inner, inputs, first_probs, routes_first, first_downs
    )
    attend_kept = attention_forward(first_resid, segments, attend_full, tables)
    attend_resid, conv_normed, joined, depth, stats = conv_front(
        first_resid, attend_kept[6], attend_out_full, vec(8), vec(9), gated_full, taps, masks
    )
    stats = total_of(stats)
    conv_resid, second_normed, second_probs = conv_tail(
        frames, depth, stats, vec(10), vec(11), point_full, attend_resid,
        embedding, second_router_full, vec(2), vec(3),
    )
    (
        second_picked,
        second_inner,
        second_branch,
        result,
        slope,
        final_gain_grad,
        final_bias_grad,
    ) = second_forward_call(
        *second_places, second_normed, conv_resid, second_probs, routes_second,
        cotangent, vec(12), vec(13), second_ups, second_downs,
    )
    slope, dgain_second, dbias_second, drouter_second, dpicked, dinner = second_back_call(
        *second_places, slope, second_probs, routes_second, second_branch, second_inner,
        second_router_full, conv_resid, second_normed, embedding, vec(2), second_ups, second_downs,
    )
    dshift, dpoint, sums = conv_turn(frames, slope, depth, stats, vec(10), vec(11), point_full)
    sums, dpicked = lax.optimization_barrier((sums, dpicked))
    second_large = scatter_second(
        second_grads_call(
            second_places[0], second_picked, second_inner, dpicked, dinner, gathered_count(devices)
        ),
        devices,
        width,
    )
    sums = total_of(sums)
    slope, dgated, dtaps, dgain_depth, dbias_depth = conv_back(
        frames, slope, dshift, depth, stats, sums, vec(10), joined, conv_normed,
        attend_resid, vec(8), gated_full, taps, masks,
    )
    slope, dao, dpq, dpk, dpv, drel, dcb, dpb, dgain_attend, dbias_attend = attention_backward(
        first_resid, slope, attend_full, tables, attend_kept
    )
    drel = drel.reshape(2, width // 2, width).transpose(1, 0, 2).reshape(width, width)
    matrices = scatter_small(
        jnp.concatenate([dpq, dpk, dpv, drel, dao, dgated, dpoint], 1).astype(jnp.bfloat16)
    )
    first_ddown, dpicked, dlogits = first_back_call(
        counts, pos_row, slope, first_probs, routes_first, first_branch, first_inner, first_downs
    )
    first_down_grad = scatter_blocks(by_devices(first_ddown), True)
    first_dup, dinner = first_middle_call(
        counts, dpicked, first_picked, first_inner, first_ups, first_downs
    )
    first_up_grad = scatter_blocks(by_devices(first_dup), False)
    slope, dgain_first, dbias_first, drouter_first = first_leave_call(
        counts, pos_col, dinner, dlogits, first_router_full, slope, inputs, first_normed, embedding,
        vec(0), first_ups,
    )

    def columns_of(grad):
        return (
            grad[:EXPERTS]
            .reshape(EXPERTS, devices, 2, -1)
            .transpose(1, 3, 2, 0)
            .reshape(width, 2 * EXPERTS)
        )

    small_grad = scatter_small(
        jnp.concatenate(
            [
                jnp.concatenate(
                    [
                        dgain_first,
                        dbias_first,
                        dgain_second,
                        dbias_second,
                        dgain_attend,
                        dbias_attend,
                        dcb,
                        dpb,
                        dgain_depth,
                        dbias_depth,
                        final_gain_grad,
                        final_bias_grad,
                        dtaps,
                    ],
                    0,
                ).T,
                columns_of(drouter_first),
                columns_of(drouter_second),
            ],
            1,
        )
    )
    own = small_grad.shape[0]
    start = own * lax.axis_index(AXES)
    own_sums = lax.dynamic_slice_in_dim(sums, start, own, 1)

    def vector(index):
        return small_grad[:, index]

    def router_of(start):
        block = small_grad[:, start : start + 2 * EXPERTS]
        return block.reshape(own, 2, EXPERTS).transpose(1, 0, 2).reshape(2 * own, EXPERTS)

    return (
        result,
        slope,
        vector(0),
        vector(1),
        router_of(12 + KERNEL),
        first_up_grad,
        first_down_grad,
        vector(4),
        vector(5),
        matrices[:, : 3 * width],
        matrices[:, 3 * width : 4 * width],
        vector(6),
        vector(7),
        matrices[:, 4 * width : 5 * width],
        vector(8),
        vector(9),
        matrices[:, 5 * width : 7 * width],
        small_grad[:, 12 : 12 + KERNEL].T,
        own_sums[0],
        own_sums[1],
        matrices[:, 7 * width :],
        vector(2),
        vector(3),
        router_of(12 + KERNEL + 2 * EXPERTS),
        second_large[0],
        second_large[1],
        vector(10),
        vector(11),
    )


def solution(mesh):
    placed = (
        P(("dp", "fsdp"), None),
        P(("dp", "fsdp"), None),
        P(("dp", "fsdp"), None),
        P(("dp", "fsdp"), None),
        P(("dp", "fsdp"), None),
        P(("dp", "fsdp"), None),
        P(("dp", "fsdp")),
        P(("dp", "fsdp")),
        P(("dp", "fsdp"), None),
        P(None, ("dp", "fsdp"), None),
        P(None, ("dp", "fsdp"), None),
        P(("dp", "fsdp")),
        P(("dp", "fsdp")),
        P(("dp", "fsdp"), None),
        P(("dp", "fsdp"), None),
        P(("dp", "fsdp")),
        P(("dp", "fsdp")),
        P(("dp", "fsdp"), None),
        P(("dp", "fsdp")),
        P(("dp", "fsdp")),
        P(("dp", "fsdp"), None),
        P(None, ("dp", "fsdp")),
        P(("dp", "fsdp")),
        P(("dp", "fsdp")),
        P(("dp", "fsdp"), None),
        P(("dp", "fsdp")),
        P(("dp", "fsdp")),
        P(("dp", "fsdp"), None),
        P(None, ("dp", "fsdp"), None),
        P(None, ("dp", "fsdp"), None),
        P(("dp", "fsdp")),
        P(("dp", "fsdp")),
    )
    return jax.shard_map(
        on_device,
        mesh=mesh,
        in_specs=placed,
        out_specs=(
            P(("dp", "fsdp"), None),
            P(("dp", "fsdp"), None),
            P(("dp", "fsdp")),
            P(("dp", "fsdp")),
            P(("dp", "fsdp"), None),
            P(None, ("dp", "fsdp"), None),
            P(None, ("dp", "fsdp"), None),
            P(("dp", "fsdp")),
            P(("dp", "fsdp")),
            P(("dp", "fsdp"), None),
            P(("dp", "fsdp"), None),
            P(("dp", "fsdp")),
            P(("dp", "fsdp")),
            P(("dp", "fsdp"), None),
            P(("dp", "fsdp")),
            P(("dp", "fsdp")),
            P(("dp", "fsdp"), None),
            P(None, ("dp", "fsdp")),
            P(("dp", "fsdp")),
            P(("dp", "fsdp")),
            P(("dp", "fsdp"), None),
            P(("dp", "fsdp")),
            P(("dp", "fsdp")),
            P(("dp", "fsdp"), None),
            P(None, ("dp", "fsdp"), None),
            P(None, ("dp", "fsdp"), None),
            P(("dp", "fsdp")),
            P(("dp", "fsdp")),
        ),
        check_vma=False,
    )
```

```python
import functools

import jax
import jax.numpy as jnp
from jax import lax
from jax.experimental import pallas as pl
from jax.experimental.pallas import tpu as pltpu
from jax.sharding import PartitionSpec as P

HEADS = 8
EXPERTS = 4
KERNEL = 15
HEAD_DIM = 64
CAPACITY = 512
AXES = ("dp", "fsdp")

eps = 1e-05
blocked = -1000000000.0


def product(left, right):
    return jnp.dot(left, right, preferred_element_type=jnp.float32)


NN = (((1,), (0,)), ((), ()))
NT = (((1,), (1,)), ((), ()))
TN = (((0,), (0,)), ((), ()))


def mul(left, right, dims=NN):
    return lax.dot_general(left, right, dims, preferred_element_type=jnp.float32)


def norm_parts(value):
    average = jnp.mean(value, -1, keepdims=True)
    centered = value - average
    spread = jnp.mean(centered * centered, -1, keepdims=True)
    inverse = lax.rsqrt(spread + eps)
    return centered * inverse, inverse


def norm_slope(unit, inverse, slope, gain):
    scaled = slope * gain
    first = jnp.mean(scaled, -1, keepdims=True)
    second = jnp.mean(scaled * unit, -1, keepdims=True)
    return (scaled - first - unit * second) * inverse


def head_mask(rows, head):
    lane = lax.broadcasted_iota(jnp.int32, (rows, 2 * HEAD_DIM), 1)
    return (lane >= head * HEAD_DIM) & (lane < (head + 1) * HEAD_DIM)


def angles(length, width):
    freqs = jnp.exp(jnp.arange(0, width, 2).astype(jnp.float32) * (-jnp.log(10000.0) / width))
    coarse = (jnp.arange(length // 32) * 32).astype(jnp.float32)[:, None] * freqs[None, :]
    fine = jnp.arange(32).astype(jnp.float32)[:, None] * freqs[None, :]
    cos_a, sin_a = jnp.cos(coarse)[:, None], jnp.sin(coarse)[:, None]
    cos_b, sin_b = jnp.cos(fine)[None], jnp.sin(fine)[None]
    cosine = (cos_a * cos_b - sin_a * sin_b).reshape(length, width // 2)
    sine = (sin_a * cos_b + cos_a * sin_b).reshape(length, width // 2)
    return cosine, sine


def halves_matrix(width):
    row = lax.broadcasted_iota(jnp.int32, (width, width), 0)
    column = lax.broadcasted_iota(jnp.int32, (width, width), 1)
    half = width // 2
    source = jnp.where(row < half, 2 * row, 2 * (row - half) + 1)
    return (column == source).astype(jnp.float32).astype(jnp.bfloat16)


def attend_forward_kernel(
    resid_ref,
    gain_ref,
    bias_ref,
    pq_ref,
    pk_ref,
    pv_ref,
    rel_ref,
    cb_ref,
    pb_ref,
    segr_ref,
    segc_ref,
    tab_ref,
    cos_ref,
    sin_ref,
    ha_ref,
    qu_ref,
    qv_ref,
    k_ref,
    v_ref,
    p_ref,
    ctx_ref,
    kt_ref,
    sort_ref,
):
    length = resid_ref.shape[0]
    half = cos_ref.shape[1]
    pair = 2 * HEAD_DIM
    rows = 256

    @pl.when(pl.program_id(0) == 0)
    def first():
        unit, inverse = norm_parts(resid_ref[...])
        ha_ref[...] = (unit * gain_ref[...] + bias_ref[...]).astype(jnp.bfloat16)
        kt_ref[:, pair:] = tab_ref[...]
        sort_ref[...] = halves_matrix(rel_ref.shape[0])

    relative = mul(sort_ref[...], rel_ref[...]).astype(jnp.bfloat16)
    normed = ha_ref[...]
    query = mul(normed, pq_ref[...])
    keys = mul(normed, pk_ref[...]).astype(jnp.bfloat16)
    k_ref[...] = keys
    kt_ref[:, :pair] = keys
    v_ref[...] = mul(normed, pv_ref[...]).astype(jnp.bfloat16)
    qu_ref[...] = (query + cb_ref[...]).astype(jnp.bfloat16)
    qv_ref[...] = (query + pb_ref[...]).astype(jnp.bfloat16)

    def block(index, carry):
        at = pl.ds(pl.multiple_of(index * rows, rows), rows)
        same = segc_ref[at, :] == segr_ref[...]
        cosine, sine = cos_ref[at, :], sin_ref[at, :]
        contexts = []
        for head in range(2):
            own = head_mask(rows, head)
            part_u = jnp.where(own, qu_ref[at, :], 0) * 0.125
            part_v = jnp.where(own, qv_ref[at, :], 0)
            coef = mul(part_v, relative, NT) * 0.125
            left, right = coef[:, :half], coef[:, half:]
            turned_a = (left * sine + right * cosine).astype(jnp.bfloat16)
            turned_b = (right * sine - left * cosine).astype(jnp.bfloat16)
            scores = mul(
                jnp.concatenate([part_u.astype(jnp.bfloat16), turned_a, turned_b], 1), kt_ref[...], NT
            )
            scores = jnp.where(same, scores, blocked)
            peak = jnp.max(scores, -1, keepdims=True)
            raised = jnp.exp(scores - peak)
            summed = jnp.sum(raised, -1, keepdims=True)
            chances = (raised * (1.0 / summed)).astype(jnp.bfloat16)
            p_ref[head, at, :] = chances
            contexts.append(mul(chances, v_ref[...]))
        ctx_ref[at, :] = jnp.where(head_mask(rows, 0), contexts[0], contexts[1]).astype(jnp.bfloat16)
        return carry

    lax.fori_loop(0, length // rows, block, 0)


def attend_backward_kernel(resumed, ends, *refs):
    operands = 18
    if not resumed:
        refs = refs[:operands] + (None,) + refs[operands:]
    attend_backward_body(ends, *refs)


def attend_backward_body(
    ends,
    p_ref,
    tab_ref,
    cos_ref,
    sin_ref,
    resid_ref,
    slope_ref,
    ha_ref,
    qu_ref,
    qv_ref,
    k_ref,
    v_ref,
    ctx_ref,
    ao_ref,
    pq_ref,
    pk_ref,
    pv_ref,
    rel_ref,
    gain_ref,
    begin_ref,
    g1_ref,
    dao_ref,
    dpq_ref,
    dpk_ref,
    dpv_ref,
    drel_ref,
    vec_ref,
    kt_ref,
    dout_ref,
    dctx_ref,
    dn_ref,
    dq_ref,
    dkt_ref,
    dvt_ref,
    drt_ref,
    sort_ref,
):
    length = resid_ref.shape[0]
    half = cos_ref.shape[1]
    pair = 2 * HEAD_DIM
    rows = 256
    step = pl.program_id(0)
    lanes = pl.ds(pl.multiple_of(step * pair, pair), pair)

    @pl.when(step == 0)
    def first():
        dout_ref[...] = slope_ref[...].astype(jnp.bfloat16)
        kt_ref[:, pair:] = tab_ref[...]
        dn_ref[...] = jnp.zeros_like(dn_ref) if begin_ref is None else begin_ref[...]
        vec_ref[...] = jnp.zeros_like(vec_ref)
        sort_ref[...] = halves_matrix(rel_ref.shape[0])

    kt_ref[:, :pair] = k_ref[...]
    relative = mul(sort_ref[...], rel_ref[...]).astype(jnp.bfloat16)
    dao_ref[...] = mul(ctx_ref[...], dout_ref[...], TN).astype(jnp.bfloat16)
    dctx_ref[...] = mul(dout_ref[...], ao_ref[...], NT).astype(jnp.bfloat16)
    dkt_ref[...] = jnp.zeros_like(dkt_ref)
    dvt_ref[...] = jnp.zeros_like(dvt_ref)
    drt_ref[...] = jnp.zeros_like(drt_ref)

    def block(index, carry):
        at = pl.ds(pl.multiple_of(index * rows, rows), rows)
        cosine, sine = cos_ref[at, :], sin_ref[at, :]
        total = jnp.zeros((rows, pair), jnp.float32)
        sum_u = jnp.zeros((1, pair), jnp.float32)
        sum_v = jnp.zeros((1, pair), jnp.float32)
        for head in range(2):
            own = head_mask(rows, head)
            part = jnp.where(own, dctx_ref[at, :], 0)
            low = p_ref[head, at, :]
            chances = low.astype(jnp.float32)
            raw = mul(part, v_ref[...], NT)
            weighted = chances * raw
            delta = jnp.sum(weighted, -1, keepdims=True)
            slope = ((weighted - chances * delta) * 0.125).astype(jnp.bfloat16)
            dvt_ref[...] += mul(part, low, TN)
            dkt_ref[...] += mul(jnp.where(own, qu_ref[at, :], 0), slope, TN)
            wide = mul(slope, kt_ref[...])
            slope_u = jnp.where(own, wide[:, :pair], 0.0)
            first, second = wide[:, pair : pair + half], wide[:, pair + half :]
            coef = jnp.concatenate(
                [
                    (first * sine - second * cosine).astype(jnp.bfloat16),
                    (first * cosine + second * sine).astype(jnp.bfloat16),
                ],
                1,
            )
            slope_v = jnp.where(own, mul(coef, relative), 0.0)
            drt_ref[...] += mul(jnp.where(own, qv_ref[at, :], 0), coef, TN)
            total = total + slope_u + slope_v
            sum_u = sum_u + jnp.sum(slope_u, 0, keepdims=True)
            sum_v = sum_v + jnp.sum(slope_v, 0, keepdims=True)
        dq_ref[at, :] = total
        vec_ref[0:1, lanes] += sum_u
        vec_ref[1:2, lanes] += sum_v
        return carry

    lax.fori_loop(0, length // rows, block, 0)
    low_q = dq_ref[...].astype(jnp.bfloat16)
    low_k = dkt_ref[...].T.astype(jnp.bfloat16)
    low_v = dvt_ref[...].T.astype(jnp.bfloat16)
    drel = drt_ref[...].T.astype(jnp.bfloat16)
    drel_ref[...] = mul(sort_ref[...], drel, TN).astype(jnp.bfloat16)
    normed = ha_ref[...]
    dpq_ref[...] = mul(normed, low_q, TN).astype(jnp.bfloat16)
    dpk_ref[...] = mul(normed, low_k, TN).astype(jnp.bfloat16)
    dpv_ref[...] = mul(normed, low_v, TN).astype(jnp.bfloat16)
    dn_ref[...] += (
        mul(low_q, pq_ref[...], NT) + mul(low_k, pk_ref[...], NT) + mul(low_v, pv_ref[...], NT)
    )

    @pl.when(step == pl.num_programs(0) - 1)
    def last():
        slope = dn_ref[...]
        if not ends:
            g1_ref[...] = slope
            return
        unit, inverse = norm_parts(resid_ref[...])
        vec_ref[2:3, :] = jnp.sum(slope * unit, 0, keepdims=True)
        vec_ref[3:4, :] = jnp.sum(slope, 0, keepdims=True)
        g1_ref[...] = slope_ref[...] + norm_slope(unit, inverse, slope, gain_ref[...])


def whole(shape):
    return pl.BlockSpec(shape, lambda p: (0,) * len(shape))


def columns(rows, width, shift=0):
    return pl.BlockSpec((rows, width), lambda p: (0, p + shift))


def attention_forward(first, count, resid, segments, segment_column, weights, tables):
    gain, bias, packed, content_bias, position_bias = weights
    table, cosine, sine = tables
    length, width = resid.shape
    pair = 2 * HEAD_DIM
    pairs = HEADS // 2
    low = jnp.bfloat16
    shape = jax.ShapeDtypeStruct
    return pl.pallas_call(
        attend_forward_kernel,
        grid=(count,),
        in_specs=[
            whole((length, width)),
            pl.BlockSpec((None, 1, width), lambda p: (gain[1], 0, 0)),
            pl.BlockSpec((None, 1, width), lambda p: (bias[1], 0, 0)),
            columns(width, pair, first),
            columns(width, pair, first + pairs),
            columns(width, pair, first + 2 * pairs),
            columns(width, pair, first + 3 * pairs),
            pl.BlockSpec((None, 1, pair), lambda p: (content_bias[1], 0, p + first)),
            pl.BlockSpec((None, 1, pair), lambda p: (position_bias[1], 0, p + first)),
            whole((1, length)),
            whole((length, 1)),
            whole((length, width)),
            whole((length, width // 2)),
            whole((length, width // 2)),
        ],
        out_specs=[whole((length, width))]
        + [columns(length, pair)] * 4
        + [pl.BlockSpec((2, length, length), lambda p: (p, 0, 0)), columns(length, pair)],
        out_shape=[shape((length, width), low)]
        + [shape((length, count * pair), low)] * 4
        + [shape((2 * count, length, length), low), shape((length, count * pair), low)],
        scratch_shapes=[pltpu.VMEM((length, pair + width), low), pltpu.VMEM((width, width), low)],
        compiler_params=pltpu.CompilerParams(vmem_limit_bytes=56 * 1024 * 1024),
        cost_estimate=pl.CostEstimate(flops=count * 6 * 10**9, bytes_accessed=count * 8 * 10**6, transcendentals=count * 2 * 10**6),
        name="attend_forward",
    )(
        resid,
        gain[0],
        bias[0],
        packed,
        packed,
        packed,
        packed,
        content_bias[0],
        position_bias[0],
        segments,
        segment_column,
        table,
        cosine,
        sine,
    )


def attention_backward(first, count, last, resid, slope, weights, tables, kept, partial):
    gain, bias, packed, content_bias, position_bias = weights
    table, cosine, sine = tables
    normed, query_u, query_v, keys, values, chances, context = kept
    length, width = resid.shape
    pair = 2 * HEAD_DIM
    pairs = HEADS // 2
    low, full = jnp.bfloat16, jnp.float32
    shape = jax.ShapeDtypeStruct
    begin = [] if partial is None else [partial]
    return pl.pallas_call(
        functools.partial(attend_backward_kernel, bool(begin), last),
        grid=(count,),
        in_specs=[
            pl.BlockSpec((2, length, length), lambda p: (p + first, 0, 0)),
            whole((length, width)),
            whole((length, width // 2)),
            whole((length, width // 2)),
            whole((length, width)),
            whole((length, width)),
            whole((length, width)),
        ]
        + [columns(length, pair, first)] * 5
        + [
            pl.BlockSpec((pair, width), lambda p: (p + first, pairs)),
            columns(width, pair, first),
            columns(width, pair, first + pairs),
            columns(width, pair, first + 2 * pairs),
            columns(width, pair, first + 3 * pairs),
            pl.BlockSpec((None, 1, width), lambda p: (gain[1], 0, 0)),
        ]
        + [whole((length, width))] * len(begin),
        out_specs=[
            whole((length, width)),
            pl.BlockSpec((pair, width), lambda p: (p, 0)),
            columns(width, pair),
            columns(width, pair),
            columns(width, pair),
            columns(width, pair),
            whole((8, width)),
        ],
        out_shape=[shape((length, width), full), shape((count * pair, width), low)]
        + [shape((width, count * pair), low)] * 4
        + [shape((8, width), full)],
        scratch_shapes=[
            pltpu.VMEM((length, pair + width), low),
            pltpu.VMEM((length, width), low),
            pltpu.VMEM((length, pair), low),
            pltpu.VMEM((length, width), full),
            pltpu.VMEM((length, pair), full),
            pltpu.VMEM((pair, length), full),
            pltpu.VMEM((pair, length), full),
            pltpu.VMEM((pair, width), full),
            pltpu.VMEM((width, width), low),
        ],
        compiler_params=pltpu.CompilerParams(vmem_limit_bytes=60 * 1024 * 1024),
        cost_estimate=pl.CostEstimate(
            flops=count * 10**10, bytes_accessed=20 * 10**6, transcendentals=0
        ),
        name="attend_backward",
    )(
        chances,
        table,
        cosine,
        sine,
        resid,
        slope,
        normed,
        query_u,
        query_v,
        keys,
        values,
        context,
        packed,
        packed,
        packed,
        packed,
        packed,
        gain[0],
        *begin,
    )


FAST = {"z": 4, "y": 2, "x": 2, "c": 2}


def grid_of(count_dp, count_fsdp):
    depth = 4 if count_dp % 4 == 0 else count_dp
    cores = 2 if count_fsdp % 2 == 0 else 1
    return {"z": depth, "y": count_dp // depth, "x": count_fsdp // cores, "c": cores}


def sizes():
    return grid_of(lax.axis_size("dp"), lax.axis_size("fsdp"))


def place(grid, axis):
    index = lax.axis_index(AXES)
    for name in ("c", "x", "y", "z"):
        if name == axis:
            return index % grid[name]
        index = index // grid[name]


def number(grid, at):
    return ((at["z"] * grid["y"] + at["y"]) * grid["x"] + at["x"]) * grid["c"] + at["c"]


def move(value, grid, **steps):
    pairs = []
    for z in range(grid["z"]):
        for y in range(grid["y"]):
            for x in range(grid["x"]):
                for c in range(grid["c"]):
                    at = {"z": z, "y": y, "x": x, "c": c}
                    to = {name: (at[name] + steps.get(name, 0)) % grid[name] for name in at}
                    pairs.append((number(grid, at), number(grid, to)))
    return lax.ppermute(value, AXES, pairs)


PLANE = ((0, 1), (1, 0), (1, 1))


def tie(*values):
    return lax.optimization_barrier(values)


def total_of(value, beside=None):
    grid = sizes()
    if grid != FAST:
        done = beside(value) if beside else None
        return lax.psum(value, AXES), done
    value = value + move(value, grid, c=1)
    moved = [move(value, grid, y=dy, x=dx) for dy, dx in PLANE]
    done = None
    if beside:
        done = beside(value)
        *moved, done = tie(*moved, done)
    value = value + sum(moved)
    return value + sum(move(value, grid, z=step) for step in range(1, grid["z"])), done


class Chain:
    def __init__(self, steps, grid):
        self.steps, self.grid, self.value = steps, grid, None
        self.start(next(steps))

    def start(self, sends):
        self.pending = [move(value, self.grid, **how) for value, how in sends]

    def step(self, *held):
        count = len(self.pending)
        tied = tie(*self.pending, *held)
        arrived, held = tied[:count], tied[count:]
        try:
            sends = self.steps.send(list(arrived))
        except StopIteration as stop:
            self.value, self.pending = stop.value, []
            return held
        count = len(sends)
        tied = tie(*[value for value, _ in sends], *held)
        self.start([(value, how) for value, (_, how) in zip(tied[:count], sends, strict=True)])
        return tied[count:]

    def finish(self):
        while self.pending:
            try:
                self.start(self.steps.send(self.pending))
            except StopIteration as stop:
                self.value, self.pending = stop.value, []
        return self.value


class Still:
    def __init__(self, value):
        self.value, self.pending = value, []

    def step(self, *held):
        return held

    def finish(self):
        return self.value


def advance(chains, *held):
    pending = [value for chain in chains for value in chain.pending]
    tied = list(tie(*pending, *held))
    held = tied[len(pending) :]
    sends = []
    for chain in chains:
        arrived = [tied.pop(0) for _ in chain.pending]
        chain.pending = []
        if not arrived:
            sends.append([])
            continue
        try:
            sends.append(chain.steps.send(arrived))
        except StopIteration as stop:
            chain.value = stop.value
            sends.append([])
    values = [value for part in sends for value, _ in part]
    if not values:
        return held
    tied = list(tie(*values, *held))
    held = tied[len(values) :]
    for chain, part in zip(chains, sends, strict=True):
        chain.pending = [move(tied.pop(0), chain.grid, **how) for _, how in part]
    return held


def gather_steps(value, depth_first):
    value = value[None]
    plane = [{"y": dy, "x": dx} for dy, dx in PLANE]
    if depth_first:
        column = [value] + (yield [(value, {"z": step}) for step in range(1, 4)])
        value = jnp.concatenate(column, 0)
        pieces = [value] + (yield [(value, how) for how in plane])
    else:
        chips = [value] + (yield [(value, how) for how in plane])
        value = jnp.concatenate(chips, 0)
        pieces = [value]
        for _ in range(3):
            (value,) = yield [(value, {"z": 1})]
            pieces.append(value)
    return pieces + (yield [(piece, {"c": 1}) for piece in pieces])


def gathered_from(grid, depth_first):
    own = {axis: place(grid, axis) for axis in grid}
    column = [{"z": -step} for step in range(4)]
    plane = [{}] + [{"y": dy, "x": dx} for dy, dx in PLANE]
    found = []
    for core in range(2):
        for outer in plane if depth_first else column:
            for inner in column if depth_first else plane:
                at = {"c": core, **outer, **inner}
                found.append(
                    number(grid, {axis: (own[axis] + at.get(axis, 0)) % grid[axis] for axis in grid})
                )
    return jnp.stack(found)


def gather_experts(value, depth_first):
    grid = sizes()
    if grid == FAST:
        return Chain(gather_steps(value, depth_first), grid), gathered_from(grid, depth_first)
    pieces, ids = gather_whole(value)
    return Still(pieces), ids


def gather_whole(value):
    grid = sizes()
    if grid == FAST:
        blocks = lax.all_gather(value, AXES, axis=0, tiled=False)
        return [blocks], jnp.arange(blocks.shape[0], dtype=jnp.int32)
    blocks = lax.all_gather(value, AXES, axis=1, tiled=True)
    return [blocks[None]], jnp.zeros((1,), jnp.int32)


def block_at(value, index, at):
    return lax.dynamic_index_in_dim(value, index % value.shape[at], at, keepdims=False)


def wide(value):
    return value.astype(jnp.float32)


def scatter_steps(keep, send, depth_first, grid):
    shape = (4, 2, 2) + keep.shape[1:]
    low = jnp.bfloat16
    z, y, x = (place(grid, axis) for axis in "zyx")
    (other,) = yield [(send, {"c": 1})]
    keep, other = keep.reshape(shape), other.reshape(shape)

    def near(value, at, dy, dx):
        return wide(block_at(block_at(value, y + dy, at), x + dx, at))

    def below(value, step):
        return wide(block_at(value, z + 4 - step, 0))

    if depth_first:
        part = (below(keep, 1) + below(other, 1)).astype(low)
        for step in (2, 3, 0):
            (part,) = yield [(part, {"z": 1})]
            part = (wide(part) + below(keep, step) + below(other, step)).astype(low)
        moved = yield [(near(part, 0, dy, dx).astype(low), {"y": dy, "x": dx}) for dy, dx in PLANE]
        return near(part, 0, 0, 0) + sum(wide(value) for value in moved)
    sends = [
        ((near(keep, 1, dy, dx) + near(other, 1, dy, dx)).astype(low), {"y": dy, "x": dx})
        for dy, dx in PLANE
    ]
    moved = yield sends
    column = near(keep, 1, 0, 0) + near(other, 1, 0, 0) + sum(wide(value) for value in moved)
    column = column.astype(low)
    moved = yield [(block_at(column, z + step, 0), {"z": step}) for step in range(1, 4)]
    return wide(block_at(column, z, 0)) + sum(wide(value) for value in moved)


def scatter_parts(parts, depth_first):
    grid = sizes()
    if len(parts) == 2:
        return Chain(scatter_steps(*parts, depth_first, grid), grid)
    return Still(wide(scatter_rows(by_devices(parts[0]))))


def scatter_rows(value):
    return lax.psum_scatter(value, AXES, scatter_dimension=0, tiled=False)


def halves(value):
    grid = sizes()
    if grid != FAST:
        return [value]
    value = value.reshape((16, 2) + value.shape[1:])
    core = place(grid, "c")
    return [block_at(value, core, 1), block_at(value, core + 1, 1)]


def by_devices(value):
    if value.ndim < 4:
        return value
    devices = lax.axis_size(AXES)
    return value.reshape((EXPERTS, devices, -1, value.shape[3])).transpose(1, 0, 2, 3)


def single(kernel, name, inputs, outputs, scratch, flops, size):
    values, specs = [], []
    for item in inputs:
        if not isinstance(item, tuple):
            value, block, index = item, item.shape, (0,) * item.ndim
        elif len(item) == 2:
            value, block, index = item[0], (None,) + item[0].shape[1:], (item[1], 0, 0)
        else:
            value, block, index = item
        values.append(value)
        specs.append(pl.BlockSpec(block, functools.partial(lambda index, step: index, index)))
    return pl.pallas_call(
        kernel,
        grid=(1,),
        in_specs=specs,
        out_specs=[pl.BlockSpec(o.shape, lambda step: (0, 0)) for o in outputs],
        out_shape=outputs,
        scratch_shapes=scratch,
        compiler_params=pltpu.CompilerParams(vmem_limit_bytes=60 * 1024 * 1024),
        cost_estimate=pl.CostEstimate(flops=flops, bytes_accessed=size, transcendentals=10**6),
        name=name,
    )(*values)


CHUNK = 64
EDGE = 8


def tap_masks(segments):
    half = KERNEL // 2
    segment = segments[0]
    length = segment.shape[0]
    padded = jnp.pad(segment, (half, half), constant_values=-1)
    same = [padded[k : k + length] == segment for k in range(KERNEL)]
    masks = jnp.stack(same, 1).astype(jnp.float32)
    return jnp.pad(masks, ((0, 0), (0, 128 - KERNEL)))


def conv_front_kernel(
    resid_ref, ctx_ref, ao_ref, gain_ref, bias_ref, gated_ref, taps_ref, mask_ref,
    out_ref, normed_ref, joined_ref, depth_ref, sums_ref,
    pad_ref,
):
    length, width = resid_ref.shape
    resid = resid_ref[...] + mul(ctx_ref[...], ao_ref[...])
    out_ref[...] = resid
    unit, inverse = norm_parts(resid)
    normed = (unit * gain_ref[...] + bias_ref[...]).astype(jnp.bfloat16)
    normed_ref[...] = normed
    joined = mul(normed, gated_ref[...])
    joined_ref[...] = joined
    pad_ref[:EDGE, :] = jnp.zeros((EDGE, width), jnp.float32)
    pad_ref[EDGE + length :, :] = jnp.zeros((EDGE, width), jnp.float32)
    pad_ref[EDGE : EDGE + length, :] = joined[:, :width] * sigmoid(joined[:, width:])
    sums_ref[...] = jnp.zeros_like(sums_ref)

    def chunk(index, carry):
        at = pl.ds(pl.multiple_of(index * CHUNK, CHUNK), CHUNK)
        window = pad_ref[pl.ds(pl.multiple_of(index * CHUNK, CHUNK), CHUNK + 2 * EDGE), :]
        masks = mask_ref[at, :]
        total = jnp.zeros((CHUNK, width), jnp.float32)
        for k in range(KERNEL):
            total = total + window[k + 1 : k + 1 + CHUNK] * masks[:, k : k + 1] * taps_ref[k : k + 1, :]
        depth_ref[at, :] = total
        sums_ref[0:1, :] += jnp.sum(total, 0, keepdims=True)
        sums_ref[1:2, :] += jnp.sum(total * total, 0, keepdims=True)
        return carry

    lax.fori_loop(0, length // CHUNK, chunk, 0)


def conv_front(resid, context, attend_out, gain, bias, gated_in, taps, masks):
    length, width = resid.shape
    low, full = jnp.bfloat16, jnp.float32
    shape = jax.ShapeDtypeStruct
    return single(
        conv_front_kernel,
        "conv_front",
        [resid, context, attend_out, gain, bias, gated_in, taps, masks],
        [
            shape((length, width), full),
            shape((length, width), low),
            shape((length, 2 * width), full),
            shape((length, width), full),
            shape((2, width), full),
        ],
        [pltpu.VMEM((length + 2 * EDGE, width), full)],
        4 * 10**9,
        16 * 10**6,
    )


def batch_stats(stats, frames):
    average = stats[0:1, :] * (1.0 / frames)
    spread = stats[1:2, :] * (1.0 / frames) - average * average
    return average, lax.rsqrt(spread + eps)


def conv_tail_kernel(
    frames, depth_ref, stats_ref, bgain_ref, bbias_ref, point_ref, resid_ref,
    embed_ref, router_ref, gain_ref, bias_ref,
    out_ref, normed_ref, probs_ref,
):
    average, inverse = batch_stats(stats_ref[...], frames)
    shifted = (depth_ref[...] - average) * inverse * bgain_ref[...] + bbias_ref[...]
    tail = (shifted * sigmoid(shifted)).astype(jnp.bfloat16)
    resid = resid_ref[...] + mul(tail, point_ref[...])
    out_ref[...] = resid
    unit, spread = norm_parts(resid)
    normed = (unit * gain_ref[...] + bias_ref[...]).astype(jnp.bfloat16)
    normed_ref[...] = normed
    probs_ref[...] = route_probs(normed, embed_ref[...], router_ref)


def conv_tail(frames, depth, stats, bgain, bbias, point_out, resid, embedding, router, gain, bias):
    length, width = resid.shape
    shape = jax.ShapeDtypeStruct
    return single(
        functools.partial(conv_tail_kernel, frames),
        "conv_tail",
        [depth, stats, bgain, bbias, point_out, resid, embedding, router, gain, bias],
        [
            shape((length, width), jnp.float32),
            shape((length, width), jnp.bfloat16),
            shape((length, 128), jnp.float32),
        ],
        [],
        10**9,
        8 * 10**6,
    )


def conv_turn_kernel(
    frames, slope_ref, depth_ref, stats_ref, bgain_ref, bbias_ref, point_ref,
    dshift_ref, dpoint_ref, sums_ref,
):
    average, inverse = batch_stats(stats_ref[...], frames)
    centered = (depth_ref[...] - average) * inverse
    shifted = centered * bgain_ref[...] + bbias_ref[...]
    sigma = sigmoid(shifted)
    low = slope_ref[...].astype(jnp.bfloat16)
    dpoint_ref[...] = mul((shifted * sigma).astype(jnp.bfloat16), low, TN).astype(jnp.bfloat16)
    dshift = mul(low, point_ref[...], NT) * (sigma * (1.0 + shifted * (1.0 - sigma)))
    dshift_ref[...] = dshift
    sums_ref[0:1, :] = jnp.sum(dshift * centered, 0, keepdims=True)
    sums_ref[1:2, :] = jnp.sum(dshift, 0, keepdims=True)


def conv_turn(frames, slope, depth, stats, bgain, bbias, point_out):
    length, width = slope.shape
    shape = jax.ShapeDtypeStruct
    return single(
        functools.partial(conv_turn_kernel, frames),
        "conv_turn",
        [slope, depth, stats, bgain, bbias, point_out],
        [
            shape((length, width), jnp.float32),
            shape((width, width), jnp.bfloat16),
            shape((2, width), jnp.float32),
        ],
        [],
        10**9,
        8 * 10**6,
    )


def conv_back_kernel(
    frames, slope_ref, dshift_ref, depth_ref, stats_ref, sums_ref, bgain_ref, joined_ref, normed_ref,
    resid_ref, gain_ref, gated_ref, taps_ref, mask_ref,
    out_ref, dgated_ref, dtaps_ref, dgain_ref, dbias_ref,
    pad_ref, dpad_ref, dtap_ref, dglu_ref,
):
    length, width = resid_ref.shape
    average, inverse = batch_stats(stats_ref[...], frames)
    bgain = bgain_ref[...]
    sums = sums_ref[...] * (1.0 / frames) * bgain
    centered = (depth_ref[...] - average) * inverse
    edge = jnp.zeros((EDGE, width), jnp.float32)
    left = joined_ref[:, :width]
    sigma = sigmoid(joined_ref[:, width:])
    for ref, value in (
        (pad_ref, left * sigma),
        (dpad_ref, inverse * (dshift_ref[...] * bgain - sums[1:2, :] - centered * sums[0:1, :])),
    ):
        ref[:EDGE, :] = edge
        ref[EDGE + length :, :] = edge
        ref[EDGE : EDGE + length, :] = value
    dtap_ref[...] = jnp.zeros_like(dtap_ref)

    def chunk(index, carry):
        at = pl.ds(pl.multiple_of(index * CHUNK, CHUNK), CHUNK)
        around = pl.ds(pl.multiple_of(index * CHUNK, CHUNK), CHUNK + 2 * EDGE)
        window = pad_ref[around, :]
        dwindow = dpad_ref[around, :]
        masks = mask_ref[at, :]
        middle = dwindow[EDGE : EDGE + CHUNK]
        total = jnp.zeros((CHUNK, width), jnp.float32)
        for k in range(KERNEL):
            mask = masks[:, k : k + 1]
            back = KERNEL - 1 - k
            total = total + dwindow[k + 1 : k + 1 + CHUNK] * mask * taps_ref[back : back + 1, :]
            term = window[k + 1 : k + 1 + CHUNK] * mask * middle
            dtap_ref[8 * k : 8 * k + 8, :] += jnp.sum(term.reshape(CHUNK // 8, 8, width), 0)
        dglu_ref[at, :] = total
        return carry

    lax.fori_loop(0, length // CHUNK, chunk, 0)
    for k in range(KERNEL):
        dtaps_ref[k : k + 1, :] = jnp.sum(dtap_ref[8 * k : 8 * k + 8, :], 0, keepdims=True)
    dglu = dglu_ref[...]
    low = jnp.concatenate(
        [
            (dglu * sigma).astype(jnp.bfloat16),
            (dglu * left * sigma * (1.0 - sigma)).astype(jnp.bfloat16),
        ],
        1,
    )
    dgated_ref[...] = mul(normed_ref[...], low, TN).astype(jnp.bfloat16)
    slope = mul(low, gated_ref[...], NT)
    unit, spread = norm_parts(resid_ref[...])
    dgain_ref[...] = jnp.sum(slope * unit, 0, keepdims=True)
    dbias_ref[...] = jnp.sum(slope, 0, keepdims=True)
    out_ref[...] = slope_ref[...] + norm_slope(unit, spread, slope, gain_ref[...])


def conv_back(
    frames, slope, dshift, depth, stats, sums, bgain, joined, normed, resid, gain, gated_in, taps, masks
):
    length, width = resid.shape
    full = jnp.float32
    shape = jax.ShapeDtypeStruct
    padded = pltpu.VMEM((length + 2 * EDGE, width), full)
    return single(
        functools.partial(conv_back_kernel, frames),
        "conv_back",
        [slope, dshift, depth, stats, sums, bgain, joined, normed, resid, gain, gated_in, taps, masks],
        [
            shape((length, width), full),
            shape((width, 2 * width), jnp.bfloat16),
            shape((KERNEL, width), full),
            shape((1, width), full),
            shape((1, width), full),
        ],
        [
            padded,
            padded,
            pltpu.VMEM((8 * KERNEL, width), full),
            pltpu.VMEM((length, width), full),
        ],
        6 * 10**9,
        20 * 10**6,
    )


ROWS = (256, 384, 512)


def one_hot_rows(pos_row, base, rows):
    slot = lax.broadcasted_iota(jnp.int32, (rows, pos_row.shape[1]), 0) + base
    return (slot == pos_row).astype(jnp.float32).astype(jnp.bfloat16)


def one_hot_columns(pos_col, base, rows):
    slot = lax.broadcasted_iota(jnp.int32, (pos_col.shape[0], rows), 1) + base
    return (slot == pos_col).astype(jnp.float32).astype(jnp.bfloat16)


def routed(route_col):
    lane = lax.broadcasted_iota(jnp.int32, (route_col.shape[0], 128), 1)
    return (lane == route_col).astype(jnp.float32)


def sigmoid(value):
    return 1.0 / (1.0 + jnp.exp(-value))


def split_mul(wide, narrow, dims):
    high = wide.astype(jnp.bfloat16)
    rest = (wide - high.astype(jnp.float32)).astype(jnp.bfloat16)
    return mul(high, narrow, dims) + mul(rest, narrow, dims)


def route_probs(normed, embed, router_ref):
    width = normed.shape[1]
    logits = mul(normed, router_ref[:width, :]) + mul(embed, router_ref[width:, :])
    lane = lax.broadcasted_iota(jnp.int32, logits.shape, 1)
    logits = jnp.where(lane < EXPERTS, logits, -jnp.inf)
    raised = jnp.exp(logits - jnp.max(logits, -1, keepdims=True))
    return raised / jnp.sum(raised, -1, keepdims=True)


def sized(count, body):
    lower = -1
    for rows in ROWS:
        pl.when((count > lower) & (count <= rows))(functools.partial(body, rows))
        lower = rows


def assemble(refs, ids_ref, whole_ref):
    at = 0
    for ref in refs:
        rows = ref.shape[2]
        for block in range(ref.shape[0]):
            start = pl.multiple_of(ids_ref[at] * rows, rows)
            whole_ref[pl.ds(start, rows), :] = ref[block, 0]
            at += 1


class Weights:
    def __init__(self, pieces, ids):
        self.arrays, self.ids = pieces, ids
        rows = sum(piece.shape[0] * piece.shape[2] for piece in self.arrays)
        self.shape = (rows, self.arrays[0].shape[3])
        self.rows = self.arrays[0].shape[2]

    def specs(self):
        return [by_owner(piece.shape) for piece in self.arrays]


def fixed(shape):
    return pl.BlockSpec(shape, lambda e, *_: (0,) * len(shape))


def by_expert(shape):
    return pl.BlockSpec((1,) + shape, lambda e, *_: (e,) + (0,) * len(shape))


def by_owner(shape):
    return pl.BlockSpec((shape[0], 1) + shape[2:], lambda e, *_: (0, e, 0, 0))


def grads_outputs(weights):
    count = weights.shape[0] // weights.rows
    if count == 1:
        shapes = [(1, EXPERTS) + weights.shape]
    else:
        shapes = [(count // 2, EXPERTS, weights.rows, weights.shape[1])] * 2
    return [(struct(shape, jnp.bfloat16), by_owner(shape)) for shape in shapes]


def expert_call(kernel, name, counts, weights, inputs, outputs, scratch, flops, with_core=False):
    scalars = [counts] + [weight.ids for weight in weights]
    arrays = [piece for weight in weights for piece in weight.arrays]
    n_in, n_out = len(inputs), len(outputs)

    def body(*refs):
        count_ref, *ids = refs[: len(scalars)]
        refs = refs[len(scalars) :]
        pieces, refs = refs[: len(arrays)], refs[len(arrays) :]
        operands, results, rest = refs[:n_in], refs[n_in : n_in + n_out], refs[n_in + n_out :]
        expert = pl.program_id(0)
        for at, weight in enumerate(weights):
            own = pieces[: len(weight.arrays)]
            pieces = pieces[len(weight.arrays) :]
            assemble(own, ids[at], rest[at])
        kernel(
            expert, count_ref[expert], *rest[: len(weights)], *operands, *results, *rest[len(weights) :],
            **({"core": count_ref[EXPERTS]} if with_core else {}),
        )

    return pl.pallas_call(
        body,
        grid_spec=pltpu.PrefetchScalarGridSpec(
            num_scalar_prefetch=len(scalars),
            grid=(EXPERTS,),
            in_specs=[spec for weight in weights for spec in weight.specs()]
            + [spec for _, spec in inputs],
            out_specs=[spec for _, spec in outputs],
            scratch_shapes=[pltpu.VMEM(weight.shape, jnp.bfloat16) for weight in weights] + scratch,
        ),
        out_shape=[shape for shape, _ in outputs],
        compiler_params=pltpu.CompilerParams(vmem_limit_bytes=60 * 1024 * 1024),
        cost_estimate=pl.CostEstimate(
            flops=flops, bytes_accessed=20 * 10**6, transcendentals=4 * 10**6
        ),
        name=name,
    )(*scalars, *arrays, *[value for value, _ in inputs])


def struct(shape, dtype=jnp.float32):
    return jax.ShapeDtypeStruct(shape, dtype)


def whole_in(value):
    if isinstance(value, tuple):
        return row_in(*value)
    return (value, fixed(value.shape))


def row_in(vectors, index):
    return (vectors, pl.BlockSpec((None, 1, vectors.shape[2]), lambda e, *_: (index, 0, 0)))


def whole_out(shape, dtype=jnp.float32):
    return (struct(shape, dtype), fixed(shape))


def expert_in(value):
    return (value, by_expert(value.shape[1:]))


def expert_out(shape, dtype=jnp.bfloat16):
    return (struct((EXPERTS,) + shape, dtype), by_expert(shape))


def spans(hidden):
    chunk = 512
    return [slice(start, start + chunk) for start in range(0, hidden, chunk)]


def up_part(expert, rows, up_ref, normed_ref, posr_ref, picked_ref, inner_ref, then=None):
    hot = one_hot_rows(posr_ref[...], expert * CAPACITY, rows)
    picked = mul(hot, normed_ref[...]).astype(jnp.bfloat16)
    picked_ref[0, :rows, :] = picked
    total = None
    for span in spans(up_ref.shape[1]):
        inner = mul(picked, up_ref[:, span])
        inner_ref[0, :rows, span] = inner.astype(jnp.bfloat16)
        if then is not None:
            part = then(inner, span)
            total = part if total is None else total + part
    return total


def first_up_kernel(expert, count, up_ref, normed_ref, posr_ref, picked_ref, inner_ref):
    def run(rows):
        up_part(expert, rows, up_ref, normed_ref, posr_ref, picked_ref, inner_ref)

    sized(count, run)


def first_up_call(counts, pos_row, normed, up):
    length, width = normed.shape
    return expert_call(
        first_up_kernel,
        "first_up",
        counts,
        [up],
        [whole_in(normed), whole_in(pos_row)],
        [expert_out((CAPACITY, width)), expert_out((CAPACITY, up.shape[1]))],
        [],
        5 * 10**9,
    )


def first_down_kernel(
    expert, count, down_ref, inner_ref, posc_ref, resid_ref, probs_ref, route_ref, out_ref, branch_ref
):
    @pl.when(expert == 0)
    def clear():
        branch_ref[...] = jnp.zeros_like(branch_ref)

    def run(rows):
        total = None
        for span in spans(down_ref.shape[0]):
            inner = inner_ref[0, :rows, span].astype(jnp.float32)
            part = mul((inner * sigmoid(inner)).astype(jnp.bfloat16), down_ref[span, :])
            total = part if total is None else total + part
        hot = one_hot_columns(posc_ref[...], expert * CAPACITY, rows)
        branch_ref[...] += mul(hot, total.astype(jnp.bfloat16))

    sized(count, run)

    @pl.when(expert == EXPERTS - 1)
    def last():
        gate = jnp.sum(probs_ref[...] * routed(route_ref[...]), -1, keepdims=True)
        out_ref[...] = resid_ref[...].astype(jnp.float32) + 0.5 * gate * branch_ref[...]


def first_down_call(counts, pos_col, inner, resid, probs, routes, down):
    shape = resid.shape
    return expert_call(
        first_down_kernel,
        "first_down",
        counts,
        [down],
        [expert_in(inner)] + [whole_in(v) for v in (pos_col, resid, probs, routes)],
        [whole_out(shape), whole_out(shape)],
        [],
        5 * 10**9,
    )


def second_forward_kernel(
    expert, count, up_ref, down_ref,
    normed_ref, posr_ref, posc_ref, resid_ref, probs_ref, route_ref, cot_ref, gain_ref, bias_ref,
    picked_ref, inner_ref, branch_ref, result_ref, g4_ref, dgain_ref, dbias_ref,
):
    @pl.when(expert == 0)
    def clear():
        branch_ref[...] = jnp.zeros_like(branch_ref)

    def run(rows):
        def then(inner, span):
            return mul((inner * sigmoid(inner)).astype(jnp.bfloat16), down_ref[span, :])

        total = up_part(expert, rows, up_ref, normed_ref, posr_ref, picked_ref, inner_ref, then)
        hot = one_hot_columns(posc_ref[...], expert * CAPACITY, rows)
        branch_ref[...] += mul(hot, total.astype(jnp.bfloat16))

    sized(count, run)

    @pl.when(expert == EXPERTS - 1)
    def last():
        gate = jnp.sum(probs_ref[...] * routed(route_ref[...]), -1, keepdims=True)
        unit, inverse = norm_parts(resid_ref[...] + 0.5 * gate * branch_ref[...])
        gain = gain_ref[...]
        cot = cot_ref[...].astype(jnp.float32)
        result_ref[...] = (unit * gain + bias_ref[...]).astype(jnp.bfloat16)
        dgain_ref[...] = jnp.sum(cot * unit, 0, keepdims=True)
        dbias_ref[...] = jnp.sum(cot, 0, keepdims=True)
        g4_ref[...] = norm_slope(unit, inverse, cot, gain)


def second_forward_call(counts, pos_row, pos_col, normed, resid, probs, routes, cot, gain, bias, up, down):
    length, width = normed.shape
    return expert_call(
        second_forward_kernel,
        "second_forward",
        counts,
        [up, down],
        [whole_in(v) for v in (normed, pos_row, pos_col, resid, probs, routes, cot, gain, bias)],
        [
            expert_out((CAPACITY, width)),
            expert_out((CAPACITY, up.shape[1])),
            whole_out((length, width)),
            whole_out((length, width), jnp.bfloat16),
            whole_out((length, width)),
            whole_out((1, width)),
            whole_out((1, width)),
        ],
        [],
        10 * 10**9,
    )


def enter_slope(slope_ref, probs_ref, route_ref, branch_ref, low_ref, dlogits_ref):
    chosen = routed(route_ref[...])
    probs = probs_ref[...]
    gate = jnp.sum(probs * chosen, -1, keepdims=True)
    slope = slope_ref[...]
    low_ref[...] = (0.5 * gate * slope).astype(jnp.bfloat16)
    dgate = 0.5 * jnp.sum(slope * branch_ref[...], -1, keepdims=True)
    dlogits_ref[...] = probs * (chosen - gate) * dgate


def leave_slope(
    dnorm, dlogits, slope_ref, resid_ref, normed_ref, embed_ref, gain_ref,
    out_ref, dgain_ref, dbias_ref, drouter_ref,
):
    width = resid_ref.shape[1]
    unit, inverse = norm_parts(resid_ref[...].astype(jnp.float32))
    dgain_ref[...] = jnp.sum(dnorm * unit, 0, keepdims=True)
    dbias_ref[...] = jnp.sum(dnorm, 0, keepdims=True)
    out_ref[...] = slope_ref[...] + norm_slope(unit, inverse, dnorm, gain_ref[...])
    drouter_ref[:, :width] = split_mul(dlogits, normed_ref[...], TN)
    drouter_ref[:, width:] = split_mul(dlogits, embed_ref[...], TN)


def active_of(inner):
    inner = inner.astype(jnp.float32)
    return (inner * sigmoid(inner)).astype(jnp.bfloat16)


def slope_of(inner):
    inner = inner.astype(jnp.float32)
    sigma = sigmoid(inner)
    return sigma * (1.0 + inner * (1.0 - sigma))


def store_rows(refs, core, first, span, value):
    rows = value.shape[0]
    if len(refs) == 1:
        refs[0][0, 0, first : first + rows, span] = value
        return
    owned = refs[0].shape[2]
    value = value.reshape((rows // owned // 2, 2, 1, owned, value.shape[1]))
    at = slice(first // owned // 2, (first + rows) // owned // 2)
    for own in range(2):

        @pl.when(core == own)
        def store():
            refs[0][at, :, :, span] = value[:, own]
            refs[1][at, :, :, span] = value[:, 1 - own]


def down_grads(rows, core, inner_ref, dpicked, ddown_refs):
    for span in spans(inner_ref.shape[2]):
        grads = mul(active_of(inner_ref[0, :rows, span]), dpicked, TN)
        store_rows(ddown_refs, core, span.start, slice(None), grads.astype(jnp.bfloat16))


def up_grads(core, picked, dinner, span, dup_refs):
    store_rows(dup_refs, core, 0, span, mul(picked, dinner, TN).astype(jnp.bfloat16))


def first_back_kernel(
    expert, count, slope_ref, probs_ref, route_ref, branch_ref, posr_ref, inner_ref, *rest, core
):
    *ddown_refs, dpicked_ref, dlogits_ref, low_ref = rest

    @pl.when(expert == 0)
    def first():
        enter_slope(slope_ref, probs_ref, route_ref, branch_ref, low_ref, dlogits_ref)

    def run(rows):
        hot = one_hot_rows(posr_ref[...], expert * CAPACITY, rows)
        dpicked = mul(hot, low_ref[...]).astype(jnp.bfloat16)
        dpicked_ref[0, :rows, :] = dpicked
        down_grads(rows, core, inner_ref, dpicked, ddown_refs)

    sized(count, run)


def first_back_call(counts, pos_row, slope, probs, routes, branch, inner, down):
    length, width = slope.shape
    return expert_call(
        first_back_kernel,
        "first_down_grads",
        counts,
        [],
        [whole_in(v) for v in (slope, probs, routes, branch, pos_row)] + [expert_in(inner)],
        grads_outputs(down) + [expert_out((CAPACITY, width)), whole_out((length, 128))],
        [pltpu.VMEM((length, width), jnp.bfloat16)],
        5 * 10**9,
        True,
    )


def first_middle_kernel(expert, count, down_ref, dpicked_ref, picked_ref, inner_ref, *rest, core):
    *dup_refs, dinner_ref = rest

    def run(rows):
        dpicked = dpicked_ref[0, :rows, :]
        picked = picked_ref[0, :rows, :]
        for span in spans(inner_ref.shape[2]):
            dactive = mul(dpicked, down_ref[span, :], NT)
            dinner = (dactive * slope_of(inner_ref[0, :rows, span])).astype(jnp.bfloat16)
            dinner_ref[0, :rows, span] = dinner
            up_grads(core, picked, dinner, span, dup_refs)

    sized(count, run)


def first_middle_call(counts, dpicked, picked, inner, up, down):
    return expert_call(
        first_middle_kernel,
        "first_up_grads",
        counts,
        [down],
        [expert_in(v) for v in (dpicked, picked, inner)],
        grads_outputs(up) + [expert_out(inner.shape[1:])],
        [],
        9 * 10**9,
        True,
    )


def first_leave_kernel(
    expert, count, up_ref, dinner_ref, posc_ref, dlogits_ref, router_ref, slope_ref, resid_ref, normed_ref,
    embed_ref, gain_ref,
    out_ref, dgain_ref, dbias_ref, drouter_ref,
    dnorm_ref,
):
    width = up_ref.shape[0]

    @pl.when(expert == 0)
    def first():
        dnorm_ref[...] = split_mul(dlogits_ref[...], router_ref[:width, :], NT)

    def run(rows):
        total = mul(dinner_ref[0, :rows, :], up_ref[...], NT).astype(jnp.bfloat16)
        dnorm_ref[...] += mul(one_hot_columns(posc_ref[...], expert * CAPACITY, rows), total)

    sized(count, run)

    @pl.when(expert == EXPERTS - 1)
    def last():
        leave_slope(
            dnorm_ref[...], dlogits_ref[...], slope_ref, resid_ref, normed_ref, embed_ref, gain_ref,
            out_ref, dgain_ref, dbias_ref, drouter_ref,
        )


def first_leave_call(counts, pos_col, dinner, dlogits, router, slope, resid, normed, embedding, gain, up):
    length, width = slope.shape
    return expert_call(
        first_leave_kernel,
        "first_leave",
        counts,
        [up],
        [expert_in(dinner)]
        + [whole_in(v) for v in (pos_col, dlogits, router, slope, resid, normed, embedding, gain)],
        [
            whole_out((length, width)),
            whole_out((1, width)),
            whole_out((1, width)),
            whole_out((128, 2 * width)),
        ],
        [pltpu.VMEM((length, width), jnp.float32)],
        5 * 10**9,
    )


def second_back_kernel(
    expert, count, up_ref, down_ref, slope_ref, probs_ref, route_ref, branch_ref, posr_ref, posc_ref, inner_ref,
    router_ref, resid_ref, normed_ref, embed_ref, gain_ref,
    out_ref, dgain_ref, dbias_ref, drouter_ref, dpicked_ref, dinner_ref,
    low_ref, dlogits_ref, dnorm_ref,
):
    width = up_ref.shape[0]

    @pl.when(expert == 0)
    def first():
        enter_slope(slope_ref, probs_ref, route_ref, branch_ref, low_ref, dlogits_ref)
        dnorm_ref[...] = split_mul(dlogits_ref[...], router_ref[:width, :], NT)

    def run(rows):
        hot = one_hot_rows(posr_ref[...], expert * CAPACITY, rows)
        dpicked = mul(hot, low_ref[...]).astype(jnp.bfloat16)
        dpicked_ref[0, :rows, :] = dpicked
        total = None
        for span in spans(up_ref.shape[1]):
            dactive = mul(dpicked, down_ref[span, :], NT)
            dinner = (dactive * slope_of(inner_ref[0, :rows, span])).astype(jnp.bfloat16)
            dinner_ref[0, :rows, span] = dinner
            part = mul(dinner, up_ref[:, span], NT)
            total = part if total is None else total + part
        hot = one_hot_columns(posc_ref[...], expert * CAPACITY, rows)
        dnorm_ref[...] += mul(hot, total.astype(jnp.bfloat16))

    sized(count, run)

    @pl.when(expert == EXPERTS - 1)
    def last():
        leave_slope(
            dnorm_ref[...], dlogits_ref[...], slope_ref, resid_ref, normed_ref, embed_ref, gain_ref,
            out_ref, dgain_ref, dbias_ref, drouter_ref,
        )


def second_back_call(
    counts, pos_row, pos_col, slope, probs, routes, branch, inner, router, resid, normed, embedding, gain, up, down
):
    length, width = slope.shape
    return expert_call(
        second_back_kernel,
        "second_back",
        counts,
        [up, down],
        [whole_in(v) for v in (slope, probs, routes, branch, pos_row, pos_col)]
        + [expert_in(inner)]
        + [whole_in(v) for v in (router, resid, normed, embedding, gain)],
        [
            whole_out((length, width)),
            whole_out((1, width)),
            whole_out((1, width)),
            whole_out((128, 2 * width)),
            expert_out((CAPACITY, width)),
            expert_out(inner.shape[1:]),
        ],
        [
            pltpu.VMEM((length, width), jnp.bfloat16),
            pltpu.VMEM((length, 128), jnp.float32),
            pltpu.VMEM((length, width), jnp.float32),
        ],
        10 * 10**9,
    )


def second_grads_kernel(expert, count, picked_ref, inner_ref, dpicked_ref, dinner_ref, out_ref):
    def run(rows):
        picked = picked_ref[0, :rows, :]
        dpicked = dpicked_ref[0, :rows, :]
        owned = out_ref.shape[2] // 2
        width = dpicked.shape[1]
        for span in spans(inner_ref.shape[2]):
            chunk = span.stop - span.start
            grads = mul(picked, dinner_ref[0, :rows, span], TN).astype(jnp.bfloat16)
            out_ref[:, :, :owned, span] = grads.reshape((-1, 1, owned, chunk))
            grads = mul(active_of(inner_ref[0, :rows, span]), dpicked, TN).astype(jnp.bfloat16)
            across = inner_ref.shape[2] // width
            if owned >= chunk:
                at = span.start // owned * width
                out_ref[0, 0, owned:, at : at + width] = grads
                continue
            first = span.start // (across * owned)
            count = chunk // (across * owned)
            grads = grads.reshape((count, 1, across, owned, width))
            for at in range(across):
                out_ref[first : first + count, :, owned:, at * width : (at + 1) * width] = grads[:, :, at]

    sized(count, run)


def second_grads_call(counts, picked, inner, dpicked, dinner, devices):
    hidden, width = inner.shape[2], picked.shape[2]
    shape = (devices, EXPERTS, 2 * width // devices, hidden)
    return expert_call(
        second_grads_kernel,
        "second_grads",
        counts,
        [],
        [expert_in(v) for v in (picked, inner, dpicked, dinner)],
        [(struct(shape, jnp.bfloat16), by_owner(shape))],
        [],
        10 * 10**9,
    )[0]


def enter_kernel(resid_ref, embed_ref, router_ref, gain_ref, bias_ref, normed_ref, probs_ref):
    unit, inverse = norm_parts(resid_ref[...].astype(jnp.float32))
    normed = (unit * gain_ref[...] + bias_ref[...]).astype(jnp.bfloat16)
    normed_ref[...] = normed
    probs_ref[...] = route_probs(normed, embed_ref[...], router_ref)


def expert_enter(resid, embedding, router, gain, bias):
    length, width = resid.shape
    return single(
        enter_kernel,
        "expert_enter",
        [resid, embedding, router, gain, bias],
        [struct((length, width), jnp.bfloat16), struct((length, 128))],
        [],
        10**9,
        4 * 10**6,
    )


def places(routes, core):
    length = routes.shape[0]
    chosen = (routes == jnp.arange(EXPERTS, dtype=jnp.int32)[None, :]).astype(jnp.float32)
    row = lax.broadcasted_iota(jnp.int32, (length, length), 0)
    before = (lax.broadcasted_iota(jnp.int32, (length, length), 1) < row).astype(jnp.bfloat16)
    earlier = product(before, chosen.astype(jnp.bfloat16))
    slot = jnp.sum(earlier * chosen, 1).astype(jnp.int32) + routes[:, 0] * CAPACITY
    counts = jnp.concatenate([jnp.sum(chosen, 0).astype(jnp.int32), core])
    return counts, slot[None, :], slot[:, None]


def gather_rows(value):
    return lax.all_gather(value, AXES, axis=0, tiled=True)


def gathered_count(devices):
    return devices if sizes() == FAST else 1


def scatter_second(value, devices, width):
    if value.shape[0] == 1:
        up = by_devices(value[:, :, :width])
        down = value[0, :, width:].reshape(EXPERTS, width, -1, width).transpose(0, 2, 1, 3)
        down = by_devices(down.reshape(1, EXPERTS, -1, width))
        return [wide(scatter_rows(part)) for part in (up, down)]
    total = wide(scatter_rows(value))
    owned = width // devices
    down = total[:, owned:].reshape(EXPERTS, owned, -1, width).transpose(0, 2, 1, 3)
    return [total[:, :owned], down.reshape(EXPERTS, -1, width)]


def on_device(
    inputs,
    embedding,
    segments,
    routes_first,
    routes_second,
    cotangent,
    first_gain,
    first_bias,
    first_router,
    first_up,
    first_down,
    attend_gain,
    attend_bias,
    project_in,
    relative_weight,
    content_bias,
    position_bias,
    attend_out,
    depth_gain,
    depth_bias,
    gated_in,
    depth_kernel,
    batch_gain,
    batch_bias,
    point_out,
    second_gain,
    second_bias,
    second_router,
    second_up,
    second_down,
    final_gain,
    final_bias,
):
    devices = lax.axis_size(AXES)
    length, width = inputs.shape
    frames = length * devices
    core = jnp.reshape(place(sizes(), "c"), (1,))

    first_up_chain, up_ids = gather_experts(first_up, True)
    first_down_chain, down_ids = gather_experts(first_down, False)
    n_vec = 14
    taps_at = n_vec * first_gain.shape[0]
    routers_at = taps_at + depth_kernel.size
    n_router = first_router.size
    small = jnp.concatenate(
        [
            first_gain,
            first_bias,
            second_gain,
            second_bias,
            attend_gain,
            attend_bias,
            content_bias,
            position_bias,
            depth_gain,
            depth_bias,
            batch_gain,
            batch_bias,
            final_gain,
            final_bias,
            depth_kernel.reshape(-1),
            first_router.reshape(-1),
            second_router.reshape(-1),
        ]
    )
    own = project_in.shape[0]
    small = jnp.pad(small, (0, -small.size % (128 * own))).reshape(own, -1)
    packed = gather_rows(
        jnp.concatenate([project_in, relative_weight, attend_out, point_out, gated_in, small], 1)
    )
    small = packed[:, 8 * width :].reshape(devices, -1)
    second_ups = Weights(*gather_whole(second_up))
    second_downs = Weights(*gather_whole(second_down))

    first_places = places(routes_first, core)
    second_places = places(routes_second, core)
    masks = tap_masks(segments)
    segment_column = segments.reshape(length, 1)
    cosine, sine = angles(length, width)
    table = jnp.concatenate([cosine, sine], 1).astype(jnp.bfloat16)
    masks, table, cosine, sine = advance(
        [first_up_chain, first_down_chain], masks, table, cosine, sine
    )
    pos_row, pos_col = first_down_chain.step(first_places[1], first_places[2])
    tables = (table, cosine, sine)
    counts = first_places[0]

    floats = small[:, :taps_at].reshape(devices, n_vec, -1).transpose(1, 0, 2)
    floats = floats.reshape(n_vec, 1, width).astype(jnp.float32)
    taps = small[:, taps_at:routers_at].reshape(devices, KERNEL, -1).transpose(1, 0, 2)
    taps = taps.reshape(KERNEL, width).astype(jnp.float32)

    def router_wide(start):
        router = small[:, start : start + n_router].reshape(2 * width, EXPERTS)
        return jnp.pad(router, ((0, 0), (0, 128 - EXPERTS)))

    first_router_full = router_wide(routers_at)
    second_router_full = router_wide(routers_at + n_router)

    def vec(index):
        return (floats, index)

    first_normed, first_probs = expert_enter(inputs, embedding, first_router_full, vec(0), vec(1))
    first_normed, first_probs, floats, taps, second_router_full = first_up_chain.step(
        first_normed, first_probs, floats, taps, second_router_full
    )
    first_ups = Weights(first_up_chain.finish(), up_ids)

    attend_full = (vec(4), vec(5), packed, vec(6), vec(7))
    attend_out_full = (packed, (width, width), (0, 4))
    point_full = (packed, (width, width), (0, 5))
    gated_full = (packed, (width, 2 * width), (0, 3))

    first_picked, first_inner = first_up_call(counts, pos_row, first_normed, first_ups)
    first_downs = Weights(first_down_chain.finish(), down_ids)
    first_resid, first_branch = first_down_call(
        counts, pos_col, first_inner, inputs, first_probs, routes_first, first_downs
    )
    pairs = HEADS // 2
    kept = attention_forward(
        0, pairs, first_resid, segments, segment_column, attend_full, tables
    )
    attend_resid, conv_normed, joined, depth, stats = conv_front(
        first_resid, kept[6], attend_out_full, vec(8), vec(9), gated_full, taps, masks
    )
    stats, _ = total_of(stats)
    conv_resid, second_normed, second_probs = conv_tail(
        frames, depth, stats, vec(10), vec(11), point_full, attend_resid,
        embedding, second_router_full, vec(2), vec(3),
    )
    (
        second_picked,
        second_inner,
        second_branch,
        result,
        slope,
        final_gain_grad,
        final_bias_grad,
    ) = second_forward_call(
        *second_places, second_normed, conv_resid, second_probs, routes_second,
        cotangent, vec(12), vec(13), second_ups, second_downs,
    )
    slope, dgain_second, dbias_second, drouter_second, dpicked, dinner = second_back_call(
        *second_places, slope, second_probs, routes_second, second_branch, second_inner,
        second_router_full, conv_resid, second_normed, embedding, vec(2), second_ups, second_downs,
    )
    dshift, dpoint, sums = conv_turn(frames, slope, depth, stats, vec(10), vec(11), point_full)

    def deferred(sums):
        held, _ = tie(dpicked, sums)
        return second_grads_call(
            second_places[0], second_picked, second_inner, held, dinner, gathered_count(devices)
        )

    sums, second_large = total_of(sums, deferred)
    second_large = scatter_second(second_large, devices, width)
    slope, dgated, dtaps, dgain_depth, dbias_depth = conv_back(
        frames, slope, dshift, depth, stats, sums, vec(10), joined, conv_normed,
        attend_resid, vec(8), gated_full, taps, masks,
    )
    slope, dao, dpq, dpk, dpv, drel, attend_vec = attention_backward(
        0, pairs, True, first_resid, slope, attend_full, tables, kept, None
    )
    *first_ddown, first_dpicked, dlogits = first_back_call(
        counts, pos_row, slope, first_probs, routes_first, first_branch, first_inner, first_downs
    )
    first_ddown = scatter_parts(first_ddown, True)
    *first_dup, first_dinner = first_middle_call(
        counts, first_dpicked, first_picked, first_inner, first_ups, first_downs
    )
    first_dup = scatter_parts(first_dup, False)
    (first_dinner,) = first_ddown.step(first_dinner)
    slope, dgain_first, dbias_first, drouter_first = first_leave_call(
        counts, pos_col, first_dinner, dlogits, first_router_full, slope, inputs, first_normed, embedding,
        vec(0), first_ups,
    )
    (slope,) = advance([first_ddown], slope)
    (slope,) = advance([first_dup], slope)

    def columns_of(grad):
        return (
            grad[:EXPERTS]
            .reshape(EXPERTS, devices, 2, -1)
            .transpose(1, 3, 2, 0)
            .reshape(width, 2 * EXPERTS)
        )

    small_grad = jnp.concatenate(
        [
            jnp.concatenate(
                [
                    dgain_first,
                    dbias_first,
                    dgain_second,
                    dbias_second,
                    attend_vec[2:4],
                    attend_vec[0:2],
                    dgain_depth,
                    dbias_depth,
                    final_gain_grad,
                    final_bias_grad,
                    dtaps,
                ],
                0,
            ).T,
            columns_of(drouter_first),
            columns_of(drouter_second),
        ],
        1,
    )
    n_small = small_grad.shape[1]
    small_grad = jnp.pad(small_grad, ((0, 0), (0, -n_small % 128))).astype(jnp.bfloat16)
    matrices = jnp.concatenate([dpq, dpk, dpv, drel, dao, dgated, dpoint, small_grad], 1)
    matrices = matrices.reshape((devices, -1) + matrices.shape[1:])
    matrices = scatter_parts(halves(matrices), False)
    (slope,) = advance([first_ddown], slope)
    (slope,) = advance([first_dup, matrices], slope)
    (slope,) = advance([first_ddown, matrices], slope)
    first_up_grad = first_dup.finish()
    first_down_grad = first_ddown.finish()
    matrices = matrices.finish()
    small_grad = matrices[:, 8 * width : 8 * width + n_small]
    own = small_grad.shape[0]
    start = own * lax.axis_index(AXES)
    own_sums = lax.dynamic_slice_in_dim(sums, start, own, 1)

    def vector(index):
        return small_grad[:, index]

    def router_of(start):
        block = small_grad[:, start : start + 2 * EXPERTS]
        return block.reshape(own, 2, EXPERTS).transpose(1, 0, 2).reshape(2 * own, EXPERTS)

    return (
        result,
        slope,
        vector(0),
        vector(1),
        router_of(12 + KERNEL),
        first_up_grad,
        first_down_grad,
        vector(4),
        vector(5),
        matrices[:, : 3 * width],
        matrices[:, 3 * width : 4 * width],
        vector(6),
        vector(7),
        matrices[:, 4 * width : 5 * width],
        vector(8),
        vector(9),
        matrices[:, 5 * width : 7 * width],
        small_grad[:, 12 : 12 + KERNEL].T,
        own_sums[0],
        own_sums[1],
        matrices[:, 7 * width : 8 * width],
        vector(2),
        vector(3),
        router_of(12 + KERNEL + 2 * EXPERTS),
        second_large[0],
        second_large[1],
        vector(10),
        vector(11),
    )


def solution(mesh):
    placed = (
        P(("dp", "fsdp"), None),
        P(("dp", "fsdp"), None),
        P(("dp", "fsdp"), None),
        P(("dp", "fsdp"), None),
        P(("dp", "fsdp"), None),
        P(("dp", "fsdp"), None),
        P(("dp", "fsdp")),
        P(("dp", "fsdp")),
        P(("dp", "fsdp"), None),
        P(None, ("dp", "fsdp"), None),
        P(None, ("dp", "fsdp"), None),
        P(("dp", "fsdp")),
        P(("dp", "fsdp")),
        P(("dp", "fsdp"), None),
        P(("dp", "fsdp"), None),
        P(("dp", "fsdp")),
        P(("dp", "fsdp")),
        P(("dp", "fsdp"), None),
        P(("dp", "fsdp")),
        P(("dp", "fsdp")),
        P(("dp", "fsdp"), None),
        P(None, ("dp", "fsdp")),
        P(("dp", "fsdp")),
        P(("dp", "fsdp")),
        P(("dp", "fsdp"), None),
        P(("dp", "fsdp")),
        P(("dp", "fsdp")),
        P(("dp", "fsdp"), None),
        P(None, ("dp", "fsdp"), None),
        P(None, ("dp", "fsdp"), None),
        P(("dp", "fsdp")),
        P(("dp", "fsdp")),
    )
    return jax.shard_map(
        on_device,
        mesh=mesh,
        in_specs=placed,
        out_specs=(
            P(("dp", "fsdp"), None),
            P(("dp", "fsdp"), None),
            P(("dp", "fsdp")),
            P(("dp", "fsdp")),
            P(("dp", "fsdp"), None),
            P(None, ("dp", "fsdp"), None),
            P(None, ("dp", "fsdp"), None),
            P(("dp", "fsdp")),
            P(("dp", "fsdp")),
            P(("dp", "fsdp"), None),
            P(("dp", "fsdp"), None),
            P(("dp", "fsdp")),
            P(("dp", "fsdp")),
            P(("dp", "fsdp"), None),
            P(("dp", "fsdp")),
            P(("dp", "fsdp")),
            P(("dp", "fsdp"), None),
            P(None, ("dp", "fsdp")),
            P(("dp", "fsdp")),
            P(("dp", "fsdp")),
            P(("dp", "fsdp"), None),
            P(("dp", "fsdp")),
            P(("dp", "fsdp")),
            P(("dp", "fsdp"), None),
            P(None, ("dp", "fsdp"), None),
            P(None, ("dp", "fsdp"), None),
            P(("dp", "fsdp")),
            P(("dp", "fsdp")),
        ),
        check_vma=False,
    )
```

```python
import functools

import jax
import jax.numpy as jnp
from jax import lax
from jax.experimental import pallas as pl
from jax.experimental.pallas import tpu as pltpu
from jax.sharding import PartitionSpec as P

HEADS = 8
EXPERTS = 4
KERNEL = 15
HEAD_DIM = 64
CAPACITY = 512
AXES = ("dp", "fsdp")

eps = 1e-05
blocked = -1000000000.0


def product(left, right):
    return jnp.dot(left, right, preferred_element_type=jnp.float32)


NN = (((1,), (0,)), ((), ()))
NT = (((1,), (1,)), ((), ()))
TN = (((0,), (0,)), ((), ()))


def mul(left, right, dims=NN):
    return lax.dot_general(left, right, dims, preferred_element_type=jnp.float32)


def norm_parts(value):
    average = jnp.mean(value, -1, keepdims=True)
    centered = value - average
    spread = jnp.mean(centered * centered, -1, keepdims=True)
    inverse = lax.rsqrt(spread + eps)
    return centered * inverse, inverse


def norm_slope(unit, inverse, slope, gain):
    scaled = slope * gain
    first = jnp.mean(scaled, -1, keepdims=True)
    second = jnp.mean(scaled * unit, -1, keepdims=True)
    return (scaled - first - unit * second) * inverse


def head_mask(rows, head):
    lane = lax.broadcasted_iota(jnp.int32, (rows, 2 * HEAD_DIM), 1)
    return (lane >= head * HEAD_DIM) & (lane < (head + 1) * HEAD_DIM)


def angles(length, width):
    freqs = jnp.exp(jnp.arange(0, width, 2).astype(jnp.float32) * (-jnp.log(10000.0) / width))
    coarse = (jnp.arange(length // 32) * 32).astype(jnp.float32)[:, None] * freqs[None, :]
    fine = jnp.arange(32).astype(jnp.float32)[:, None] * freqs[None, :]
    cos_a, sin_a = jnp.cos(coarse)[:, None], jnp.sin(coarse)[:, None]
    cos_b, sin_b = jnp.cos(fine)[None], jnp.sin(fine)[None]
    cosine = (cos_a * cos_b - sin_a * sin_b).reshape(length, width // 2)
    sine = (sin_a * cos_b + cos_a * sin_b).reshape(length, width // 2)
    return cosine, sine


def halves_matrix(width):
    row = lax.broadcasted_iota(jnp.int32, (width, width), 0)
    column = lax.broadcasted_iota(jnp.int32, (width, width), 1)
    half = width // 2
    source = jnp.where(row < half, 2 * row, 2 * (row - half) + 1)
    return (column == source).astype(jnp.float32).astype(jnp.bfloat16)


def attend_forward_kernel(
    windows_ref,
    resid_ref,
    gain_ref,
    bias_ref,
    pq_ref,
    pk_ref,
    pv_ref,
    rel_ref,
    cb_ref,
    pb_ref,
    segr_ref,
    segc_ref,
    tab_ref,
    cos_ref,
    sin_ref,
    ha_ref,
    qu_ref,
    qv_ref,
    k_ref,
    v_ref,
    p_ref,
    ctx_ref,
    kt_ref,
    sort_ref,
):
    length = resid_ref.shape[0]
    half = cos_ref.shape[1]
    pair = 2 * HEAD_DIM
    rows = 256

    @pl.when(pl.program_id(0) == 0)
    def first():
        unit, inverse = norm_parts(resid_ref[...])
        ha_ref[...] = (unit * gain_ref[...] + bias_ref[...]).astype(jnp.bfloat16)
        kt_ref[:, pair:] = tab_ref[...]
        sort_ref[...] = halves_matrix(rel_ref.shape[0])

    relative = mul(sort_ref[...], rel_ref[...]).astype(jnp.bfloat16)
    normed = ha_ref[...]
    query = mul(normed, pq_ref[...])
    keys = mul(normed, pk_ref[...]).astype(jnp.bfloat16)
    k_ref[...] = keys
    kt_ref[:, :pair] = keys
    v_ref[...] = mul(normed, pv_ref[...]).astype(jnp.bfloat16)
    qu_ref[...] = (query + cb_ref[...]).astype(jnp.bfloat16)
    qv_ref[...] = (query + pb_ref[...]).astype(jnp.bfloat16)

    def windowed(index, size):
        keys = pl.ds(pl.multiple_of(windows_ref[index], 128), size)
        at = pl.ds(pl.multiple_of(index * rows, rows), rows)
        same = segc_ref[at, :] == segr_ref[:, keys]
        cosine, sine = cos_ref[at, :], sin_ref[at, :]
        contexts = []
        for head in range(2):
            own = head_mask(rows, head)
            part_u = jnp.where(own, qu_ref[at, :], 0) * 0.125
            part_v = jnp.where(own, qv_ref[at, :], 0)
            coef = mul(part_v, relative, NT) * 0.125
            left, right = coef[:, :half], coef[:, half:]
            turned_a = (left * sine + right * cosine).astype(jnp.bfloat16)
            turned_b = (right * sine - left * cosine).astype(jnp.bfloat16)
            scores = mul(
                jnp.concatenate([part_u.astype(jnp.bfloat16), turned_a, turned_b], 1), kt_ref[keys, :], NT
            )
            scores = jnp.where(same, scores, blocked)
            peak = jnp.max(scores, -1, keepdims=True)
            raised = jnp.exp(scores - peak)
            summed = jnp.sum(raised, -1, keepdims=True)
            chances = (raised * (1.0 / summed)).astype(jnp.bfloat16)
            p_ref[head, at, keys] = chances
            contexts.append(mul(chances, v_ref[keys, :]))
        ctx_ref[at, :] = jnp.where(head_mask(rows, 0), contexts[0], contexts[1]).astype(jnp.bfloat16)

    def block(index, carry):
        count = windows_ref[length // rows + index]
        for size in WINDOWS:
            pl.when(count == size)(functools.partial(windowed, index, size))
        return carry

    lax.fori_loop(0, length // rows, block, 0)


def attend_backward_kernel(resumed, ends, windows_ref, *refs):
    operands = 18
    if not resumed:
        refs = refs[:operands] + (None,) + refs[operands:]
    attend_backward_body(ends, windows_ref, *refs)


def attend_backward_body(
    ends,
    windows_ref,
    p_ref,
    tab_ref,
    cos_ref,
    sin_ref,
    resid_ref,
    slope_ref,
    ha_ref,
    qu_ref,
    qv_ref,
    k_ref,
    v_ref,
    ctx_ref,
    ao_ref,
    pq_ref,
    pk_ref,
    pv_ref,
    rel_ref,
    gain_ref,
    begin_ref,
    g1_ref,
    dao_ref,
    dpq_ref,
    dpk_ref,
    dpv_ref,
    drel_ref,
    vec_ref,
    kt_ref,
    dout_ref,
    dctx_ref,
    dn_ref,
    dq_ref,
    dkt_ref,
    dvt_ref,
    drt_ref,
    sort_ref,
):
    length = resid_ref.shape[0]
    half = cos_ref.shape[1]
    pair = 2 * HEAD_DIM
    rows = 256
    step = pl.program_id(0)
    lanes = pl.ds(pl.multiple_of(step * pair, pair), pair)

    @pl.when(step == 0)
    def first():
        dout_ref[...] = slope_ref[...].astype(jnp.bfloat16)
        kt_ref[:, pair:] = tab_ref[...]
        dn_ref[...] = jnp.zeros_like(dn_ref) if begin_ref is None else begin_ref[...]
        vec_ref[...] = jnp.zeros_like(vec_ref)
        sort_ref[...] = halves_matrix(rel_ref.shape[0])

    kt_ref[:, :pair] = k_ref[...]
    relative = mul(sort_ref[...], rel_ref[...]).astype(jnp.bfloat16)
    dao_ref[...] = mul(ctx_ref[...], dout_ref[...], TN).astype(jnp.bfloat16)
    dctx_ref[...] = mul(dout_ref[...], ao_ref[...], NT).astype(jnp.bfloat16)
    dkt_ref[...] = jnp.zeros_like(dkt_ref)
    dvt_ref[...] = jnp.zeros_like(dvt_ref)
    drt_ref[...] = jnp.zeros_like(drt_ref)

    def windowed(index, size):
        keys = pl.ds(pl.multiple_of(windows_ref[index], 128), size)
        at = pl.ds(pl.multiple_of(index * rows, rows), rows)
        cosine, sine = cos_ref[at, :], sin_ref[at, :]
        total = jnp.zeros((rows, pair), jnp.float32)
        sum_u = jnp.zeros((1, pair), jnp.float32)
        sum_v = jnp.zeros((1, pair), jnp.float32)
        for head in range(2):
            own = head_mask(rows, head)
            part = jnp.where(own, dctx_ref[at, :], 0)
            low = p_ref[head, at, keys]
            chances = low.astype(jnp.float32)
            raw = mul(part, v_ref[keys, :], NT)
            weighted = chances * raw
            delta = jnp.sum(weighted, -1, keepdims=True)
            slope = ((weighted - chances * delta) * 0.125).astype(jnp.bfloat16)
            dvt_ref[:, keys] += mul(part, low, TN)
            dkt_ref[:, keys] += mul(jnp.where(own, qu_ref[at, :], 0), slope, TN)
            wide = mul(slope, kt_ref[keys, :])
            slope_u = jnp.where(own, wide[:, :pair], 0.0)
            first, second = wide[:, pair : pair + half], wide[:, pair + half :]
            coef = jnp.concatenate(
                [
                    (first * sine - second * cosine).astype(jnp.bfloat16),
                    (first * cosine + second * sine).astype(jnp.bfloat16),
                ],
                1,
            )
            slope_v = jnp.where(own, mul(coef, relative), 0.0)
            drt_ref[...] += mul(jnp.where(own, qv_ref[at, :], 0), coef, TN)
            total = total + slope_u + slope_v
            sum_u = sum_u + jnp.sum(slope_u, 0, keepdims=True)
            sum_v = sum_v + jnp.sum(slope_v, 0, keepdims=True)
        dq_ref[at, :] = total
        vec_ref[0:1, lanes] += sum_u
        vec_ref[1:2, lanes] += sum_v

    def block(index, carry):
        count = windows_ref[length // rows + index]
        for size in WINDOWS:
            pl.when(count == size)(functools.partial(windowed, index, size))
        return carry

    lax.fori_loop(0, length // rows, block, 0)
    low_q = dq_ref[...].astype(jnp.bfloat16)
    low_k = dkt_ref[...].T.astype(jnp.bfloat16)
    low_v = dvt_ref[...].T.astype(jnp.bfloat16)
    drel = drt_ref[...].T.astype(jnp.bfloat16)
    drel_ref[...] = mul(sort_ref[...], drel, TN).astype(jnp.bfloat16)
    normed = ha_ref[...]
    dpq_ref[...] = mul(normed, low_q, TN).astype(jnp.bfloat16)
    dpk_ref[...] = mul(normed, low_k, TN).astype(jnp.bfloat16)
    dpv_ref[...] = mul(normed, low_v, TN).astype(jnp.bfloat16)
    dn_ref[...] += (
        mul(low_q, pq_ref[...], NT) + mul(low_k, pk_ref[...], NT) + mul(low_v, pv_ref[...], NT)
    )

    @pl.when(step == pl.num_programs(0) - 1)
    def last():
        slope = dn_ref[...]
        if not ends:
            g1_ref[...] = slope
            return
        unit, inverse = norm_parts(resid_ref[...])
        vec_ref[2:3, :] = jnp.sum(slope * unit, 0, keepdims=True)
        vec_ref[3:4, :] = jnp.sum(slope, 0, keepdims=True)
        g1_ref[...] = slope_ref[...] + norm_slope(unit, inverse, slope, gain_ref[...])


def whole(shape):
    return pl.BlockSpec(shape, lambda p, *_: (0,) * len(shape))


def columns(rows, width, shift=0):
    return pl.BlockSpec((rows, width), lambda p, *_: (0, p + shift))


ROW_BLOCK = 256
WINDOWS = (512, 640, 768, 1024)


def key_windows(segment):
    length = segment.shape[0]
    firsts = segment[::ROW_BLOCK]
    lasts = segment[ROW_BLOCK - 1 :: ROW_BLOCK]
    start = jnp.sum(segment[None, :] < firsts[:, None], 1).astype(jnp.int32) // 128 * 128
    need = jnp.sum(segment[None, :] <= lasts[:, None], 1).astype(jnp.int32) - start
    count = jnp.full_like(need, length)
    for size in WINDOWS[::-1]:
        count = jnp.where(need <= size, size, count)
    return jnp.concatenate([jnp.minimum(start, length - count), count])


def attention_forward(first, count, resid, segments, segment_column, weights, tables, windows):
    gain, bias, packed, content_bias, position_bias = weights
    table, cosine, sine = tables
    length, width = resid.shape
    pair = 2 * HEAD_DIM
    pairs = HEADS // 2
    low = jnp.bfloat16
    shape = jax.ShapeDtypeStruct
    return pl.pallas_call(
        attend_forward_kernel,
        grid_spec=pltpu.PrefetchScalarGridSpec(
            num_scalar_prefetch=1,
            grid=(count,),
            in_specs=[
            whole((length, width)),
            pl.BlockSpec((None, 1, width), lambda p, *_: (gain[1], 0, 0)),
            pl.BlockSpec((None, 1, width), lambda p, *_: (bias[1], 0, 0)),
            columns(width, pair, first),
            columns(width, pair, first + pairs),
            columns(width, pair, first + 2 * pairs),
            columns(width, pair, first + 3 * pairs),
            pl.BlockSpec((None, 1, pair), lambda p, *_: (content_bias[1], 0, p + first)),
            pl.BlockSpec((None, 1, pair), lambda p, *_: (position_bias[1], 0, p + first)),
            whole((1, length)),
            whole((length, 1)),
            whole((length, width)),
            whole((length, width // 2)),
            whole((length, width // 2)),
        ],
        out_specs=[whole((length, width))]
        + [columns(length, pair)] * 4
        + [pl.BlockSpec((2, length, length), lambda p, *_: (p, 0, 0)), columns(length, pair)],
        scratch_shapes=[pltpu.VMEM((length, pair + width), low), pltpu.VMEM((width, width), low)],
        ),
        out_shape=[shape((length, width), low)]
        + [shape((length, count * pair), low)] * 4
        + [shape((2 * count, length, length), low), shape((length, count * pair), low)],
        compiler_params=pltpu.CompilerParams(vmem_limit_bytes=56 * 1024 * 1024),
        cost_estimate=pl.CostEstimate(flops=count * 6 * 10**9, bytes_accessed=count * 8 * 10**6, transcendentals=count * 2 * 10**6),
        name="attend_forward",
    )(
        windows,
        resid,
        gain[0],
        bias[0],
        packed,
        packed,
        packed,
        packed,
        content_bias[0],
        position_bias[0],
        segments,
        segment_column,
        table,
        cosine,
        sine,
    )


def attention_backward(first, count, last, resid, slope, weights, tables, kept, partial, windows):
    gain, bias, packed, content_bias, position_bias = weights
    table, cosine, sine = tables
    normed, query_u, query_v, keys, values, chances, context = kept
    length, width = resid.shape
    pair = 2 * HEAD_DIM
    pairs = HEADS // 2
    low, full = jnp.bfloat16, jnp.float32
    shape = jax.ShapeDtypeStruct
    begin = [] if partial is None else [partial]
    return pl.pallas_call(
        functools.partial(attend_backward_kernel, bool(begin), last),
        grid_spec=pltpu.PrefetchScalarGridSpec(
            num_scalar_prefetch=1,
            grid=(count,),
            in_specs=[
            pl.BlockSpec((2, length, length), lambda p, *_: (p + first, 0, 0)),
            whole((length, width)),
            whole((length, width // 2)),
            whole((length, width // 2)),
            whole((length, width)),
            whole((length, width)),
            whole((length, width)),
        ]
        + [columns(length, pair, first)] * 5
        + [
            pl.BlockSpec((pair, width), lambda p, *_: (p + first, pairs)),
            columns(width, pair, first),
            columns(width, pair, first + pairs),
            columns(width, pair, first + 2 * pairs),
            columns(width, pair, first + 3 * pairs),
            pl.BlockSpec((None, 1, width), lambda p, *_: (gain[1], 0, 0)),
        ]
        + [whole((length, width))] * len(begin),
        out_specs=[
            whole((length, width)),
            pl.BlockSpec((pair, width), lambda p, *_: (p, 0)),
            columns(width, pair),
            columns(width, pair),
            columns(width, pair),
            columns(width, pair),
            whole((8, width)),
        ],
        scratch_shapes=[
            pltpu.VMEM((length, pair + width), low),
            pltpu.VMEM((length, width), low),
            pltpu.VMEM((length, pair), low),
            pltpu.VMEM((length, width), full),
            pltpu.VMEM((length, pair), full),
            pltpu.VMEM((pair, length), full),
            pltpu.VMEM((pair, length), full),
            pltpu.VMEM((pair, width), full),
            pltpu.VMEM((width, width), low),
        ],
        ),
        out_shape=[shape((length, width), full), shape((count * pair, width), low)]
        + [shape((width, count * pair), low)] * 4
        + [shape((8, width), full)],
        compiler_params=pltpu.CompilerParams(vmem_limit_bytes=60 * 1024 * 1024),
        cost_estimate=pl.CostEstimate(
            flops=count * 10**10, bytes_accessed=20 * 10**6, transcendentals=0
        ),
        name="attend_backward",
    )(
        windows,
        chances,
        table,
        cosine,
        sine,
        resid,
        slope,
        normed,
        query_u,
        query_v,
        keys,
        values,
        context,
        packed,
        packed,
        packed,
        packed,
        packed,
        gain[0],
        *begin,
    )


FAST = {"z": 4, "y": 2, "x": 2, "c": 2}


def grid_of(count_dp, count_fsdp):
    depth = 4 if count_dp % 4 == 0 else count_dp
    cores = 2 if count_fsdp % 2 == 0 else 1
    return {"z": depth, "y": count_dp // depth, "x": count_fsdp // cores, "c": cores}


def sizes():
    return grid_of(lax.axis_size("dp"), lax.axis_size("fsdp"))


def place(grid, axis):
    index = lax.axis_index(AXES)
    for name in ("c", "x", "y", "z"):
        if name == axis:
            return index % grid[name]
        index = index // grid[name]


def number(grid, at):
    return ((at["z"] * grid["y"] + at["y"]) * grid["x"] + at["x"]) * grid["c"] + at["c"]


def move(value, grid, **steps):
    pairs = []
    for z in range(grid["z"]):
        for y in range(grid["y"]):
            for x in range(grid["x"]):
                for c in range(grid["c"]):
                    at = {"z": z, "y": y, "x": x, "c": c}
                    to = {name: (at[name] + steps.get(name, 0)) % grid[name] for name in at}
                    pairs.append((number(grid, at), number(grid, to)))
    return lax.ppermute(value, AXES, pairs)


PLANE = ((0, 1), (1, 0), (1, 1))


def tie(*values):
    return lax.optimization_barrier(values)


def total_of(value, beside=None):
    grid = sizes()
    if grid != FAST:
        done = beside(value) if beside else None
        return lax.psum(value, AXES), done
    value = value + move(value, grid, c=1)
    moved = [move(value, grid, y=dy, x=dx) for dy, dx in PLANE]
    done = None
    if beside:
        done = beside(value)
        *moved, done = tie(*moved, done)
    value = value + sum(moved)
    return value + sum(move(value, grid, z=step) for step in range(1, grid["z"])), done


class Chain:
    def __init__(self, steps, grid):
        self.steps, self.grid, self.value = steps, grid, None
        self.start(next(steps))

    def start(self, sends):
        self.pending = [move(value, self.grid, **how) for value, how in sends]

    def step(self, *held):
        count = len(self.pending)
        tied = tie(*self.pending, *held)
        arrived, held = tied[:count], tied[count:]
        try:
            sends = self.steps.send(list(arrived))
        except StopIteration as stop:
            self.value, self.pending = stop.value, []
            return held
        count = len(sends)
        tied = tie(*[value for value, _ in sends], *held)
        self.start([(value, how) for value, (_, how) in zip(tied[:count], sends, strict=True)])
        return tied[count:]

    def finish(self):
        while self.pending:
            try:
                self.start(self.steps.send(self.pending))
            except StopIteration as stop:
                self.value, self.pending = stop.value, []
        return self.value


class Still:
    def __init__(self, value):
        self.value, self.pending = value, []

    def step(self, *held):
        return held

    def finish(self):
        return self.value


def advance(chains, *held):
    pending = [value for chain in chains for value in chain.pending]
    tied = list(tie(*pending, *held))
    held = tied[len(pending) :]
    sends = []
    for chain in chains:
        arrived = [tied.pop(0) for _ in chain.pending]
        chain.pending = []
        if not arrived:
            sends.append([])
            continue
        try:
            sends.append(chain.steps.send(arrived))
        except StopIteration as stop:
            chain.value = stop.value
            sends.append([])
    values = [value for part in sends for value, _ in part]
    if not values:
        return held
    tied = list(tie(*values, *held))
    held = tied[len(values) :]
    for chain, part in zip(chains, sends, strict=True):
        chain.pending = [move(tied.pop(0), chain.grid, **how) for _, how in part]
    return held


def gather_steps(value, depth_first):
    value = value[None]
    plane = [{"y": dy, "x": dx} for dy, dx in PLANE]
    if depth_first:
        column = [value] + (yield [(value, {"z": step}) for step in range(1, 4)])
        value = jnp.concatenate(column, 0)
        pieces = [value] + (yield [(value, how) for how in plane])
    else:
        chips = [value] + (yield [(value, how) for how in plane])
        value = jnp.concatenate(chips, 0)
        pieces = [value]
        for _ in range(3):
            (value,) = yield [(value, {"z": 1})]
            pieces.append(value)
    return pieces + (yield [(piece, {"c": 1}) for piece in pieces])


def gathered_from(grid, depth_first):
    own = {axis: place(grid, axis) for axis in grid}
    column = [{"z": -step} for step in range(4)]
    plane = [{}] + [{"y": dy, "x": dx} for dy, dx in PLANE]
    found = []
    for core in range(2):
        for outer in plane if depth_first else column:
            for inner in column if depth_first else plane:
                at = {"c": core, **outer, **inner}
                found.append(
                    number(grid, {axis: (own[axis] + at.get(axis, 0)) % grid[axis] for axis in grid})
                )
    return jnp.stack(found)


def gather_experts(value, depth_first):
    grid = sizes()
    if grid == FAST:
        return Chain(gather_steps(value, depth_first), grid), gathered_from(grid, depth_first)
    pieces, ids = gather_whole(value)
    return Still(pieces), ids


def gather_whole(value):
    grid = sizes()
    if grid == FAST:
        blocks = lax.all_gather(value, AXES, axis=0, tiled=False)
        return [blocks], jnp.arange(blocks.shape[0], dtype=jnp.int32)
    blocks = lax.all_gather(value, AXES, axis=1, tiled=True)
    return [blocks[None]], jnp.zeros((1,), jnp.int32)


def gather_both(value):
    (blocks,), ids = gather_whole(value)
    return blocks, ids


def block_at(value, index, at):
    return lax.dynamic_index_in_dim(value, index % value.shape[at], at, keepdims=False)


def wide(value):
    return value.astype(jnp.float32)


def scatter_steps(keep, send, depth_first, grid):
    shape = (4, 2, 2) + keep.shape[1:]
    low = jnp.bfloat16
    z, y, x = (place(grid, axis) for axis in "zyx")
    (other,) = yield [(send, {"c": 1})]
    keep, other = keep.reshape(shape), other.reshape(shape)

    def near(value, at, dy, dx):
        return wide(block_at(block_at(value, y + dy, at), x + dx, at))

    def below(value, step):
        return wide(block_at(value, z + 4 - step, 0))

    if depth_first:
        part = (below(keep, 1) + below(other, 1)).astype(low)
        for step in (2, 3, 0):
            (part,) = yield [(part, {"z": 1})]
            part = (wide(part) + below(keep, step) + below(other, step)).astype(low)
        moved = yield [(near(part, 0, dy, dx).astype(low), {"y": dy, "x": dx}) for dy, dx in PLANE]
        return near(part, 0, 0, 0) + sum(wide(value) for value in moved)
    sends = [
        ((near(keep, 1, dy, dx) + near(other, 1, dy, dx)).astype(low), {"y": dy, "x": dx})
        for dy, dx in PLANE
    ]
    moved = yield sends
    column = near(keep, 1, 0, 0) + near(other, 1, 0, 0) + sum(wide(value) for value in moved)
    column = column.astype(low)
    moved = yield [(block_at(column, z + step, 0), {"z": step}) for step in range(1, 4)]
    return wide(block_at(column, z, 0)) + sum(wide(value) for value in moved)


def scatter_parts(parts, depth_first):
    grid = sizes()
    if len(parts) == 2:
        return Chain(scatter_steps(*parts, depth_first, grid), grid)
    return Still(wide(scatter_rows(by_devices(parts[0]))))


def scatter_rows(value):
    return lax.psum_scatter(value, AXES, scatter_dimension=0, tiled=False)


def halves(value):
    grid = sizes()
    if grid != FAST:
        return [value]
    value = value.reshape((16, 2) + value.shape[1:])
    core = place(grid, "c")
    return [block_at(value, core, 1), block_at(value, core + 1, 1)]


def by_devices(value):
    if value.ndim < 4:
        return value
    devices = lax.axis_size(AXES)
    return value.reshape((EXPERTS, devices, -1, value.shape[3])).transpose(1, 0, 2, 3)


def single(kernel, name, inputs, outputs, scratch, flops, size):
    values, specs = [], []
    for item in inputs:
        if not isinstance(item, tuple):
            value, block, index = item, item.shape, (0,) * item.ndim
        elif len(item) == 2:
            value, block, index = item[0], (None,) + item[0].shape[1:], (item[1], 0, 0)
        else:
            value, block, index = item
        values.append(value)
        specs.append(pl.BlockSpec(block, functools.partial(lambda index, step: index, index)))
    return pl.pallas_call(
        kernel,
        grid=(1,),
        in_specs=specs,
        out_specs=[pl.BlockSpec(o.shape, lambda step: (0, 0)) for o in outputs],
        out_shape=outputs,
        scratch_shapes=scratch,
        compiler_params=pltpu.CompilerParams(vmem_limit_bytes=60 * 1024 * 1024),
        cost_estimate=pl.CostEstimate(flops=flops, bytes_accessed=size, transcendentals=10**6),
        name=name,
    )(*values)


CHUNK = 64
EDGE = 8


def tap_masks(segments):
    half = KERNEL // 2
    segment = segments[0]
    length = segment.shape[0]
    padded = jnp.pad(segment, (half, half), constant_values=-1)
    same = [padded[k : k + length] == segment for k in range(KERNEL)]
    masks = jnp.stack(same, 1).astype(jnp.float32)
    return jnp.pad(masks, ((0, 0), (0, 128 - KERNEL)))


def conv_front_kernel(
    resid_ref, ctx_ref, ao_ref, gain_ref, bias_ref, gated_ref, taps_ref, mask_ref,
    out_ref, normed_ref, joined_ref, depth_ref, sums_ref,
    pad_ref,
):
    length, width = resid_ref.shape
    resid = resid_ref[...] + mul(ctx_ref[...], ao_ref[...])
    out_ref[...] = resid
    unit, inverse = norm_parts(resid)
    normed = (unit * gain_ref[...] + bias_ref[...]).astype(jnp.bfloat16)
    normed_ref[...] = normed
    joined = mul(normed, gated_ref[...])
    joined_ref[...] = joined
    pad_ref[:EDGE, :] = jnp.zeros((EDGE, width), jnp.float32)
    pad_ref[EDGE + length :, :] = jnp.zeros((EDGE, width), jnp.float32)
    pad_ref[EDGE : EDGE + length, :] = joined[:, :width] * sigmoid(joined[:, width:])
    sums_ref[...] = jnp.zeros_like(sums_ref)

    def chunk(index, carry):
        at = pl.ds(pl.multiple_of(index * CHUNK, CHUNK), CHUNK)
        window = pad_ref[pl.ds(pl.multiple_of(index * CHUNK, CHUNK), CHUNK + 2 * EDGE), :]
        masks = mask_ref[at, :]
        total = jnp.zeros((CHUNK, width), jnp.float32)
        for k in range(KERNEL):
            total = total + window[k + 1 : k + 1 + CHUNK] * masks[:, k : k + 1] * taps_ref[k : k + 1, :]
        depth_ref[at, :] = total
        sums_ref[0:1, :] += jnp.sum(total, 0, keepdims=True)
        sums_ref[1:2, :] += jnp.sum(total * total, 0, keepdims=True)
        return carry

    lax.fori_loop(0, length // CHUNK, chunk, 0)


def conv_front(resid, context, attend_out, gain, bias, gated_in, taps, masks):
    length, width = resid.shape
    low, full = jnp.bfloat16, jnp.float32
    shape = jax.ShapeDtypeStruct
    return single(
        conv_front_kernel,
        "conv_front",
        [resid, context, attend_out, gain, bias, gated_in, taps, masks],
        [
            shape((length, width), full),
            shape((length, width), low),
            shape((length, 2 * width), full),
            shape((length, width), full),
            shape((2, width), full),
        ],
        [pltpu.VMEM((length + 2 * EDGE, width), full)],
        4 * 10**9,
        16 * 10**6,
    )


def batch_stats(stats, frames):
    average = stats[0:1, :] * (1.0 / frames)
    spread = stats[1:2, :] * (1.0 / frames) - average * average
    return average, lax.rsqrt(spread + eps)


def conv_tail_kernel(
    frames, depth_ref, stats_ref, bgain_ref, bbias_ref, point_ref, resid_ref,
    embed_ref, router_ref, gain_ref, bias_ref,
    out_ref, normed_ref, probs_ref,
):
    average, inverse = batch_stats(stats_ref[...], frames)
    shifted = (depth_ref[...] - average) * inverse * bgain_ref[...] + bbias_ref[...]
    tail = (shifted * sigmoid(shifted)).astype(jnp.bfloat16)
    resid = resid_ref[...] + mul(tail, point_ref[...])
    out_ref[...] = resid
    unit, spread = norm_parts(resid)
    normed = (unit * gain_ref[...] + bias_ref[...]).astype(jnp.bfloat16)
    normed_ref[...] = normed
    probs_ref[...] = route_probs(normed, embed_ref[...], router_ref)


def conv_tail(frames, depth, stats, bgain, bbias, point_out, resid, embedding, router, gain, bias):
    length, width = resid.shape
    shape = jax.ShapeDtypeStruct
    return single(
        functools.partial(conv_tail_kernel, frames),
        "conv_tail",
        [depth, stats, bgain, bbias, point_out, resid, embedding, router, gain, bias],
        [
            shape((length, width), jnp.float32),
            shape((length, width), jnp.bfloat16),
            shape((length, 128), jnp.float32),
        ],
        [],
        10**9,
        8 * 10**6,
    )


def conv_turn_kernel(
    frames, slope_ref, depth_ref, stats_ref, bgain_ref, bbias_ref, point_ref,
    dshift_ref, dpoint_ref, sums_ref,
):
    average, inverse = batch_stats(stats_ref[...], frames)
    centered = (depth_ref[...] - average) * inverse
    shifted = centered * bgain_ref[...] + bbias_ref[...]
    sigma = sigmoid(shifted)
    low = slope_ref[...].astype(jnp.bfloat16)
    dpoint_ref[...] = mul((shifted * sigma).astype(jnp.bfloat16), low, TN).astype(jnp.bfloat16)
    dshift = mul(low, point_ref[...], NT) * (sigma * (1.0 + shifted * (1.0 - sigma)))
    dshift_ref[...] = dshift
    sums_ref[0:1, :] = jnp.sum(dshift * centered, 0, keepdims=True)
    sums_ref[1:2, :] = jnp.sum(dshift, 0, keepdims=True)


def conv_turn(frames, slope, depth, stats, bgain, bbias, point_out):
    length, width = slope.shape
    shape = jax.ShapeDtypeStruct
    return single(
        functools.partial(conv_turn_kernel, frames),
        "conv_turn",
        [slope, depth, stats, bgain, bbias, point_out],
        [
            shape((length, width), jnp.float32),
            shape((width, width), jnp.bfloat16),
            shape((2, width), jnp.float32),
        ],
        [],
        10**9,
        8 * 10**6,
    )


def conv_back_kernel(
    frames, slope_ref, dshift_ref, depth_ref, stats_ref, sums_ref, bgain_ref, joined_ref, normed_ref,
    resid_ref, gain_ref, gated_ref, taps_ref, mask_ref,
    out_ref, dgated_ref, dtaps_ref, dgain_ref, dbias_ref,
    pad_ref, dpad_ref, dtap_ref, dglu_ref,
):
    length, width = resid_ref.shape
    average, inverse = batch_stats(stats_ref[...], frames)
    bgain = bgain_ref[...]
    sums = sums_ref[...] * (1.0 / frames) * bgain
    centered = (depth_ref[...] - average) * inverse
    edge = jnp.zeros((EDGE, width), jnp.float32)
    left = joined_ref[:, :width]
    sigma = sigmoid(joined_ref[:, width:])
    for ref, value in (
        (pad_ref, left * sigma),
        (dpad_ref, inverse * (dshift_ref[...] * bgain - sums[1:2, :] - centered * sums[0:1, :])),
    ):
        ref[:EDGE, :] = edge
        ref[EDGE + length :, :] = edge
        ref[EDGE : EDGE + length, :] = value
    dtap_ref[...] = jnp.zeros_like(dtap_ref)

    def chunk(index, carry):
        at = pl.ds(pl.multiple_of(index * CHUNK, CHUNK), CHUNK)
        around = pl.ds(pl.multiple_of(index * CHUNK, CHUNK), CHUNK + 2 * EDGE)
        window = pad_ref[around, :]
        dwindow = dpad_ref[around, :]
        masks = mask_ref[at, :]
        middle = dwindow[EDGE : EDGE + CHUNK]
        total = jnp.zeros((CHUNK, width), jnp.float32)
        for k in range(KERNEL):
            mask = masks[:, k : k + 1]
            back = KERNEL - 1 - k
            total = total + dwindow[k + 1 : k + 1 + CHUNK] * mask * taps_ref[back : back + 1, :]
            term = window[k + 1 : k + 1 + CHUNK] * mask * middle
            dtap_ref[8 * k : 8 * k + 8, :] += jnp.sum(term.reshape(CHUNK // 8, 8, width), 0)
        dglu_ref[at, :] = total
        return carry

    lax.fori_loop(0, length // CHUNK, chunk, 0)
    for k in range(KERNEL):
        dtaps_ref[k : k + 1, :] = jnp.sum(dtap_ref[8 * k : 8 * k + 8, :], 0, keepdims=True)
    dglu = dglu_ref[...]
    low = jnp.concatenate(
        [
            (dglu * sigma).astype(jnp.bfloat16),
            (dglu * left * sigma * (1.0 - sigma)).astype(jnp.bfloat16),
        ],
        1,
    )
    dgated_ref[...] = mul(normed_ref[...], low, TN).astype(jnp.bfloat16)
    slope = mul(low, gated_ref[...], NT)
    unit, spread = norm_parts(resid_ref[...])
    dgain_ref[...] = jnp.sum(slope * unit, 0, keepdims=True)
    dbias_ref[...] = jnp.sum(slope, 0, keepdims=True)
    out_ref[...] = slope_ref[...] + norm_slope(unit, spread, slope, gain_ref[...])


def conv_back(
    frames, slope, dshift, depth, stats, sums, bgain, joined, normed, resid, gain, gated_in, taps, masks
):
    length, width = resid.shape
    full = jnp.float32
    shape = jax.ShapeDtypeStruct
    padded = pltpu.VMEM((length + 2 * EDGE, width), full)
    return single(
        functools.partial(conv_back_kernel, frames),
        "conv_back",
        [slope, dshift, depth, stats, sums, bgain, joined, normed, resid, gain, gated_in, taps, masks],
        [
            shape((length, width), full),
            shape((width, 2 * width), jnp.bfloat16),
            shape((KERNEL, width), full),
            shape((1, width), full),
            shape((1, width), full),
        ],
        [
            padded,
            padded,
            pltpu.VMEM((8 * KERNEL, width), full),
            pltpu.VMEM((length, width), full),
        ],
        6 * 10**9,
        20 * 10**6,
    )


ROWS = (256, 384, 512)


def one_hot_rows(pos_row, base, rows):
    slot = lax.broadcasted_iota(jnp.int32, (rows, pos_row.shape[1]), 0) + base
    return (slot == pos_row).astype(jnp.float32).astype(jnp.bfloat16)


def one_hot_columns(pos_col, base, rows):
    slot = lax.broadcasted_iota(jnp.int32, (pos_col.shape[0], rows), 1) + base
    return (slot == pos_col).astype(jnp.float32).astype(jnp.bfloat16)


def routed(route_col):
    lane = lax.broadcasted_iota(jnp.int32, (route_col.shape[0], 128), 1)
    return (lane == route_col).astype(jnp.float32)


def sigmoid(value):
    return 1.0 / (1.0 + jnp.exp(-value))


def split_mul(wide, narrow, dims):
    high = wide.astype(jnp.bfloat16)
    rest = (wide - high.astype(jnp.float32)).astype(jnp.bfloat16)
    return mul(high, narrow, dims) + mul(rest, narrow, dims)


def route_probs(normed, embed, router_ref):
    width = normed.shape[1]
    logits = mul(normed, router_ref[:width, :]) + mul(embed, router_ref[width:, :])
    lane = lax.broadcasted_iota(jnp.int32, logits.shape, 1)
    logits = jnp.where(lane < EXPERTS, logits, -jnp.inf)
    raised = jnp.exp(logits - jnp.max(logits, -1, keepdims=True))
    return raised / jnp.sum(raised, -1, keepdims=True)


def sized(count, body):
    lower = -1
    for rows in ROWS:
        pl.when((count > lower) & (count <= rows))(functools.partial(body, rows))
        lower = rows


def assemble(refs, ids_ref, whole_ref):
    at = 0
    for ref in refs:
        rows = ref.shape[2]
        for block in range(ref.shape[0]):
            start = pl.multiple_of(ids_ref[at] * rows, rows)
            whole_ref[pl.ds(start, rows), :] = ref[block, 0]
            at += 1


class Weights:
    def __init__(self, pieces, ids):
        self.arrays, self.ids = pieces, ids
        rows = sum(piece.shape[0] * piece.shape[2] for piece in self.arrays)
        self.shape = (rows, self.arrays[0].shape[3])
        self.rows = self.arrays[0].shape[2]

        self.scratch = [pltpu.VMEM(self.shape, jnp.bfloat16)]

    def specs(self):
        return [by_owner(piece.shape) for piece in self.arrays]

    def assemble(self, refs, ids_ref, whole_refs):
        assemble(refs, ids_ref, whole_refs[0])


class Both:
    def __init__(self, array, ids, width):
        self.arrays, self.ids = [array], ids
        devices, _, rows, hidden = array.shape
        self.rows, self.across = rows // 2, hidden // width
        self.shape = (devices * self.rows, hidden)
        down = (devices * self.rows * self.across, width)
        self.scratch = [pltpu.VMEM(self.shape, jnp.bfloat16), pltpu.VMEM(down, jnp.bfloat16)]

    def specs(self):
        return [by_owner(self.arrays[0].shape)]

    def assemble(self, refs, ids_ref, whole_refs):
        (ref,), (up_ref, down_ref) = refs, whole_refs
        rows, width = self.rows, down_ref.shape[1]
        for block in range(ref.shape[0]):
            up_ref[block * rows : (block + 1) * rows, :] = ref[block, 0, :rows, :]
            for at in range(self.across):
                start = (block * self.across + at) * rows
                down_ref[start : start + rows, :] = ref[block, 0, rows:, at * width : (at + 1) * width]


def side_by_side(up, down):
    experts, rows, hidden = up.shape
    width = down.shape[2]
    down = down.reshape(experts, hidden // width, rows, width).transpose(0, 2, 1, 3)
    return jnp.concatenate([up, down.reshape(experts, rows, hidden)], 1)


def fixed(shape):
    return pl.BlockSpec(shape, lambda e, *_: (0,) * len(shape))


def by_expert(shape):
    return pl.BlockSpec((1,) + shape, lambda e, *_: (e,) + (0,) * len(shape))


def by_owner(shape):
    return pl.BlockSpec((shape[0], 1) + shape[2:], lambda e, *_: (0, e, 0, 0))


def grads_outputs(weights):
    count = weights.shape[0] // weights.rows
    if count == 1:
        shapes = [(1, EXPERTS) + weights.shape]
    else:
        shapes = [(count // 2, EXPERTS, weights.rows, weights.shape[1])] * 2
    return [(struct(shape, jnp.bfloat16), by_owner(shape)) for shape in shapes]


def expert_call(kernel, name, counts, weights, inputs, outputs, scratch, flops, with_core=False):
    scalars = [counts] + [weight.ids for weight in weights]
    arrays = [piece for weight in weights for piece in weight.arrays]
    n_in, n_out = len(inputs), len(outputs)

    def body(*refs):
        count_ref, *ids = refs[: len(scalars)]
        refs = refs[len(scalars) :]
        pieces, refs = refs[: len(arrays)], refs[len(arrays) :]
        operands, results, rest = refs[:n_in], refs[n_in : n_in + n_out], refs[n_in + n_out :]
        expert = pl.program_id(0)
        n_whole = 0
        for at, weight in enumerate(weights):
            own = pieces[: len(weight.arrays)]
            pieces = pieces[len(weight.arrays) :]
            weight.assemble(own, ids[at], rest[n_whole : n_whole + len(weight.scratch)])
            n_whole += len(weight.scratch)
        kernel(
            expert, count_ref[expert], *rest[:n_whole], *operands, *results, *rest[n_whole:],
            **({"core": count_ref[EXPERTS]} if with_core else {}),
        )

    return pl.pallas_call(
        body,
        grid_spec=pltpu.PrefetchScalarGridSpec(
            num_scalar_prefetch=len(scalars),
            grid=(EXPERTS,),
            in_specs=[spec for weight in weights for spec in weight.specs()]
            + [spec for _, spec in inputs],
            out_specs=[spec for _, spec in outputs],
            scratch_shapes=[whole for weight in weights for whole in weight.scratch] + scratch,
        ),
        out_shape=[shape for shape, _ in outputs],
        compiler_params=pltpu.CompilerParams(vmem_limit_bytes=60 * 1024 * 1024),
        cost_estimate=pl.CostEstimate(
            flops=flops, bytes_accessed=20 * 10**6, transcendentals=4 * 10**6
        ),
        name=name,
    )(*scalars, *arrays, *[value for value, _ in inputs])


def struct(shape, dtype=jnp.float32):
    return jax.ShapeDtypeStruct(shape, dtype)


def whole_in(value):
    if isinstance(value, tuple):
        return row_in(*value)
    return (value, fixed(value.shape))


def row_in(vectors, index):
    return (vectors, pl.BlockSpec((None, 1, vectors.shape[2]), lambda e, *_: (index, 0, 0)))


def whole_out(shape, dtype=jnp.float32):
    return (struct(shape, dtype), fixed(shape))


def expert_in(value):
    return (value, by_expert(value.shape[1:]))


def expert_out(shape, dtype=jnp.bfloat16):
    return (struct((EXPERTS,) + shape, dtype), by_expert(shape))


def spans(hidden):
    chunk = 512
    return [slice(start, start + chunk) for start in range(0, hidden, chunk)]


def up_part(expert, rows, up_ref, normed_ref, posr_ref, picked_ref, inner_ref, then=None):
    hot = one_hot_rows(posr_ref[...], expert * CAPACITY, rows)
    picked = mul(hot, normed_ref[...]).astype(jnp.bfloat16)
    picked_ref[0, :rows, :] = picked
    total = None
    for span in spans(up_ref.shape[1]):
        inner = mul(picked, up_ref[:, span])
        inner_ref[0, :rows, span] = inner.astype(jnp.bfloat16)
        if then is not None:
            part = then(inner, span)
            total = part if total is None else total + part
    return total


def first_up_kernel(expert, count, up_ref, normed_ref, posr_ref, picked_ref, inner_ref):
    def run(rows):
        up_part(expert, rows, up_ref, normed_ref, posr_ref, picked_ref, inner_ref)

    sized(count, run)


def first_up_call(counts, pos_row, normed, up):
    length, width = normed.shape
    return expert_call(
        first_up_kernel,
        "first_up",
        counts,
        [up],
        [whole_in(normed), whole_in(pos_row)],
        [expert_out((CAPACITY, width)), expert_out((CAPACITY, up.shape[1]))],
        [],
        5 * 10**9,
    )


def first_down_kernel(
    expert, count, down_ref, inner_ref, posc_ref, resid_ref, probs_ref, route_ref, out_ref, branch_ref
):
    @pl.when(expert == 0)
    def clear():
        branch_ref[...] = jnp.zeros_like(branch_ref)

    def run(rows):
        total = None
        for span in spans(down_ref.shape[0]):
            inner = inner_ref[0, :rows, span].astype(jnp.float32)
            part = mul((inner * sigmoid(inner)).astype(jnp.bfloat16), down_ref[span, :])
            total = part if total is None else total + part
        hot = one_hot_columns(posc_ref[...], expert * CAPACITY, rows)
        branch_ref[...] += mul(hot, total.astype(jnp.bfloat16))

    sized(count, run)

    @pl.when(expert == EXPERTS - 1)
    def last():
        gate = jnp.sum(probs_ref[...] * routed(route_ref[...]), -1, keepdims=True)
        out_ref[...] = resid_ref[...].astype(jnp.float32) + 0.5 * gate * branch_ref[...]


def first_down_call(counts, pos_col, inner, resid, probs, routes, down):
    shape = resid.shape
    return expert_call(
        first_down_kernel,
        "first_down",
        counts,
        [down],
        [expert_in(inner)] + [whole_in(v) for v in (pos_col, resid, probs, routes)],
        [whole_out(shape), whole_out(shape)],
        [],
        5 * 10**9,
    )


def second_forward_kernel(
    expert, count, up_ref, down_ref,
    normed_ref, posr_ref, posc_ref, resid_ref, probs_ref, route_ref, cot_ref, gain_ref, bias_ref,
    picked_ref, inner_ref, branch_ref, result_ref, g4_ref, dgain_ref, dbias_ref,
):
    @pl.when(expert == 0)
    def clear():
        branch_ref[...] = jnp.zeros_like(branch_ref)

    def run(rows):
        def then(inner, span):
            return mul((inner * sigmoid(inner)).astype(jnp.bfloat16), down_ref[span, :])

        total = up_part(expert, rows, up_ref, normed_ref, posr_ref, picked_ref, inner_ref, then)
        hot = one_hot_columns(posc_ref[...], expert * CAPACITY, rows)
        branch_ref[...] += mul(hot, total.astype(jnp.bfloat16))

    sized(count, run)

    @pl.when(expert == EXPERTS - 1)
    def last():
        gate = jnp.sum(probs_ref[...] * routed(route_ref[...]), -1, keepdims=True)
        unit, inverse = norm_parts(resid_ref[...] + 0.5 * gate * branch_ref[...])
        gain = gain_ref[...]
        cot = cot_ref[...].astype(jnp.float32)
        result_ref[...] = (unit * gain + bias_ref[...]).astype(jnp.bfloat16)
        dgain_ref[...] = jnp.sum(cot * unit, 0, keepdims=True)
        dbias_ref[...] = jnp.sum(cot, 0, keepdims=True)
        g4_ref[...] = norm_slope(unit, inverse, cot, gain)


def second_forward_call(counts, pos_row, pos_col, normed, resid, probs, routes, cot, gain, bias, weights):
    length, width = normed.shape
    return expert_call(
        second_forward_kernel,
        "second_forward",
        counts,
        weights,
        [whole_in(v) for v in (normed, pos_row, pos_col, resid, probs, routes, cot, gain, bias)],
        [
            expert_out((CAPACITY, width)),
            expert_out((CAPACITY, weights[0].shape[1])),
            whole_out((length, width)),
            whole_out((length, width), jnp.bfloat16),
            whole_out((length, width)),
            whole_out((1, width)),
            whole_out((1, width)),
        ],
        [],
        10 * 10**9,
    )


def enter_slope(slope_ref, probs_ref, route_ref, branch_ref, low_ref, dlogits_ref):
    chosen = routed(route_ref[...])
    probs = probs_ref[...]
    gate = jnp.sum(probs * chosen, -1, keepdims=True)
    slope = slope_ref[...]
    low_ref[...] = (0.5 * gate * slope).astype(jnp.bfloat16)
    dgate = 0.5 * jnp.sum(slope * branch_ref[...], -1, keepdims=True)
    dlogits_ref[...] = probs * (chosen - gate) * dgate


def leave_slope(
    dnorm, dlogits, slope_ref, resid_ref, normed_ref, embed_ref, gain_ref,
    out_ref, dgain_ref, dbias_ref, drouter_ref,
):
    width = resid_ref.shape[1]
    unit, inverse = norm_parts(resid_ref[...].astype(jnp.float32))
    dgain_ref[...] = jnp.sum(dnorm * unit, 0, keepdims=True)
    dbias_ref[...] = jnp.sum(dnorm, 0, keepdims=True)
    out_ref[...] = slope_ref[...] + norm_slope(unit, inverse, dnorm, gain_ref[...])
    drouter_ref[:, :width] = split_mul(dlogits, normed_ref[...], TN)
    drouter_ref[:, width:] = split_mul(dlogits, embed_ref[...], TN)


def active_of(inner):
    inner = inner.astype(jnp.float32)
    return (inner * sigmoid(inner)).astype(jnp.bfloat16)


def slope_of(inner):
    inner = inner.astype(jnp.float32)
    sigma = sigmoid(inner)
    return sigma * (1.0 + inner * (1.0 - sigma))


def store_rows(refs, core, first, span, value):
    rows = value.shape[0]
    if len(refs) == 1:
        refs[0][0, 0, first : first + rows, span] = value
        return
    owned = refs[0].shape[2]
    value = value.reshape((rows // owned // 2, 2, 1, owned, value.shape[1]))
    at = slice(first // owned // 2, (first + rows) // owned // 2)
    for own in range(2):

        @pl.when(core == own)
        def store():
            refs[0][at, :, :, span] = value[:, own]
            refs[1][at, :, :, span] = value[:, 1 - own]


def down_grads(rows, core, inner_ref, dpicked, ddown_refs):
    for span in spans(inner_ref.shape[2]):
        grads = mul(active_of(inner_ref[0, :rows, span]), dpicked, TN)
        store_rows(ddown_refs, core, span.start, slice(None), grads.astype(jnp.bfloat16))


def up_grads(core, picked, dinner, span, dup_refs):
    store_rows(dup_refs, core, 0, span, mul(picked, dinner, TN).astype(jnp.bfloat16))


def first_back_kernel(
    expert, count, slope_ref, probs_ref, route_ref, branch_ref, posr_ref, inner_ref, *rest, core
):
    *ddown_refs, dpicked_ref, dlogits_ref, low_ref = rest

    @pl.when(expert == 0)
    def first():
        enter_slope(slope_ref, probs_ref, route_ref, branch_ref, low_ref, dlogits_ref)

    def run(rows):
        hot = one_hot_rows(posr_ref[...], expert * CAPACITY, rows)
        dpicked = mul(hot, low_ref[...]).astype(jnp.bfloat16)
        dpicked_ref[0, :rows, :] = dpicked
        down_grads(rows, core, inner_ref, dpicked, ddown_refs)

    sized(count, run)


def first_back_call(counts, pos_row, slope, probs, routes, branch, inner, down):
    length, width = slope.shape
    return expert_call(
        first_back_kernel,
        "first_down_grads",
        counts,
        [],
        [whole_in(v) for v in (slope, probs, routes, branch, pos_row)] + [expert_in(inner)],
        grads_outputs(down) + [expert_out((CAPACITY, width)), whole_out((length, 128))],
        [pltpu.VMEM((length, width), jnp.bfloat16)],
        5 * 10**9,
        True,
    )


def first_middle_kernel(expert, count, down_ref, dpicked_ref, picked_ref, inner_ref, *rest, core):
    *dup_refs, dinner_ref = rest

    def run(rows):
        dpicked = dpicked_ref[0, :rows, :]
        picked = picked_ref[0, :rows, :]
        for span in spans(inner_ref.shape[2]):
            dactive = mul(dpicked, down_ref[span, :], NT)
            dinner = (dactive * slope_of(inner_ref[0, :rows, span])).astype(jnp.bfloat16)
            dinner_ref[0, :rows, span] = dinner
            up_grads(core, picked, dinner, span, dup_refs)

    sized(count, run)


def first_middle_call(counts, dpicked, picked, inner, up, down):
    return expert_call(
        first_middle_kernel,
        "first_up_grads",
        counts,
        [down],
        [expert_in(v) for v in (dpicked, picked, inner)],
        grads_outputs(up) + [expert_out(inner.shape[1:])],
        [],
        9 * 10**9,
        True,
    )


def first_leave_kernel(
    expert, count, up_ref, dinner_ref, posc_ref, dlogits_ref, router_ref, slope_ref, resid_ref, normed_ref,
    embed_ref, gain_ref,
    out_ref, dgain_ref, dbias_ref, drouter_ref,
    dnorm_ref,
):
    width = up_ref.shape[0]

    @pl.when(expert == 0)
    def first():
        dnorm_ref[...] = split_mul(dlogits_ref[...], router_ref[:width, :], NT)

    def run(rows):
        total = mul(dinner_ref[0, :rows, :], up_ref[...], NT).astype(jnp.bfloat16)
        dnorm_ref[...] += mul(one_hot_columns(posc_ref[...], expert * CAPACITY, rows), total)

    sized(count, run)

    @pl.when(expert == EXPERTS - 1)
    def last():
        leave_slope(
            dnorm_ref[...], dlogits_ref[...], slope_ref, resid_ref, normed_ref, embed_ref, gain_ref,
            out_ref, dgain_ref, dbias_ref, drouter_ref,
        )


def first_leave_call(counts, pos_col, dinner, dlogits, router, slope, resid, normed, embedding, gain, up):
    length, width = slope.shape
    return expert_call(
        first_leave_kernel,
        "first_leave",
        counts,
        [up],
        [expert_in(dinner)]
        + [whole_in(v) for v in (pos_col, dlogits, router, slope, resid, normed, embedding, gain)],
        [
            whole_out((length, width)),
            whole_out((1, width)),
            whole_out((1, width)),
            whole_out((128, 2 * width)),
        ],
        [pltpu.VMEM((length, width), jnp.float32)],
        5 * 10**9,
    )


def second_back_kernel(
    expert, count, up_ref, down_ref, slope_ref, probs_ref, route_ref, branch_ref, posr_ref, posc_ref, inner_ref,
    router_ref, resid_ref, normed_ref, embed_ref, gain_ref,
    out_ref, dgain_ref, dbias_ref, drouter_ref, dpicked_ref, dinner_ref,
    low_ref, dlogits_ref, dnorm_ref,
):
    width = up_ref.shape[0]

    @pl.when(expert == 0)
    def first():
        enter_slope(slope_ref, probs_ref, route_ref, branch_ref, low_ref, dlogits_ref)
        dnorm_ref[...] = split_mul(dlogits_ref[...], router_ref[:width, :], NT)

    def run(rows):
        hot = one_hot_rows(posr_ref[...], expert * CAPACITY, rows)
        dpicked = mul(hot, low_ref[...]).astype(jnp.bfloat16)
        dpicked_ref[0, :rows, :] = dpicked
        total = None
        for span in spans(up_ref.shape[1]):
            dactive = mul(dpicked, down_ref[span, :], NT)
            dinner = (dactive * slope_of(inner_ref[0, :rows, span])).astype(jnp.bfloat16)
            dinner_ref[0, :rows, span] = dinner
            part = mul(dinner, up_ref[:, span], NT)
            total = part if total is None else total + part
        hot = one_hot_columns(posc_ref[...], expert * CAPACITY, rows)
        dnorm_ref[...] += mul(hot, total.astype(jnp.bfloat16))

    sized(count, run)

    @pl.when(expert == EXPERTS - 1)
    def last():
        leave_slope(
            dnorm_ref[...], dlogits_ref[...], slope_ref, resid_ref, normed_ref, embed_ref, gain_ref,
            out_ref, dgain_ref, dbias_ref, drouter_ref,
        )


def second_back_call(
    counts, pos_row, pos_col, slope, probs, routes, branch, inner, router, resid, normed, embedding, gain, weights
):
    length, width = slope.shape
    return expert_call(
        second_back_kernel,
        "second_back",
        counts,
        weights,
        [whole_in(v) for v in (slope, probs, routes, branch, pos_row, pos_col)]
        + [expert_in(inner)]
        + [whole_in(v) for v in (router, resid, normed, embedding, gain)],
        [
            whole_out((length, width)),
            whole_out((1, width)),
            whole_out((1, width)),
            whole_out((128, 2 * width)),
            expert_out((CAPACITY, width)),
            expert_out(inner.shape[1:]),
        ],
        [
            pltpu.VMEM((length, width), jnp.bfloat16),
            pltpu.VMEM((length, 128), jnp.float32),
            pltpu.VMEM((length, width), jnp.float32),
        ],
        10 * 10**9,
    )


def second_grads_kernel(expert, count, picked_ref, inner_ref, dpicked_ref, dinner_ref, out_ref):
    def run(rows):
        picked = picked_ref[0, :rows, :]
        dpicked = dpicked_ref[0, :rows, :]
        owned = out_ref.shape[2] // 2
        width = dpicked.shape[1]
        for span in spans(inner_ref.shape[2]):
            chunk = span.stop - span.start
            grads = mul(picked, dinner_ref[0, :rows, span], TN).astype(jnp.bfloat16)
            out_ref[:, :, :owned, span] = grads.reshape((-1, 1, owned, chunk))
            grads = mul(active_of(inner_ref[0, :rows, span]), dpicked, TN).astype(jnp.bfloat16)
            across = inner_ref.shape[2] // width
            if owned >= chunk:
                at = span.start // owned * width
                out_ref[0, 0, owned:, at : at + width] = grads
                continue
            first = span.start // (across * owned)
            count = chunk // (across * owned)
            grads = grads.reshape((count, 1, across, owned, width))
            for at in range(across):
                out_ref[first : first + count, :, owned:, at * width : (at + 1) * width] = grads[:, :, at]

    sized(count, run)


def second_grads_call(counts, picked, inner, dpicked, dinner, devices):
    hidden, width = inner.shape[2], picked.shape[2]
    shape = (devices, EXPERTS, 2 * width // devices, hidden)
    return expert_call(
        second_grads_kernel,
        "second_grads",
        counts,
        [],
        [expert_in(v) for v in (picked, inner, dpicked, dinner)],
        [(struct(shape, jnp.bfloat16), by_owner(shape))],
        [],
        10 * 10**9,
    )[0]


def enter_kernel(resid_ref, embed_ref, router_ref, gain_ref, bias_ref, normed_ref, probs_ref):
    unit, inverse = norm_parts(resid_ref[...].astype(jnp.float32))
    normed = (unit * gain_ref[...] + bias_ref[...]).astype(jnp.bfloat16)
    normed_ref[...] = normed
    probs_ref[...] = route_probs(normed, embed_ref[...], router_ref)


def expert_enter(resid, embedding, router, gain, bias):
    length, width = resid.shape
    return single(
        enter_kernel,
        "expert_enter",
        [resid, embedding, router, gain, bias],
        [struct((length, width), jnp.bfloat16), struct((length, 128))],
        [],
        10**9,
        4 * 10**6,
    )


def places(routes, core):
    length = routes.shape[0]
    chosen = (routes == jnp.arange(EXPERTS, dtype=jnp.int32)[None, :]).astype(jnp.float32)
    row = lax.broadcasted_iota(jnp.int32, (length, length), 0)
    before = (lax.broadcasted_iota(jnp.int32, (length, length), 1) < row).astype(jnp.bfloat16)
    earlier = product(before, chosen.astype(jnp.bfloat16))
    slot = jnp.sum(earlier * chosen, 1).astype(jnp.int32) + routes[:, 0] * CAPACITY
    counts = jnp.concatenate([jnp.sum(chosen, 0).astype(jnp.int32), core])
    return counts, slot[None, :], slot[:, None]


def gather_rows(value):
    return lax.all_gather(value, AXES, axis=0, tiled=True)


SMALL = 32
ROUTERS = 64


def small_rows(vectors, taps, first_router, second_router):
    row = lax.broadcasted_iota(jnp.int32, (SMALL, vectors[0].shape[0]), 0)
    total = jnp.pad(taps, ((len(vectors), SMALL - len(vectors) - taps.shape[0]), (0, 0)))
    for at, vector in enumerate(vectors):
        total = jnp.where(row == at, vector[None, :], total)
    total = jnp.pad(total, ((0, 0), (0, 128 - total.shape[1])))
    for at, router in ((ROUTERS, first_router), (ROUTERS + EXPERTS, second_router)):
        below, behind = SMALL - router.shape[0], 128 - at - EXPERTS
        total = total + jnp.pad(router, ((0, below), (at, behind)))
    return total


def gathered_count(devices):
    return devices if sizes() == FAST else 1


def scatter_second(value, devices, width):
    if value.shape[0] == 1:
        up = by_devices(value[:, :, :width])
        down = value[0, :, width:].reshape(EXPERTS, width, -1, width).transpose(0, 2, 1, 3)
        down = by_devices(down.reshape(1, EXPERTS, -1, width))
        return [wide(scatter_rows(part)) for part in (up, down)]
    total = wide(scatter_rows(value))
    owned = width // devices
    down = total[:, owned:].reshape(EXPERTS, owned, -1, width).transpose(0, 2, 1, 3)
    return [total[:, :owned], down.reshape(EXPERTS, -1, width)]


def on_device(
    inputs,
    embedding,
    segments,
    routes_first,
    routes_second,
    cotangent,
    first_gain,
    first_bias,
    first_router,
    first_up,
    first_down,
    attend_gain,
    attend_bias,
    project_in,
    relative_weight,
    content_bias,
    position_bias,
    attend_out,
    depth_gain,
    depth_bias,
    gated_in,
    depth_kernel,
    batch_gain,
    batch_bias,
    point_out,
    second_gain,
    second_bias,
    second_router,
    second_up,
    second_down,
    final_gain,
    final_bias,
):
    devices = lax.axis_size(AXES)
    length, width = inputs.shape
    frames = length * devices
    core = jnp.reshape(place(sizes(), "c"), (1,))

    first_up_chain, up_ids = gather_experts(first_up, True)
    first_down_chain, down_ids = gather_experts(first_down, False)
    vectors = [
        first_gain,
        first_bias,
        second_gain,
        second_bias,
        attend_gain,
        attend_bias,
        content_bias,
        position_bias,
        depth_gain,
        depth_bias,
        batch_gain,
        batch_bias,
        final_gain,
        final_bias,
    ]
    own = project_in.shape[0]
    small = small_rows(vectors, depth_kernel, first_router, second_router)
    small = jnp.concatenate([small[start : start + own] for start in range(0, SMALL, own)], 1)
    packed = gather_rows(
        jnp.concatenate([project_in, relative_weight, attend_out, point_out, gated_in, small], 1)
    )
    second = [second_up, second_down]
    if sizes() == FAST:
        second = [side_by_side(second_up, second_down)]

    first_places = places(routes_first, core)
    second_places = places(routes_second, core)
    masks = tap_masks(segments)
    segment_column = segments.reshape(length, 1)
    cosine, sine = angles(length, width)
    table = jnp.concatenate([cosine, sine], 1).astype(jnp.bfloat16)
    masks, table, cosine, sine = advance(
        [first_up_chain, first_down_chain], masks, table, cosine, sine
    )
    pos_row, pos_col = first_down_chain.step(first_places[1], first_places[2])
    tables = (table, cosine, sine)
    counts = first_places[0]

    packed, *second = first_down_chain.step(packed, *second)
    small = packed[:, 8 * width :].reshape(devices, own, SMALL // own, 128)
    small = small.transpose(0, 2, 1, 3).reshape(devices, SMALL, 128)
    n_vec = len(vectors)
    floats = small[:, :n_vec, :own].transpose(1, 0, 2).reshape(n_vec, 1, width).astype(jnp.float32)
    taps = small[:, n_vec : n_vec + KERNEL, :own].transpose(1, 0, 2)
    taps = taps.reshape(KERNEL, width).astype(jnp.float32)

    def router_wide(at):
        router = small[:, : 2 * own, at : at + EXPERTS].reshape(2 * width, EXPERTS)
        return jnp.pad(router, ((0, 0), (0, 128 - EXPERTS)))

    first_router_full = router_wide(ROUTERS)
    second_router_full = router_wide(ROUTERS + EXPERTS)

    def vec(index):
        return (floats, index)

    first_normed, first_probs = expert_enter(inputs, embedding, first_router_full, vec(0), vec(1))
    first_normed, first_probs, floats, taps, second_router_full = first_up_chain.step(
        first_normed, first_probs, floats, taps, second_router_full
    )
    first_ups = Weights(first_up_chain.finish(), up_ids)

    windows = key_windows(segments[0])
    attend_full = (vec(4), vec(5), packed, vec(6), vec(7))
    attend_out_full = (packed, (width, width), (0, 4))
    point_full = (packed, (width, width), (0, 5))
    gated_full = (packed, (width, 2 * width), (0, 3))

    first_normed, *second = first_down_chain.step(first_normed, *second)
    if sizes() == FAST:
        second_weights = [Both(*gather_both(second[0]), width)]
    else:
        second_weights = [Weights(*gather_whole(value)) for value in second]
    first_picked, first_inner = first_up_call(counts, pos_row, first_normed, first_ups)
    first_downs = Weights(first_down_chain.finish(), down_ids)
    first_resid, first_branch = first_down_call(
        counts, pos_col, first_inner, inputs, first_probs, routes_first, first_downs
    )
    pairs = HEADS // 2
    kept = attention_forward(
        0, pairs, first_resid, segments, segment_column, attend_full, tables, windows
    )
    attend_resid, conv_normed, joined, depth, stats = conv_front(
        first_resid, kept[6], attend_out_full, vec(8), vec(9), gated_full, taps, masks
    )
    stats, _ = total_of(stats)
    conv_resid, second_normed, second_probs = conv_tail(
        frames, depth, stats, vec(10), vec(11), point_full, attend_resid,
        embedding, second_router_full, vec(2), vec(3),
    )
    (
        second_picked,
        second_inner,
        second_branch,
        result,
        slope,
        final_gain_grad,
        final_bias_grad,
    ) = second_forward_call(
        *second_places, second_normed, conv_resid, second_probs, routes_second,
        cotangent, vec(12), vec(13), second_weights,
    )
    slope, dgain_second, dbias_second, drouter_second, dpicked, dinner = second_back_call(
        *second_places, slope, second_probs, routes_second, second_branch, second_inner,
        second_router_full, conv_resid, second_normed, embedding, vec(2), second_weights,
    )
    dshift, dpoint, sums = conv_turn(frames, slope, depth, stats, vec(10), vec(11), point_full)

    def deferred(sums):
        held, _ = tie(dpicked, sums)
        return second_grads_call(
            second_places[0], second_picked, second_inner, held, dinner, gathered_count(devices)
        )

    sums, second_large = total_of(sums, deferred)
    second_large = scatter_second(second_large, devices, width)
    slope, dgated, dtaps, dgain_depth, dbias_depth = conv_back(
        frames, slope, dshift, depth, stats, sums, vec(10), joined, conv_normed,
        attend_resid, vec(8), gated_full, taps, masks,
    )
    slope, dao, dpq, dpk, dpv, drel, attend_vec = attention_backward(
        0, pairs, True, first_resid, slope, attend_full, tables, kept, None, windows
    )
    *first_ddown, first_dpicked, dlogits = first_back_call(
        counts, pos_row, slope, first_probs, routes_first, first_branch, first_inner, first_downs
    )
    first_ddown = scatter_parts(first_ddown, True)
    *first_dup, first_dinner = first_middle_call(
        counts, first_dpicked, first_picked, first_inner, first_ups, first_downs
    )
    first_dup = scatter_parts(first_dup, False)
    (first_dinner,) = first_ddown.step(first_dinner)
    slope, dgain_first, dbias_first, drouter_first = first_leave_call(
        counts, pos_col, first_dinner, dlogits, first_router_full, slope, inputs, first_normed, embedding,
        vec(0), first_ups,
    )
    slope, dgain_first, dbias_first, drouter_first, *matrices = advance(
        [first_ddown, first_dup], slope, dgain_first, dbias_first, drouter_first,
        dpq, dpk, dpv, drel, dao, dgated, dpoint,
    )

    def columns_of(grad):
        return (
            grad[:EXPERTS]
            .reshape(EXPERTS, devices, 2, -1)
            .transpose(1, 3, 2, 0)
            .reshape(width, 2 * EXPERTS)
        )

    small_grad = jnp.concatenate(
        [
            jnp.concatenate(
                [
                    dgain_first,
                    dbias_first,
                    dgain_second,
                    dbias_second,
                    attend_vec[2:4],
                    attend_vec[0:2],
                    dgain_depth,
                    dbias_depth,
                    final_gain_grad,
                    final_bias_grad,
                    dtaps,
                ],
                0,
            ).T,
            columns_of(drouter_first),
            columns_of(drouter_second),
        ],
        1,
    )
    n_small = small_grad.shape[1]
    small_grad = jnp.pad(small_grad, ((0, 0), (0, -n_small % 128))).astype(jnp.bfloat16)
    matrices = jnp.concatenate([*matrices, small_grad], 1)
    matrices = matrices.reshape((devices, -1) + matrices.shape[1:])
    matrices = scatter_parts(halves(matrices), False)
    (slope,) = advance([first_ddown], slope)
    (slope,) = advance([first_dup, matrices], slope)
    (slope,) = advance([first_ddown], slope)
    (slope,) = advance([matrices], slope)
    first_up_grad = first_dup.finish()
    first_down_grad = first_ddown.finish()
    matrices = matrices.finish()
    small_grad = matrices[:, 8 * width : 8 * width + n_small]
    own = small_grad.shape[0]
    start = own * lax.axis_index(AXES)
    own_sums = lax.dynamic_slice_in_dim(sums, start, own, 1)

    def vector(index):
        return small_grad[:, index]

    def router_of(start):
        block = small_grad[:, start : start + 2 * EXPERTS]
        return block.reshape(own, 2, EXPERTS).transpose(1, 0, 2).reshape(2 * own, EXPERTS)

    return (
        result,
        slope,
        vector(0),
        vector(1),
        router_of(12 + KERNEL),
        first_up_grad,
        first_down_grad,
        vector(4),
        vector(5),
        matrices[:, : 3 * width],
        matrices[:, 3 * width : 4 * width],
        vector(6),
        vector(7),
        matrices[:, 4 * width : 5 * width],
        vector(8),
        vector(9),
        matrices[:, 5 * width : 7 * width],
        small_grad[:, 12 : 12 + KERNEL].T,
        own_sums[0],
        own_sums[1],
        matrices[:, 7 * width : 8 * width],
        vector(2),
        vector(3),
        router_of(12 + KERNEL + 2 * EXPERTS),
        second_large[0],
        second_large[1],
        vector(10),
        vector(11),
    )


def solution(mesh):
    placed = (
        P(("dp", "fsdp"), None),
        P(("dp", "fsdp"), None),
        P(("dp", "fsdp"), None),
        P(("dp", "fsdp"), None),
        P(("dp", "fsdp"), None),
        P(("dp", "fsdp"), None),
        P(("dp", "fsdp")),
        P(("dp", "fsdp")),
        P(("dp", "fsdp"), None),
        P(None, ("dp", "fsdp"), None),
        P(None, ("dp", "fsdp"), None),
        P(("dp", "fsdp")),
        P(("dp", "fsdp")),
        P(("dp", "fsdp"), None),
        P(("dp", "fsdp"), None),
        P(("dp", "fsdp")),
        P(("dp", "fsdp")),
        P(("dp", "fsdp"), None),
        P(("dp", "fsdp")),
        P(("dp", "fsdp")),
        P(("dp", "fsdp"), None),
        P(None, ("dp", "fsdp")),
        P(("dp", "fsdp")),
        P(("dp", "fsdp")),
        P(("dp", "fsdp"), None),
        P(("dp", "fsdp")),
        P(("dp", "fsdp")),
        P(("dp", "fsdp"), None),
        P(None, ("dp", "fsdp"), None),
        P(None, ("dp", "fsdp"), None),
        P(("dp", "fsdp")),
        P(("dp", "fsdp")),
    )
    return jax.shard_map(
        on_device,
        mesh=mesh,
        in_specs=placed,
        out_specs=(
            P(("dp", "fsdp"), None),
            P(("dp", "fsdp"), None),
            P(("dp", "fsdp")),
            P(("dp", "fsdp")),
            P(("dp", "fsdp"), None),
            P(None, ("dp", "fsdp"), None),
            P(None, ("dp", "fsdp"), None),
            P(("dp", "fsdp")),
            P(("dp", "fsdp")),
            P(("dp", "fsdp"), None),
            P(("dp", "fsdp"), None),
            P(("dp", "fsdp")),
            P(("dp", "fsdp")),
            P(("dp", "fsdp"), None),
            P(("dp", "fsdp")),
            P(("dp", "fsdp")),
            P(("dp", "fsdp"), None),
            P(None, ("dp", "fsdp")),
            P(("dp", "fsdp")),
            P(("dp", "fsdp")),
            P(("dp", "fsdp"), None),
            P(("dp", "fsdp")),
            P(("dp", "fsdp")),
            P(("dp", "fsdp"), None),
            P(None, ("dp", "fsdp"), None),
            P(None, ("dp", "fsdp"), None),
            P(("dp", "fsdp")),
            P(("dp", "fsdp")),
        ),
        check_vma=False,
    )
```

```python
import functools

import jax
import jax.numpy as jnp
from jax import lax
from jax.experimental import pallas as pl
from jax.experimental.pallas import tpu as pltpu
from jax.sharding import PartitionSpec as P

HEADS = 8
EXPERTS = 4
KERNEL = 15
HEAD_DIM = 64
CAPACITY = 512
AXES = ("dp", "fsdp")

eps = 1e-05
blocked = -1000000000.0


def product(left, right):
    return jnp.dot(left, right, preferred_element_type=jnp.float32)


NN = (((1,), (0,)), ((), ()))
NT = (((1,), (1,)), ((), ()))
TN = (((0,), (0,)), ((), ()))


def mul(left, right, dims=NN):
    return lax.dot_general(left, right, dims, preferred_element_type=jnp.float32)


def norm_parts(value):
    average = jnp.mean(value, -1, keepdims=True)
    centered = value - average
    spread = jnp.mean(centered * centered, -1, keepdims=True)
    inverse = lax.rsqrt(spread + eps)
    return centered * inverse, inverse


def norm_slope(unit, inverse, slope, gain):
    scaled = slope * gain
    first = jnp.mean(scaled, -1, keepdims=True)
    second = jnp.mean(scaled * unit, -1, keepdims=True)
    return (scaled - first - unit * second) * inverse


def head_mask(rows, head):
    lane = lax.broadcasted_iota(jnp.int32, (rows, 2 * HEAD_DIM), 1)
    return (lane >= head * HEAD_DIM) & (lane < (head + 1) * HEAD_DIM)


def angles(length, width):
    freqs = jnp.exp(jnp.arange(0, width, 2).astype(jnp.float32) * (-jnp.log(10000.0) / width))
    coarse = (jnp.arange(length // 32) * 32).astype(jnp.float32)[:, None] * freqs[None, :]
    fine = jnp.arange(32).astype(jnp.float32)[:, None] * freqs[None, :]
    cos_a, sin_a = jnp.cos(coarse)[:, None], jnp.sin(coarse)[:, None]
    cos_b, sin_b = jnp.cos(fine)[None], jnp.sin(fine)[None]
    cosine = (cos_a * cos_b - sin_a * sin_b).reshape(length, width // 2)
    sine = (sin_a * cos_b + cos_a * sin_b).reshape(length, width // 2)
    return cosine, sine


def halves_matrix(width):
    row = lax.broadcasted_iota(jnp.int32, (width, width), 0)
    column = lax.broadcasted_iota(jnp.int32, (width, width), 1)
    half = width // 2
    source = jnp.where(row < half, 2 * row, 2 * (row - half) + 1)
    return (column == source).astype(jnp.float32).astype(jnp.bfloat16)


def attend_forward_kernel(
    windows_ref,
    resid_ref,
    gain_ref,
    bias_ref,
    pq_ref,
    pk_ref,
    pv_ref,
    rel_ref,
    cb_ref,
    pb_ref,
    segr_ref,
    segc_ref,
    tab_ref,
    cos_ref,
    sin_ref,
    ha_ref,
    qu_ref,
    qv_ref,
    k_ref,
    v_ref,
    p_ref,
    ctx_ref,
    kt_ref,
    sort_ref,
):
    length = resid_ref.shape[0]
    half = cos_ref.shape[1]
    pair = 2 * HEAD_DIM
    rows = 256

    @pl.when(pl.program_id(0) == 0)
    def first():
        unit, inverse = norm_parts(resid_ref[...])
        ha_ref[...] = (unit * gain_ref[...] + bias_ref[...]).astype(jnp.bfloat16)
        kt_ref[:, pair:] = tab_ref[...]
        sort_ref[...] = halves_matrix(rel_ref.shape[0])

    relative = mul(sort_ref[...], rel_ref[...]).astype(jnp.bfloat16)
    normed = ha_ref[...]
    query = mul(normed, pq_ref[...])
    keys = mul(normed, pk_ref[...]).astype(jnp.bfloat16)
    k_ref[...] = keys
    kt_ref[:, :pair] = keys
    v_ref[...] = mul(normed, pv_ref[...]).astype(jnp.bfloat16)
    qu_ref[...] = (query + cb_ref[...]).astype(jnp.bfloat16)
    qv_ref[...] = (query + pb_ref[...]).astype(jnp.bfloat16)

    def windowed(index, size):
        keys = pl.ds(pl.multiple_of(windows_ref[index], 128), size)
        at = pl.ds(pl.multiple_of(index * rows, rows), rows)
        same = segc_ref[at, :] == segr_ref[:, keys]
        cosine, sine = cos_ref[at, :], sin_ref[at, :]
        contexts = []
        for head in range(2):
            own = head_mask(rows, head)
            part_u = jnp.where(own, qu_ref[at, :], 0) * 0.125
            part_v = jnp.where(own, qv_ref[at, :], 0)
            coef = mul(part_v, relative, NT) * 0.125
            left, right = coef[:, :half], coef[:, half:]
            turned_a = (left * sine + right * cosine).astype(jnp.bfloat16)
            turned_b = (right * sine - left * cosine).astype(jnp.bfloat16)
            scores = mul(
                jnp.concatenate([part_u.astype(jnp.bfloat16), turned_a, turned_b], 1), kt_ref[keys, :], NT
            )
            scores = jnp.where(same, scores, blocked)
            peak = jnp.max(scores, -1, keepdims=True)
            raised = jnp.exp(scores - peak)
            summed = jnp.sum(raised, -1, keepdims=True)
            chances = (raised * (1.0 / summed)).astype(jnp.bfloat16)
            p_ref[head, at, keys] = chances
            contexts.append(mul(chances, v_ref[keys, :]))
        ctx_ref[at, :] = jnp.where(head_mask(rows, 0), contexts[0], contexts[1]).astype(jnp.bfloat16)

    def block(index, carry):
        count = windows_ref[length // rows + index]
        for size in WINDOWS:
            pl.when(count == size)(functools.partial(windowed, index, size))
        return carry

    lax.fori_loop(0, length // rows, block, 0)


def attend_backward_kernel(resumed, ends, windows_ref, *refs):
    operands = 18
    if not resumed:
        refs = refs[:operands] + (None,) + refs[operands:]
    attend_backward_body(ends, windows_ref, *refs)


def attend_backward_body(
    ends,
    windows_ref,
    p_ref,
    tab_ref,
    cos_ref,
    sin_ref,
    resid_ref,
    slope_ref,
    ha_ref,
    qu_ref,
    qv_ref,
    k_ref,
    v_ref,
    ctx_ref,
    ao_ref,
    pq_ref,
    pk_ref,
    pv_ref,
    rel_ref,
    gain_ref,
    begin_ref,
    g1_ref,
    dao_ref,
    dpq_ref,
    dpk_ref,
    dpv_ref,
    drel_ref,
    vec_ref,
    kt_ref,
    dout_ref,
    dctx_ref,
    dn_ref,
    dq_ref,
    dkt_ref,
    dvt_ref,
    drt_ref,
    sort_ref,
):
    length = resid_ref.shape[0]
    half = cos_ref.shape[1]
    pair = 2 * HEAD_DIM
    rows = 256
    step = pl.program_id(0)
    lanes = pl.ds(pl.multiple_of(step * pair, pair), pair)

    @pl.when(step == 0)
    def first():
        dout_ref[...] = slope_ref[...].astype(jnp.bfloat16)
        kt_ref[:, pair:] = tab_ref[...]
        dn_ref[...] = jnp.zeros_like(dn_ref) if begin_ref is None else begin_ref[...]
        vec_ref[...] = jnp.zeros_like(vec_ref)
        sort_ref[...] = halves_matrix(rel_ref.shape[0])

    kt_ref[:, :pair] = k_ref[...]
    relative = mul(sort_ref[...], rel_ref[...]).astype(jnp.bfloat16)
    dao_ref[...] = mul(ctx_ref[...], dout_ref[...], TN).astype(jnp.bfloat16)
    dctx_ref[...] = mul(dout_ref[...], ao_ref[...], NT).astype(jnp.bfloat16)
    dkt_ref[...] = jnp.zeros_like(dkt_ref)
    dvt_ref[...] = jnp.zeros_like(dvt_ref)
    drt_ref[...] = jnp.zeros_like(drt_ref)

    def windowed(index, size):
        keys = pl.ds(pl.multiple_of(windows_ref[index], 128), size)
        at = pl.ds(pl.multiple_of(index * rows, rows), rows)
        cosine, sine = cos_ref[at, :], sin_ref[at, :]
        total = jnp.zeros((rows, pair), jnp.float32)
        sum_u = jnp.zeros((1, pair), jnp.float32)
        sum_v = jnp.zeros((1, pair), jnp.float32)
        for head in range(2):
            own = head_mask(rows, head)
            part = jnp.where(own, dctx_ref[at, :], 0)
            low = p_ref[head, at, keys]
            chances = low.astype(jnp.float32)
            raw = mul(part, v_ref[keys, :], NT)
            weighted = chances * raw
            delta = jnp.sum(weighted, -1, keepdims=True)
            slope = ((weighted - chances * delta) * 0.125).astype(jnp.bfloat16)
            dvt_ref[:, keys] += mul(part, low, TN)
            dkt_ref[:, keys] += mul(jnp.where(own, qu_ref[at, :], 0), slope, TN)
            wide = mul(slope, kt_ref[keys, :])
            slope_u = jnp.where(own, wide[:, :pair], 0.0)
            first, second = wide[:, pair : pair + half], wide[:, pair + half :]
            coef = jnp.concatenate(
                [
                    (first * sine - second * cosine).astype(jnp.bfloat16),
                    (first * cosine + second * sine).astype(jnp.bfloat16),
                ],
                1,
            )
            slope_v = jnp.where(own, mul(coef, relative), 0.0)
            drt_ref[...] += mul(jnp.where(own, qv_ref[at, :], 0), coef, TN)
            total = total + slope_u + slope_v
            sum_u = sum_u + jnp.sum(slope_u, 0, keepdims=True)
            sum_v = sum_v + jnp.sum(slope_v, 0, keepdims=True)
        dq_ref[at, :] = total
        vec_ref[0:1, lanes] += sum_u
        vec_ref[1:2, lanes] += sum_v

    def block(index, carry):
        count = windows_ref[length // rows + index]
        for size in WINDOWS:
            pl.when(count == size)(functools.partial(windowed, index, size))
        return carry

    lax.fori_loop(0, length // rows, block, 0)
    low_q = dq_ref[...].astype(jnp.bfloat16)
    low_k = dkt_ref[...].T.astype(jnp.bfloat16)
    low_v = dvt_ref[...].T.astype(jnp.bfloat16)
    drel = drt_ref[...].T.astype(jnp.bfloat16)
    drel_ref[...] = mul(sort_ref[...], drel, TN).astype(jnp.bfloat16)
    normed = ha_ref[...]
    dpq_ref[...] = mul(normed, low_q, TN).astype(jnp.bfloat16)
    dpk_ref[...] = mul(normed, low_k, TN).astype(jnp.bfloat16)
    dpv_ref[...] = mul(normed, low_v, TN).astype(jnp.bfloat16)
    dn_ref[...] += (
        mul(low_q, pq_ref[...], NT) + mul(low_k, pk_ref[...], NT) + mul(low_v, pv_ref[...], NT)
    )

    @pl.when(step == pl.num_programs(0) - 1)
    def last():
        slope = dn_ref[...]
        if not ends:
            g1_ref[...] = slope
            return
        unit, inverse = norm_parts(resid_ref[...])
        vec_ref[2:3, :] = jnp.sum(slope * unit, 0, keepdims=True)
        vec_ref[3:4, :] = jnp.sum(slope, 0, keepdims=True)
        g1_ref[...] = slope_ref[...] + norm_slope(unit, inverse, slope, gain_ref[...])


def whole(shape):
    return pl.BlockSpec(shape, lambda p, *_: (0,) * len(shape))


def columns(rows, width, shift=0):
    return pl.BlockSpec((rows, width), lambda p, *_: (0, p + shift))


ROW_BLOCK = 256
WINDOWS = (512, 640, 768, 1024)


def key_windows(segment):
    length = segment.shape[0]
    firsts = segment[::ROW_BLOCK]
    lasts = segment[ROW_BLOCK - 1 :: ROW_BLOCK]
    start = jnp.sum(segment[None, :] < firsts[:, None], 1).astype(jnp.int32) // 128 * 128
    need = jnp.sum(segment[None, :] <= lasts[:, None], 1).astype(jnp.int32) - start
    count = jnp.full_like(need, length)
    for size in WINDOWS[::-1]:
        count = jnp.where(need <= size, size, count)
    return jnp.concatenate([jnp.minimum(start, length - count), count])


def attention_forward(first, count, resid, segments, segment_column, weights, tables, windows):
    gain, bias, packed, content_bias, position_bias = weights
    table, cosine, sine = tables
    length, width = resid.shape
    pair = 2 * HEAD_DIM
    pairs = HEADS // 2
    low = jnp.bfloat16
    shape = jax.ShapeDtypeStruct
    return pl.pallas_call(
        attend_forward_kernel,
        grid_spec=pltpu.PrefetchScalarGridSpec(
            num_scalar_prefetch=1,
            grid=(count,),
            in_specs=[
            whole((length, width)),
            pl.BlockSpec((None, 1, width), lambda p, *_: (gain[1], 0, 0)),
            pl.BlockSpec((None, 1, width), lambda p, *_: (bias[1], 0, 0)),
            columns(width, pair, first),
            columns(width, pair, first + pairs),
            columns(width, pair, first + 2 * pairs),
            columns(width, pair, first + 3 * pairs),
            pl.BlockSpec((None, 1, pair), lambda p, *_: (content_bias[1], 0, p + first)),
            pl.BlockSpec((None, 1, pair), lambda p, *_: (position_bias[1], 0, p + first)),
            whole((1, length)),
            whole((length, 1)),
            whole((length, width)),
            whole((length, width // 2)),
            whole((length, width // 2)),
        ],
        out_specs=[whole((length, width))]
        + [columns(length, pair)] * 4
        + [pl.BlockSpec((2, length, length), lambda p, *_: (p, 0, 0)), columns(length, pair)],
        scratch_shapes=[pltpu.VMEM((length, pair + width), low), pltpu.VMEM((width, width), low)],
        ),
        out_shape=[shape((length, width), low)]
        + [shape((length, count * pair), low)] * 4
        + [shape((2 * count, length, length), low), shape((length, count * pair), low)],
        compiler_params=pltpu.CompilerParams(vmem_limit_bytes=56 * 1024 * 1024),
        cost_estimate=pl.CostEstimate(flops=count * 6 * 10**9, bytes_accessed=count * 8 * 10**6, transcendentals=count * 2 * 10**6),
        name="attend_forward",
    )(
        windows,
        resid,
        gain[0],
        bias[0],
        packed,
        packed,
        packed,
        packed,
        content_bias[0],
        position_bias[0],
        segments,
        segment_column,
        table,
        cosine,
        sine,
    )


def attention_backward(first, count, last, resid, slope, weights, tables, kept, partial, windows):
    gain, bias, packed, content_bias, position_bias = weights
    table, cosine, sine = tables
    normed, query_u, query_v, keys, values, chances, context = kept
    length, width = resid.shape
    pair = 2 * HEAD_DIM
    pairs = HEADS // 2
    low, full = jnp.bfloat16, jnp.float32
    shape = jax.ShapeDtypeStruct
    begin = [] if partial is None else [partial]
    return pl.pallas_call(
        functools.partial(attend_backward_kernel, bool(begin), last),
        grid_spec=pltpu.PrefetchScalarGridSpec(
            num_scalar_prefetch=1,
            grid=(count,),
            in_specs=[
            pl.BlockSpec((2, length, length), lambda p, *_: (p + first, 0, 0)),
            whole((length, width)),
            whole((length, width // 2)),
            whole((length, width // 2)),
            whole((length, width)),
            whole((length, width)),
            whole((length, width)),
        ]
        + [columns(length, pair, first)] * 5
        + [
            pl.BlockSpec((pair, width), lambda p, *_: (p + first, pairs)),
            columns(width, pair, first),
            columns(width, pair, first + pairs),
            columns(width, pair, first + 2 * pairs),
            columns(width, pair, first + 3 * pairs),
            pl.BlockSpec((None, 1, width), lambda p, *_: (gain[1], 0, 0)),
        ]
        + [whole((length, width))] * len(begin),
        out_specs=[
            whole((length, width)),
            pl.BlockSpec((pair, width), lambda p, *_: (p, 0)),
            columns(width, pair),
            columns(width, pair),
            columns(width, pair),
            columns(width, pair),
            whole((8, width)),
        ],
        scratch_shapes=[
            pltpu.VMEM((length, pair + width), low),
            pltpu.VMEM((length, width), low),
            pltpu.VMEM((length, pair), low),
            pltpu.VMEM((length, width), full),
            pltpu.VMEM((length, pair), full),
            pltpu.VMEM((pair, length), full),
            pltpu.VMEM((pair, length), full),
            pltpu.VMEM((pair, width), full),
            pltpu.VMEM((width, width), low),
        ],
        ),
        out_shape=[shape((length, width), full), shape((count * pair, width), low)]
        + [shape((width, count * pair), low)] * 4
        + [shape((8, width), full)],
        compiler_params=pltpu.CompilerParams(vmem_limit_bytes=60 * 1024 * 1024),
        cost_estimate=pl.CostEstimate(
            flops=count * 10**10, bytes_accessed=20 * 10**6, transcendentals=0
        ),
        name="attend_backward",
    )(
        windows,
        chances,
        table,
        cosine,
        sine,
        resid,
        slope,
        normed,
        query_u,
        query_v,
        keys,
        values,
        context,
        packed,
        packed,
        packed,
        packed,
        packed,
        gain[0],
        *begin,
    )


FAST = {"z": 4, "y": 2, "x": 2, "c": 2}


def grid_of(count_dp, count_fsdp):
    depth = 4 if count_dp % 4 == 0 else count_dp
    cores = 2 if count_fsdp % 2 == 0 else 1
    return {"z": depth, "y": count_dp // depth, "x": count_fsdp // cores, "c": cores}


def sizes():
    return grid_of(lax.axis_size("dp"), lax.axis_size("fsdp"))


def place(grid, axis):
    index = lax.axis_index(AXES)
    for name in ("c", "x", "y", "z"):
        if name == axis:
            return index % grid[name]
        index = index // grid[name]


def number(grid, at):
    return ((at["z"] * grid["y"] + at["y"]) * grid["x"] + at["x"]) * grid["c"] + at["c"]


def move(value, grid, **steps):
    pairs = []
    for z in range(grid["z"]):
        for y in range(grid["y"]):
            for x in range(grid["x"]):
                for c in range(grid["c"]):
                    at = {"z": z, "y": y, "x": x, "c": c}
                    to = {name: (at[name] + steps.get(name, 0)) % grid[name] for name in at}
                    pairs.append((number(grid, at), number(grid, to)))
    return lax.ppermute(value, AXES, pairs)


PLANE = ((0, 1), (1, 0), (1, 1))


def tie(*values):
    return lax.optimization_barrier(values)


def total_of(value, beside=None):
    grid = sizes()
    if grid != FAST:
        done = beside(value) if beside else None
        return lax.psum(value, AXES), done
    value = value + move(value, grid, c=1)
    moved = [move(value, grid, y=dy, x=dx) for dy, dx in PLANE]
    done = None
    if beside:
        done = beside(value)
        *moved, done = tie(*moved, done)
    value = value + sum(moved)
    return value + sum(move(value, grid, z=step) for step in range(1, grid["z"])), done


class Chain:
    def __init__(self, steps, grid):
        self.steps, self.grid, self.value = steps, grid, None
        self.start(next(steps))

    def start(self, sends):
        self.pending = [move(value, self.grid, **how) for value, how in sends]

    def step(self, *held):
        count = len(self.pending)
        tied = tie(*self.pending, *held)
        arrived, held = tied[:count], tied[count:]
        try:
            sends = self.steps.send(list(arrived))
        except StopIteration as stop:
            self.value, self.pending = stop.value, []
            return held
        count = len(sends)
        tied = tie(*[value for value, _ in sends], *held)
        self.start([(value, how) for value, (_, how) in zip(tied[:count], sends, strict=True)])
        return tied[count:]

    def finish(self):
        while self.pending:
            try:
                self.start(self.steps.send(self.pending))
            except StopIteration as stop:
                self.value, self.pending = stop.value, []
        return self.value


class Still:
    def __init__(self, value):
        self.value, self.pending = value, []

    def step(self, *held):
        return held

    def finish(self):
        return self.value


def advance(chains, *held):
    pending = [value for chain in chains for value in chain.pending]
    tied = list(tie(*pending, *held))
    held = tied[len(pending) :]
    sends = []
    for chain in chains:
        arrived = [tied.pop(0) for _ in chain.pending]
        chain.pending = []
        if not arrived:
            sends.append([])
            continue
        try:
            sends.append(chain.steps.send(arrived))
        except StopIteration as stop:
            chain.value = stop.value
            sends.append([])
    values = [value for part in sends for value, _ in part]
    if not values:
        return held
    tied = list(tie(*values, *held))
    held = tied[len(values) :]
    for chain, part in zip(chains, sends, strict=True):
        chain.pending = [move(tied.pop(0), chain.grid, **how) for _, how in part]
    return held


def gather_steps(value, depth_first):
    value = value[None]
    plane = [{"y": dy, "x": dx} for dy, dx in PLANE]
    if depth_first:
        column = [value] + (yield [(value, {"z": step}) for step in range(1, 4)])
        value = jnp.concatenate(column, 0)
        pieces = [value] + (yield [(value, how) for how in plane])
    else:
        chips = [value] + (yield [(value, how) for how in plane])
        value = jnp.concatenate(chips, 0)
        pieces = [value]
        for _ in range(3):
            (value,) = yield [(value, {"z": 1})]
            pieces.append(value)
    return pieces + (yield [(piece, {"c": 1}) for piece in pieces])


def gathered_from(grid, depth_first):
    own = {axis: place(grid, axis) for axis in grid}
    column = [{"z": -step} for step in range(4)]
    plane = [{}] + [{"y": dy, "x": dx} for dy, dx in PLANE]
    found = []
    for core in range(2):
        for outer in plane if depth_first else column:
            for inner in column if depth_first else plane:
                at = {"c": core, **outer, **inner}
                found.append(
                    number(grid, {axis: (own[axis] + at.get(axis, 0)) % grid[axis] for axis in grid})
                )
    return jnp.stack(found)


def gather_experts(value, depth_first):
    grid = sizes()
    if grid == FAST:
        return Chain(gather_steps(value, depth_first), grid), gathered_from(grid, depth_first)
    pieces, ids = gather_whole(value)
    return Still(pieces), ids


def gather_whole(value):
    grid = sizes()
    if grid == FAST:
        blocks = lax.all_gather(value, AXES, axis=0, tiled=False)
        return [blocks], jnp.arange(blocks.shape[0], dtype=jnp.int32)
    blocks = lax.all_gather(value, AXES, axis=1, tiled=True)
    return [blocks[None]], jnp.zeros((1,), jnp.int32)


def gather_both(value):
    (blocks,), ids = gather_whole(value)
    return blocks, ids


def block_at(value, index, at):
    return lax.dynamic_index_in_dim(value, index % value.shape[at], at, keepdims=False)


def wide(value):
    return value.astype(jnp.float32)


def scatter_steps(keep, send, depth_first, grid):
    shape = (4, 2, 2) + keep.shape[1:]
    low = jnp.bfloat16
    z, y, x = (place(grid, axis) for axis in "zyx")
    (other,) = yield [(send, {"c": 1})]
    keep, other = keep.reshape(shape), other.reshape(shape)

    def near(value, at, dy, dx):
        return wide(block_at(block_at(value, y + dy, at), x + dx, at))

    def below(value, step):
        return wide(block_at(value, z + 4 - step, 0))

    if depth_first:
        part = (below(keep, 1) + below(other, 1)).astype(low)
        for step in (2, 3, 0):
            (part,) = yield [(part, {"z": 1})]
            part = (wide(part) + below(keep, step) + below(other, step)).astype(low)
        moved = yield [(near(part, 0, dy, dx).astype(low), {"y": dy, "x": dx}) for dy, dx in PLANE]
        return near(part, 0, 0, 0) + sum(wide(value) for value in moved)
    sends = [
        ((near(keep, 1, dy, dx) + near(other, 1, dy, dx)).astype(low), {"y": dy, "x": dx})
        for dy, dx in PLANE
    ]
    moved = yield sends
    column = near(keep, 1, 0, 0) + near(other, 1, 0, 0) + sum(wide(value) for value in moved)
    column = column.astype(low)
    moved = yield [(block_at(column, z + step, 0), {"z": step}) for step in range(1, 4)]
    return wide(block_at(column, z, 0)) + sum(wide(value) for value in moved)


def scatter_parts(parts, depth_first):
    grid = sizes()
    if len(parts) == 2:
        return Chain(scatter_steps(*parts, depth_first, grid), grid)
    return Still(wide(scatter_rows(by_devices(parts[0]))))


def scatter_rows(value):
    return lax.psum_scatter(value, AXES, scatter_dimension=0, tiled=False)


def halves(value):
    grid = sizes()
    if grid != FAST:
        return [value]
    value = value.reshape((16, 2) + value.shape[1:])
    core = place(grid, "c")
    return [block_at(value, core, 1), block_at(value, core + 1, 1)]


def by_devices(value):
    if value.ndim < 4:
        return value
    devices = lax.axis_size(AXES)
    return value.reshape((EXPERTS, devices, -1, value.shape[3])).transpose(1, 0, 2, 3)


def single(kernel, name, inputs, outputs, scratch, flops, size):
    values, specs = [], []
    for item in inputs:
        if not isinstance(item, tuple):
            value, block, index = item, item.shape, (0,) * item.ndim
        elif len(item) == 2:
            value, block, index = item[0], (None,) + item[0].shape[1:], (item[1], 0, 0)
        else:
            value, block, index = item
        values.append(value)
        specs.append(pl.BlockSpec(block, functools.partial(lambda index, step: index, index)))
    return pl.pallas_call(
        kernel,
        grid=(1,),
        in_specs=specs,
        out_specs=[pl.BlockSpec(o.shape, lambda step: (0, 0)) for o in outputs],
        out_shape=outputs,
        scratch_shapes=scratch,
        compiler_params=pltpu.CompilerParams(vmem_limit_bytes=60 * 1024 * 1024),
        cost_estimate=pl.CostEstimate(flops=flops, bytes_accessed=size, transcendentals=10**6),
        name=name,
    )(*values)


CHUNK = 64
EDGE = 8


def tap_masks(segments):
    half = KERNEL // 2
    segment = segments[0]
    length = segment.shape[0]
    padded = jnp.pad(segment, (half, half), constant_values=-1)
    same = [padded[k : k + length] == segment for k in range(KERNEL)]
    masks = jnp.stack(same, 1).astype(jnp.float32)
    return jnp.pad(masks, ((0, 0), (0, 128 - KERNEL)))


def conv_front_kernel(
    resid_ref, ctx_ref, ao_ref, gain_ref, bias_ref, gated_ref, taps_ref, mask_ref,
    out_ref, normed_ref, joined_ref, depth_ref, sums_ref,
    pad_ref,
):
    length, width = resid_ref.shape
    resid = resid_ref[...] + mul(ctx_ref[...], ao_ref[...])
    out_ref[...] = resid
    unit, inverse = norm_parts(resid)
    normed = (unit * gain_ref[...] + bias_ref[...]).astype(jnp.bfloat16)
    normed_ref[...] = normed
    joined = mul(normed, gated_ref[...])
    joined_ref[...] = joined
    pad_ref[:EDGE, :] = jnp.zeros((EDGE, width), jnp.float32)
    pad_ref[EDGE + length :, :] = jnp.zeros((EDGE, width), jnp.float32)
    pad_ref[EDGE : EDGE + length, :] = joined[:, :width] * sigmoid(joined[:, width:])
    sums_ref[...] = jnp.zeros_like(sums_ref)

    def chunk(index, carry):
        at = pl.ds(pl.multiple_of(index * CHUNK, CHUNK), CHUNK)
        window = pad_ref[pl.ds(pl.multiple_of(index * CHUNK, CHUNK), CHUNK + 2 * EDGE), :]
        masks = mask_ref[at, :]
        total = jnp.zeros((CHUNK, width), jnp.float32)
        for k in range(KERNEL):
            total = total + window[k + 1 : k + 1 + CHUNK] * masks[:, k : k + 1] * taps_ref[k : k + 1, :]
        depth_ref[at, :] = total
        sums_ref[0:1, :] += jnp.sum(total, 0, keepdims=True)
        sums_ref[1:2, :] += jnp.sum(total * total, 0, keepdims=True)
        return carry

    lax.fori_loop(0, length // CHUNK, chunk, 0)


def conv_front(resid, context, attend_out, gain, bias, gated_in, taps, masks):
    length, width = resid.shape
    low, full = jnp.bfloat16, jnp.float32
    shape = jax.ShapeDtypeStruct
    return single(
        conv_front_kernel,
        "conv_front",
        [resid, context, attend_out, gain, bias, gated_in, taps, masks],
        [
            shape((length, width), full),
            shape((length, width), low),
            shape((length, 2 * width), full),
            shape((length, width), full),
            shape((2, width), full),
        ],
        [pltpu.VMEM((length + 2 * EDGE, width), full)],
        4 * 10**9,
        16 * 10**6,
    )


def batch_stats(stats, frames):
    average = stats[0:1, :] * (1.0 / frames)
    spread = stats[1:2, :] * (1.0 / frames) - average * average
    return average, lax.rsqrt(spread + eps)


def conv_tail_kernel(
    frames, depth_ref, stats_ref, bgain_ref, bbias_ref, point_ref, resid_ref,
    embed_ref, router_ref, gain_ref, bias_ref,
    out_ref, normed_ref, probs_ref,
):
    average, inverse = batch_stats(stats_ref[...], frames)
    shifted = (depth_ref[...] - average) * inverse * bgain_ref[...] + bbias_ref[...]
    tail = (shifted * sigmoid(shifted)).astype(jnp.bfloat16)
    resid = resid_ref[...] + mul(tail, point_ref[...])
    out_ref[...] = resid
    unit, spread = norm_parts(resid)
    normed = (unit * gain_ref[...] + bias_ref[...]).astype(jnp.bfloat16)
    normed_ref[...] = normed
    probs_ref[...] = route_probs(normed, embed_ref[...], router_ref)


def conv_tail(frames, depth, stats, bgain, bbias, point_out, resid, embedding, router, gain, bias):
    length, width = resid.shape
    shape = jax.ShapeDtypeStruct
    return single(
        functools.partial(conv_tail_kernel, frames),
        "conv_tail",
        [depth, stats, bgain, bbias, point_out, resid, embedding, router, gain, bias],
        [
            shape((length, width), jnp.float32),
            shape((length, width), jnp.bfloat16),
            shape((length, 128), jnp.float32),
        ],
        [],
        10**9,
        8 * 10**6,
    )


def conv_turn_kernel(
    frames, slope_ref, depth_ref, stats_ref, bgain_ref, bbias_ref, point_ref,
    dshift_ref, dpoint_ref, sums_ref,
):
    average, inverse = batch_stats(stats_ref[...], frames)
    centered = (depth_ref[...] - average) * inverse
    shifted = centered * bgain_ref[...] + bbias_ref[...]
    sigma = sigmoid(shifted)
    low = slope_ref[...].astype(jnp.bfloat16)
    dpoint_ref[...] = mul((shifted * sigma).astype(jnp.bfloat16), low, TN).astype(jnp.bfloat16)
    dshift = mul(low, point_ref[...], NT) * (sigma * (1.0 + shifted * (1.0 - sigma)))
    dshift_ref[...] = dshift
    sums_ref[0:1, :] = jnp.sum(dshift * centered, 0, keepdims=True)
    sums_ref[1:2, :] = jnp.sum(dshift, 0, keepdims=True)


def conv_turn(frames, slope, depth, stats, bgain, bbias, point_out):
    length, width = slope.shape
    shape = jax.ShapeDtypeStruct
    return single(
        functools.partial(conv_turn_kernel, frames),
        "conv_turn",
        [slope, depth, stats, bgain, bbias, point_out],
        [
            shape((length, width), jnp.float32),
            shape((width, width), jnp.bfloat16),
            shape((2, width), jnp.float32),
        ],
        [],
        10**9,
        8 * 10**6,
    )


def conv_back_kernel(
    frames, slope_ref, dshift_ref, depth_ref, stats_ref, sums_ref, bgain_ref, joined_ref, normed_ref,
    resid_ref, gain_ref, gated_ref, taps_ref, mask_ref,
    out_ref, dgated_ref, dtaps_ref, dgain_ref, dbias_ref,
    pad_ref, dpad_ref, dtap_ref, dglu_ref,
):
    length, width = resid_ref.shape
    average, inverse = batch_stats(stats_ref[...], frames)
    bgain = bgain_ref[...]
    sums = sums_ref[...] * (1.0 / frames) * bgain
    centered = (depth_ref[...] - average) * inverse
    edge = jnp.zeros((EDGE, width), jnp.float32)
    left = joined_ref[:, :width]
    sigma = sigmoid(joined_ref[:, width:])
    for ref, value in (
        (pad_ref, left * sigma),
        (dpad_ref, inverse * (dshift_ref[...] * bgain - sums[1:2, :] - centered * sums[0:1, :])),
    ):
        ref[:EDGE, :] = edge
        ref[EDGE + length :, :] = edge
        ref[EDGE : EDGE + length, :] = value
    dtap_ref[...] = jnp.zeros_like(dtap_ref)

    def chunk(index, carry):
        at = pl.ds(pl.multiple_of(index * CHUNK, CHUNK), CHUNK)
        around = pl.ds(pl.multiple_of(index * CHUNK, CHUNK), CHUNK + 2 * EDGE)
        window = pad_ref[around, :]
        dwindow = dpad_ref[around, :]
        masks = mask_ref[at, :]
        middle = dwindow[EDGE : EDGE + CHUNK]
        total = jnp.zeros((CHUNK, width), jnp.float32)
        for k in range(KERNEL):
            mask = masks[:, k : k + 1]
            back = KERNEL - 1 - k
            total = total + dwindow[k + 1 : k + 1 + CHUNK] * mask * taps_ref[back : back + 1, :]
            term = window[k + 1 : k + 1 + CHUNK] * mask * middle
            dtap_ref[8 * k : 8 * k + 8, :] += jnp.sum(term.reshape(CHUNK // 8, 8, width), 0)
        dglu_ref[at, :] = total
        return carry

    lax.fori_loop(0, length // CHUNK, chunk, 0)
    for k in range(KERNEL):
        dtaps_ref[k : k + 1, :] = jnp.sum(dtap_ref[8 * k : 8 * k + 8, :], 0, keepdims=True)
    dglu = dglu_ref[...]
    low = jnp.concatenate(
        [
            (dglu * sigma).astype(jnp.bfloat16),
            (dglu * left * sigma * (1.0 - sigma)).astype(jnp.bfloat16),
        ],
        1,
    )
    dgated_ref[...] = mul(normed_ref[...], low, TN).astype(jnp.bfloat16)
    slope = mul(low, gated_ref[...], NT)
    unit, spread = norm_parts(resid_ref[...])
    dgain_ref[...] = jnp.sum(slope * unit, 0, keepdims=True)
    dbias_ref[...] = jnp.sum(slope, 0, keepdims=True)
    out_ref[...] = slope_ref[...] + norm_slope(unit, spread, slope, gain_ref[...])


def conv_back(
    frames, slope, dshift, depth, stats, sums, bgain, joined, normed, resid, gain, gated_in, taps, masks
):
    length, width = resid.shape
    full = jnp.float32
    shape = jax.ShapeDtypeStruct
    padded = pltpu.VMEM((length + 2 * EDGE, width), full)
    return single(
        functools.partial(conv_back_kernel, frames),
        "conv_back",
        [slope, dshift, depth, stats, sums, bgain, joined, normed, resid, gain, gated_in, taps, masks],
        [
            shape((length, width), full),
            shape((width, 2 * width), jnp.bfloat16),
            shape((KERNEL, width), full),
            shape((1, width), full),
            shape((1, width), full),
        ],
        [
            padded,
            padded,
            pltpu.VMEM((8 * KERNEL, width), full),
            pltpu.VMEM((length, width), full),
        ],
        6 * 10**9,
        20 * 10**6,
    )


ROWS = (256, 384, 512)


def one_hot_rows(pos_row, base, rows):
    slot = lax.broadcasted_iota(jnp.int32, (rows, pos_row.shape[1]), 0) + base
    return (slot == pos_row).astype(jnp.float32).astype(jnp.bfloat16)


def one_hot_columns(pos_col, base, rows):
    slot = lax.broadcasted_iota(jnp.int32, (pos_col.shape[0], rows), 1) + base
    return (slot == pos_col).astype(jnp.float32).astype(jnp.bfloat16)


def routed(route_col):
    lane = lax.broadcasted_iota(jnp.int32, (route_col.shape[0], 128), 1)
    return (lane == route_col).astype(jnp.float32)


def sigmoid(value):
    return 1.0 / (1.0 + jnp.exp(-value))


def split_mul(wide, narrow, dims):
    high = wide.astype(jnp.bfloat16)
    rest = (wide - high.astype(jnp.float32)).astype(jnp.bfloat16)
    return mul(high, narrow, dims) + mul(rest, narrow, dims)


def route_probs(normed, embed, router_ref):
    width = normed.shape[1]
    logits = mul(normed, router_ref[:width, :]) + mul(embed, router_ref[width:, :])
    lane = lax.broadcasted_iota(jnp.int32, logits.shape, 1)
    logits = jnp.where(lane < EXPERTS, logits, -jnp.inf)
    raised = jnp.exp(logits - jnp.max(logits, -1, keepdims=True))
    return raised / jnp.sum(raised, -1, keepdims=True)


def sized(count, body):
    lower = -1
    for rows in ROWS:
        pl.when((count > lower) & (count <= rows))(functools.partial(body, rows))
        lower = rows


def assemble(refs, ids_ref, whole_ref):
    at = 0
    for ref in refs:
        rows = ref.shape[2]
        for block in range(ref.shape[0]):
            start = pl.multiple_of(ids_ref[at] * rows, rows)
            whole_ref[pl.ds(start, rows), :] = ref[block, 0]
            at += 1


class Weights:
    def __init__(self, pieces, ids):
        self.arrays, self.ids = pieces, ids
        rows = sum(piece.shape[0] * piece.shape[2] for piece in self.arrays)
        self.shape = (rows, self.arrays[0].shape[3])
        self.rows = self.arrays[0].shape[2]

        self.scratch = [pltpu.VMEM(self.shape, jnp.bfloat16)]

    def specs(self):
        return [by_owner(piece.shape) for piece in self.arrays]

    def assemble(self, refs, ids_ref, whole_refs):
        assemble(refs, ids_ref, whole_refs[0])


class Both:
    def __init__(self, array, ids, width):
        self.arrays, self.ids = [array], ids
        devices, _, rows, hidden = array.shape
        self.rows, self.across = rows // 2, hidden // width
        self.shape = (devices * self.rows, hidden)
        down = (devices * self.rows * self.across, width)
        self.scratch = [pltpu.VMEM(self.shape, jnp.bfloat16), pltpu.VMEM(down, jnp.bfloat16)]

    def specs(self):
        return [by_owner(self.arrays[0].shape)]

    def assemble(self, refs, ids_ref, whole_refs):
        (ref,), (up_ref, down_ref) = refs, whole_refs
        rows, width = self.rows, down_ref.shape[1]
        for block in range(ref.shape[0]):
            up_ref[block * rows : (block + 1) * rows, :] = ref[block, 0, :rows, :]
            for at in range(self.across):
                start = (block * self.across + at) * rows
                down_ref[start : start + rows, :] = ref[block, 0, rows:, at * width : (at + 1) * width]


def side_by_side(up, down):
    experts, rows, hidden = up.shape
    width = down.shape[2]
    down = down.reshape(experts, hidden // width, rows, width).transpose(0, 2, 1, 3)
    return jnp.concatenate([up, down.reshape(experts, rows, hidden)], 1)


def fixed(shape):
    return pl.BlockSpec(shape, lambda e, *_: (0,) * len(shape))


def by_expert(shape):
    return pl.BlockSpec((1,) + shape, lambda e, *_: (e,) + (0,) * len(shape))


def by_owner(shape):
    return pl.BlockSpec((shape[0], 1) + shape[2:], lambda e, *_: (0, e, 0, 0))


def grads_outputs(weights):
    count = weights.shape[0] // weights.rows
    if count == 1:
        shapes = [(1, EXPERTS) + weights.shape]
    else:
        shapes = [(count // 2, EXPERTS, weights.rows, weights.shape[1])] * 2
    return [(struct(shape, jnp.bfloat16), by_owner(shape)) for shape in shapes]


def expert_call(kernel, name, counts, weights, inputs, outputs, scratch, flops, with_core=False):
    scalars = [counts] + [weight.ids for weight in weights]
    arrays = [piece for weight in weights for piece in weight.arrays]
    n_in, n_out = len(inputs), len(outputs)

    def body(*refs):
        count_ref, *ids = refs[: len(scalars)]
        refs = refs[len(scalars) :]
        pieces, refs = refs[: len(arrays)], refs[len(arrays) :]
        operands, results, rest = refs[:n_in], refs[n_in : n_in + n_out], refs[n_in + n_out :]
        expert = pl.program_id(0)
        n_whole = 0
        for at, weight in enumerate(weights):
            own = pieces[: len(weight.arrays)]
            pieces = pieces[len(weight.arrays) :]
            weight.assemble(own, ids[at], rest[n_whole : n_whole + len(weight.scratch)])
            n_whole += len(weight.scratch)
        kernel(
            expert, count_ref[expert], *rest[:n_whole], *operands, *results, *rest[n_whole:],
            **({"core": count_ref[EXPERTS]} if with_core else {}),
        )

    return pl.pallas_call(
        body,
        grid_spec=pltpu.PrefetchScalarGridSpec(
            num_scalar_prefetch=len(scalars),
            grid=(EXPERTS,),
            in_specs=[spec for weight in weights for spec in weight.specs()]
            + [spec for _, spec in inputs],
            out_specs=[spec for _, spec in outputs],
            scratch_shapes=[whole for weight in weights for whole in weight.scratch] + scratch,
        ),
        out_shape=[shape for shape, _ in outputs],
        compiler_params=pltpu.CompilerParams(vmem_limit_bytes=60 * 1024 * 1024),
        cost_estimate=pl.CostEstimate(
            flops=flops, bytes_accessed=20 * 10**6, transcendentals=4 * 10**6
        ),
        name=name,
    )(*scalars, *arrays, *[value for value, _ in inputs])


def struct(shape, dtype=jnp.float32):
    return jax.ShapeDtypeStruct(shape, dtype)


def whole_in(value):
    if isinstance(value, tuple):
        return row_in(*value)
    return (value, fixed(value.shape))


def row_in(vectors, index):
    return (vectors, pl.BlockSpec((None, 1, vectors.shape[2]), lambda e, *_: (index, 0, 0)))


def whole_out(shape, dtype=jnp.float32):
    return (struct(shape, dtype), fixed(shape))


def expert_in(value):
    return (value, by_expert(value.shape[1:]))


def expert_out(shape, dtype=jnp.bfloat16):
    return (struct((EXPERTS,) + shape, dtype), by_expert(shape))


def spans(hidden):
    chunk = 512
    return [slice(start, start + chunk) for start in range(0, hidden, chunk)]


def up_part(expert, rows, up_ref, normed_ref, posr_ref, picked_ref, inner_ref, then=None):
    hot = one_hot_rows(posr_ref[...], expert * CAPACITY, rows)
    picked = mul(hot, normed_ref[...]).astype(jnp.bfloat16)
    picked_ref[0, :rows, :] = picked
    total = None
    for span in spans(up_ref.shape[1]):
        inner = mul(picked, up_ref[:, span])
        inner_ref[0, :rows, span] = inner.astype(jnp.bfloat16)
        if then is not None:
            part = then(inner, span)
            total = part if total is None else total + part
    return total


def first_up_kernel(expert, count, up_ref, normed_ref, posr_ref, picked_ref, inner_ref):
    def run(rows):
        up_part(expert, rows, up_ref, normed_ref, posr_ref, picked_ref, inner_ref)

    sized(count, run)


def first_up_call(counts, pos_row, normed, up):
    length, width = normed.shape
    return expert_call(
        first_up_kernel,
        "first_up",
        counts,
        [up],
        [whole_in(normed), whole_in(pos_row)],
        [expert_out((CAPACITY, width)), expert_out((CAPACITY, up.shape[1]))],
        [],
        5 * 10**9,
    )


def first_down_kernel(
    expert, count, down_ref, inner_ref, posc_ref, resid_ref, probs_ref, route_ref, out_ref, branch_ref
):
    @pl.when(expert == 0)
    def clear():
        branch_ref[...] = jnp.zeros_like(branch_ref)

    def run(rows):
        total = None
        for span in spans(down_ref.shape[0]):
            inner = inner_ref[0, :rows, span].astype(jnp.float32)
            part = mul((inner * sigmoid(inner)).astype(jnp.bfloat16), down_ref[span, :])
            total = part if total is None else total + part
        hot = one_hot_columns(posc_ref[...], expert * CAPACITY, rows)
        branch_ref[...] += mul(hot, total.astype(jnp.bfloat16))

    sized(count, run)

    @pl.when(expert == EXPERTS - 1)
    def last():
        gate = jnp.sum(probs_ref[...] * routed(route_ref[...]), -1, keepdims=True)
        out_ref[...] = resid_ref[...].astype(jnp.float32) + 0.5 * gate * branch_ref[...]


def first_down_call(counts, pos_col, inner, resid, probs, routes, down):
    shape = resid.shape
    return expert_call(
        first_down_kernel,
        "first_down",
        counts,
        [down],
        [expert_in(inner)] + [whole_in(v) for v in (pos_col, resid, probs, routes)],
        [whole_out(shape), whole_out(shape)],
        [],
        5 * 10**9,
    )


def second_forward_kernel(
    expert, count, up_ref, down_ref,
    normed_ref, posr_ref, posc_ref, resid_ref, probs_ref, route_ref, cot_ref, gain_ref, bias_ref,
    picked_ref, inner_ref, branch_ref, result_ref, g4_ref, dgain_ref, dbias_ref,
):
    @pl.when(expert == 0)
    def clear():
        branch_ref[...] = jnp.zeros_like(branch_ref)

    def run(rows):
        def then(inner, span):
            return mul((inner * sigmoid(inner)).astype(jnp.bfloat16), down_ref[span, :])

        total = up_part(expert, rows, up_ref, normed_ref, posr_ref, picked_ref, inner_ref, then)
        hot = one_hot_columns(posc_ref[...], expert * CAPACITY, rows)
        branch_ref[...] += mul(hot, total.astype(jnp.bfloat16))

    sized(count, run)

    @pl.when(expert == EXPERTS - 1)
    def last():
        gate = jnp.sum(probs_ref[...] * routed(route_ref[...]), -1, keepdims=True)
        unit, inverse = norm_parts(resid_ref[...] + 0.5 * gate * branch_ref[...])
        gain = gain_ref[...]
        cot = cot_ref[...].astype(jnp.float32)
        result_ref[...] = (unit * gain + bias_ref[...]).astype(jnp.bfloat16)
        dgain_ref[...] = jnp.sum(cot * unit, 0, keepdims=True)
        dbias_ref[...] = jnp.sum(cot, 0, keepdims=True)
        g4_ref[...] = norm_slope(unit, inverse, cot, gain)


def second_forward_call(counts, pos_row, pos_col, normed, resid, probs, routes, cot, gain, bias, weights):
    length, width = normed.shape
    return expert_call(
        second_forward_kernel,
        "second_forward",
        counts,
        weights,
        [whole_in(v) for v in (normed, pos_row, pos_col, resid, probs, routes, cot, gain, bias)],
        [
            expert_out((CAPACITY, width)),
            expert_out((CAPACITY, weights[0].shape[1])),
            whole_out((length, width)),
            whole_out((length, width), jnp.bfloat16),
            whole_out((length, width)),
            whole_out((1, width)),
            whole_out((1, width)),
        ],
        [],
        10 * 10**9,
    )


def enter_slope(slope_ref, probs_ref, route_ref, branch_ref, low_ref, dlogits_ref):
    chosen = routed(route_ref[...])
    probs = probs_ref[...]
    gate = jnp.sum(probs * chosen, -1, keepdims=True)
    slope = slope_ref[...]
    low_ref[...] = (0.5 * gate * slope).astype(jnp.bfloat16)
    dgate = 0.5 * jnp.sum(slope * branch_ref[...], -1, keepdims=True)
    dlogits_ref[...] = probs * (chosen - gate) * dgate


def leave_slope(
    dnorm, dlogits, slope_ref, resid_ref, normed_ref, embed_ref, gain_ref,
    out_ref, dgain_ref, dbias_ref, drouter_ref,
):
    width = resid_ref.shape[1]
    unit, inverse = norm_parts(resid_ref[...].astype(jnp.float32))
    dgain_ref[...] = jnp.sum(dnorm * unit, 0, keepdims=True)
    dbias_ref[...] = jnp.sum(dnorm, 0, keepdims=True)
    out_ref[...] = slope_ref[...] + norm_slope(unit, inverse, dnorm, gain_ref[...])
    drouter_ref[:, :width] = split_mul(dlogits, normed_ref[...], TN)
    drouter_ref[:, width:] = split_mul(dlogits, embed_ref[...], TN)


def active_of(inner):
    inner = inner.astype(jnp.float32)
    return (inner * sigmoid(inner)).astype(jnp.bfloat16)


def slope_of(inner):
    inner = inner.astype(jnp.float32)
    sigma = sigmoid(inner)
    return sigma * (1.0 + inner * (1.0 - sigma))


def store_rows(refs, core, first, span, value):
    rows = value.shape[0]
    if len(refs) == 1:
        refs[0][0, 0, first : first + rows, span] = value
        return
    owned = refs[0].shape[2]
    value = value.reshape((rows // owned // 2, 2, 1, owned, value.shape[1]))
    at = slice(first // owned // 2, (first + rows) // owned // 2)
    for own in range(2):

        @pl.when(core == own)
        def store():
            refs[0][at, :, :, span] = value[:, own]
            refs[1][at, :, :, span] = value[:, 1 - own]


def down_grads(rows, core, inner_ref, dpicked, ddown_refs):
    for span in spans(inner_ref.shape[2]):
        grads = mul(active_of(inner_ref[0, :rows, span]), dpicked, TN)
        store_rows(ddown_refs, core, span.start, slice(None), grads.astype(jnp.bfloat16))


def up_grads(core, picked, dinner, span, dup_refs):
    store_rows(dup_refs, core, 0, span, mul(picked, dinner, TN).astype(jnp.bfloat16))


def first_back_kernel(
    expert, count, slope_ref, probs_ref, route_ref, branch_ref, posr_ref, inner_ref, *rest, core
):
    *ddown_refs, dpicked_ref, dlogits_ref, low_ref = rest

    @pl.when(expert == 0)
    def first():
        enter_slope(slope_ref, probs_ref, route_ref, branch_ref, low_ref, dlogits_ref)

    def run(rows):
        hot = one_hot_rows(posr_ref[...], expert * CAPACITY, rows)
        dpicked = mul(hot, low_ref[...]).astype(jnp.bfloat16)
        dpicked_ref[0, :rows, :] = dpicked
        down_grads(rows, core, inner_ref, dpicked, ddown_refs)

    sized(count, run)


def first_back_call(counts, pos_row, slope, probs, routes, branch, inner, down):
    length, width = slope.shape
    return expert_call(
        first_back_kernel,
        "first_down_grads",
        counts,
        [],
        [whole_in(v) for v in (slope, probs, routes, branch, pos_row)] + [expert_in(inner)],
        grads_outputs(down) + [expert_out((CAPACITY, width)), whole_out((length, 128))],
        [pltpu.VMEM((length, width), jnp.bfloat16)],
        5 * 10**9,
        True,
    )


def first_middle_kernel(expert, count, down_ref, dpicked_ref, picked_ref, inner_ref, *rest, core):
    *dup_refs, dinner_ref = rest

    def run(rows):
        dpicked = dpicked_ref[0, :rows, :]
        picked = picked_ref[0, :rows, :]
        for span in spans(inner_ref.shape[2]):
            dactive = mul(dpicked, down_ref[span, :], NT)
            dinner = (dactive * slope_of(inner_ref[0, :rows, span])).astype(jnp.bfloat16)
            dinner_ref[0, :rows, span] = dinner
            up_grads(core, picked, dinner, span, dup_refs)

    sized(count, run)


def first_middle_call(counts, dpicked, picked, inner, up, down):
    return expert_call(
        first_middle_kernel,
        "first_up_grads",
        counts,
        [down],
        [expert_in(v) for v in (dpicked, picked, inner)],
        grads_outputs(up) + [expert_out(inner.shape[1:])],
        [],
        9 * 10**9,
        True,
    )


def first_leave_kernel(
    expert, count, up_ref, dinner_ref, posc_ref, dlogits_ref, router_ref, slope_ref, resid_ref, normed_ref,
    embed_ref, gain_ref,
    out_ref, dgain_ref, dbias_ref, drouter_ref,
    dnorm_ref,
):
    width = up_ref.shape[0]

    @pl.when(expert == 0)
    def first():
        dnorm_ref[...] = split_mul(dlogits_ref[...], router_ref[:width, :], NT)

    def run(rows):
        total = mul(dinner_ref[0, :rows, :], up_ref[...], NT).astype(jnp.bfloat16)
        dnorm_ref[...] += mul(one_hot_columns(posc_ref[...], expert * CAPACITY, rows), total)

    sized(count, run)

    @pl.when(expert == EXPERTS - 1)
    def last():
        leave_slope(
            dnorm_ref[...], dlogits_ref[...], slope_ref, resid_ref, normed_ref, embed_ref, gain_ref,
            out_ref, dgain_ref, dbias_ref, drouter_ref,
        )


def first_leave_call(counts, pos_col, dinner, dlogits, router, slope, resid, normed, embedding, gain, up):
    length, width = slope.shape
    return expert_call(
        first_leave_kernel,
        "first_leave",
        counts,
        [up],
        [expert_in(dinner)]
        + [whole_in(v) for v in (pos_col, dlogits, router, slope, resid, normed, embedding, gain)],
        [
            whole_out((length, width)),
            whole_out((1, width)),
            whole_out((1, width)),
            whole_out((128, 2 * width)),
        ],
        [pltpu.VMEM((length, width), jnp.float32)],
        5 * 10**9,
    )


def second_back_kernel(
    expert, count, up_ref, down_ref, slope_ref, probs_ref, route_ref, branch_ref, posr_ref, posc_ref, inner_ref,
    router_ref, resid_ref, normed_ref, embed_ref, gain_ref,
    out_ref, dgain_ref, dbias_ref, drouter_ref, dpicked_ref, dinner_ref,
    low_ref, dlogits_ref, dnorm_ref,
):
    width = up_ref.shape[0]

    @pl.when(expert == 0)
    def first():
        enter_slope(slope_ref, probs_ref, route_ref, branch_ref, low_ref, dlogits_ref)
        dnorm_ref[...] = split_mul(dlogits_ref[...], router_ref[:width, :], NT)

    def run(rows):
        hot = one_hot_rows(posr_ref[...], expert * CAPACITY, rows)
        dpicked = mul(hot, low_ref[...]).astype(jnp.bfloat16)
        dpicked_ref[0, :rows, :] = dpicked
        total = None
        for span in spans(up_ref.shape[1]):
            dactive = mul(dpicked, down_ref[span, :], NT)
            dinner = (dactive * slope_of(inner_ref[0, :rows, span])).astype(jnp.bfloat16)
            dinner_ref[0, :rows, span] = dinner
            part = mul(dinner, up_ref[:, span], NT)
            total = part if total is None else total + part
        hot = one_hot_columns(posc_ref[...], expert * CAPACITY, rows)
        dnorm_ref[...] += mul(hot, total.astype(jnp.bfloat16))

    sized(count, run)

    @pl.when(expert == EXPERTS - 1)
    def last():
        leave_slope(
            dnorm_ref[...], dlogits_ref[...], slope_ref, resid_ref, normed_ref, embed_ref, gain_ref,
            out_ref, dgain_ref, dbias_ref, drouter_ref,
        )


def second_back_call(
    counts, pos_row, pos_col, slope, probs, routes, branch, inner, router, resid, normed, embedding, gain, weights
):
    length, width = slope.shape
    return expert_call(
        second_back_kernel,
        "second_back",
        counts,
        weights,
        [whole_in(v) for v in (slope, probs, routes, branch, pos_row, pos_col)]
        + [expert_in(inner)]
        + [whole_in(v) for v in (router, resid, normed, embedding, gain)],
        [
            whole_out((length, width)),
            whole_out((1, width)),
            whole_out((1, width)),
            whole_out((128, 2 * width)),
            expert_out((CAPACITY, width)),
            expert_out(inner.shape[1:]),
        ],
        [
            pltpu.VMEM((length, width), jnp.bfloat16),
            pltpu.VMEM((length, 128), jnp.float32),
            pltpu.VMEM((length, width), jnp.float32),
        ],
        10 * 10**9,
    )


def second_grads_kernel(expert, count, picked_ref, inner_ref, dpicked_ref, dinner_ref, out_ref):
    def run(rows):
        picked = picked_ref[0, :rows, :]
        dpicked = dpicked_ref[0, :rows, :]
        owned = out_ref.shape[2] // 2
        width = dpicked.shape[1]
        for span in spans(inner_ref.shape[2]):
            chunk = span.stop - span.start
            grads = mul(picked, dinner_ref[0, :rows, span], TN).astype(jnp.bfloat16)
            out_ref[:, :, :owned, span] = grads.reshape((-1, 1, owned, chunk))
            grads = mul(active_of(inner_ref[0, :rows, span]), dpicked, TN).astype(jnp.bfloat16)
            across = inner_ref.shape[2] // width
            if owned >= chunk:
                at = span.start // owned * width
                out_ref[0, 0, owned:, at : at + width] = grads
                continue
            first = span.start // (across * owned)
            count = chunk // (across * owned)
            grads = grads.reshape((count, 1, across, owned, width))
            for at in range(across):
                out_ref[first : first + count, :, owned:, at * width : (at + 1) * width] = grads[:, :, at]

    sized(count, run)


def second_grads_call(counts, picked, inner, dpicked, dinner, devices):
    hidden, width = inner.shape[2], picked.shape[2]
    shape = (devices, EXPERTS, 2 * width // devices, hidden)
    return expert_call(
        second_grads_kernel,
        "second_grads",
        counts,
        [],
        [expert_in(v) for v in (picked, inner, dpicked, dinner)],
        [(struct(shape, jnp.bfloat16), by_owner(shape))],
        [],
        10 * 10**9,
    )[0]


def enter_kernel(resid_ref, embed_ref, router_ref, gain_ref, bias_ref, normed_ref, probs_ref):
    unit, inverse = norm_parts(resid_ref[...].astype(jnp.float32))
    normed = (unit * gain_ref[...] + bias_ref[...]).astype(jnp.bfloat16)
    normed_ref[...] = normed
    probs_ref[...] = route_probs(normed, embed_ref[...], router_ref)


def expert_enter(resid, embedding, router, gain, bias):
    length, width = resid.shape
    return single(
        enter_kernel,
        "expert_enter",
        [resid, embedding, router, gain, bias],
        [struct((length, width), jnp.bfloat16), struct((length, 128))],
        [],
        10**9,
        4 * 10**6,
    )


def places(routes, core):
    length = routes.shape[0]
    chosen = (routes == jnp.arange(EXPERTS, dtype=jnp.int32)[None, :]).astype(jnp.float32)
    row = lax.broadcasted_iota(jnp.int32, (length, length), 0)
    before = (lax.broadcasted_iota(jnp.int32, (length, length), 1) < row).astype(jnp.bfloat16)
    earlier = product(before, chosen.astype(jnp.bfloat16))
    slot = jnp.sum(earlier * chosen, 1).astype(jnp.int32) + routes[:, 0] * CAPACITY
    counts = jnp.concatenate([jnp.sum(chosen, 0).astype(jnp.int32), core])
    return counts, slot[None, :], slot[:, None]


def gather_rows(value):
    return lax.all_gather(value, AXES, axis=0, tiled=True)


SMALL = 32
ROUTERS = 64


def small_rows(vectors, taps, first_router, second_router):
    row = lax.broadcasted_iota(jnp.int32, (SMALL, vectors[0].shape[0]), 0)
    total = jnp.pad(taps, ((len(vectors), SMALL - len(vectors) - taps.shape[0]), (0, 0)))
    for at, vector in enumerate(vectors):
        total = jnp.where(row == at, vector[None, :], total)
    total = jnp.pad(total, ((0, 0), (0, 128 - total.shape[1])))
    for at, router in ((ROUTERS, first_router), (ROUTERS + EXPERTS, second_router)):
        below, behind = SMALL - router.shape[0], 128 - at - EXPERTS
        total = total + jnp.pad(router, ((0, below), (at, behind)))
    return total


def gathered_count(devices):
    return devices if sizes() == FAST else 1


def scatter_second(value, devices, width):
    if value.shape[0] == 1:
        up = by_devices(value[:, :, :width])
        down = value[0, :, width:].reshape(EXPERTS, width, -1, width).transpose(0, 2, 1, 3)
        down = by_devices(down.reshape(1, EXPERTS, -1, width))
        return [wide(scatter_rows(part)) for part in (up, down)]
    total = wide(scatter_rows(value))
    owned = width // devices
    down = total[:, owned:].reshape(EXPERTS, owned, -1, width).transpose(0, 2, 1, 3)
    return [total[:, :owned], down.reshape(EXPERTS, -1, width)]


def on_device(
    inputs,
    embedding,
    segments,
    routes_first,
    routes_second,
    cotangent,
    first_gain,
    first_bias,
    first_router,
    first_up,
    first_down,
    attend_gain,
    attend_bias,
    project_in,
    relative_weight,
    content_bias,
    position_bias,
    attend_out,
    depth_gain,
    depth_bias,
    gated_in,
    depth_kernel,
    batch_gain,
    batch_bias,
    point_out,
    second_gain,
    second_bias,
    second_router,
    second_up,
    second_down,
    final_gain,
    final_bias,
):
    devices = lax.axis_size(AXES)
    length, width = inputs.shape
    frames = length * devices
    core = jnp.reshape(place(sizes(), "c"), (1,))

    first_up_chain, up_ids = gather_experts(first_up, True)
    first_down_chain, down_ids = gather_experts(first_down, False)
    vectors = [
        first_gain,
        first_bias,
        second_gain,
        second_bias,
        attend_gain,
        attend_bias,
        content_bias,
        position_bias,
        depth_gain,
        depth_bias,
        batch_gain,
        batch_bias,
        final_gain,
        final_bias,
    ]
    own = project_in.shape[0]
    small = small_rows(vectors, depth_kernel, first_router, second_router)
    small = jnp.concatenate([small[start : start + own] for start in range(0, SMALL, own)], 1)
    packed = gather_rows(
        jnp.concatenate([project_in, relative_weight, attend_out, point_out, gated_in, small], 1)
    )
    second = [second_up, second_down]
    if sizes() == FAST:
        second = [side_by_side(second_up, second_down)]

    first_places = places(routes_first, core)
    second_places = places(routes_second, core)
    masks = tap_masks(segments)
    segment_column = segments.reshape(length, 1)
    cosine, sine = angles(length, width)
    table = jnp.concatenate([cosine, sine], 1).astype(jnp.bfloat16)
    masks, table, cosine, sine = advance(
        [first_up_chain, first_down_chain], masks, table, cosine, sine
    )
    pos_row, pos_col = first_down_chain.step(first_places[1], first_places[2])
    tables = (table, cosine, sine)
    counts = first_places[0]

    packed, *second = first_down_chain.step(packed, *second)
    small = packed[:, 8 * width :].reshape(devices, own, SMALL // own, 128)
    small = small.transpose(0, 2, 1, 3).reshape(devices, SMALL, 128)
    n_vec = len(vectors)
    floats = small[:, :n_vec, :own].transpose(1, 0, 2).reshape(n_vec, 1, width).astype(jnp.float32)
    taps = small[:, n_vec : n_vec + KERNEL, :own].transpose(1, 0, 2)
    taps = taps.reshape(KERNEL, width).astype(jnp.float32)

    def router_wide(at):
        router = small[:, : 2 * own, at : at + EXPERTS].reshape(2 * width, EXPERTS)
        return jnp.pad(router, ((0, 0), (0, 128 - EXPERTS)))

    first_router_full = router_wide(ROUTERS)
    second_router_full = router_wide(ROUTERS + EXPERTS)

    def vec(index):
        return (floats, index)

    first_normed, first_probs = expert_enter(inputs, embedding, first_router_full, vec(0), vec(1))
    first_normed, first_probs, floats, taps, second_router_full = first_up_chain.step(
        first_normed, first_probs, floats, taps, second_router_full
    )

    windows = key_windows(segments[0])
    attend_full = (vec(4), vec(5), packed, vec(6), vec(7))
    attend_out_full = (packed, (width, width), (0, 4))
    point_full = (packed, (width, width), (0, 5))
    gated_full = (packed, (width, 2 * width), (0, 3))

    first_normed, *second = advance([first_down_chain, first_up_chain], first_normed, *second)
    first_ups = Weights(first_up_chain.finish(), up_ids)
    if sizes() == FAST:
        second_weights = [Both(*gather_both(second[0]), width)]
    else:
        second_weights = [Weights(*gather_whole(value)) for value in second]
    first_picked, first_inner = first_up_call(counts, pos_row, first_normed, first_ups)
    first_downs = Weights(first_down_chain.finish(), down_ids)
    first_resid, first_branch = first_down_call(
        counts, pos_col, first_inner, inputs, first_probs, routes_first, first_downs
    )
    pairs = HEADS // 2
    kept = attention_forward(
        0, pairs, first_resid, segments, segment_column, attend_full, tables, windows
    )
    attend_resid, conv_normed, joined, depth, stats = conv_front(
        first_resid, kept[6], attend_out_full, vec(8), vec(9), gated_full, taps, masks
    )
    stats, _ = total_of(stats)
    conv_resid, second_normed, second_probs = conv_tail(
        frames, depth, stats, vec(10), vec(11), point_full, attend_resid,
        embedding, second_router_full, vec(2), vec(3),
    )
    (
        second_picked,
        second_inner,
        second_branch,
        result,
        slope,
        final_gain_grad,
        final_bias_grad,
    ) = second_forward_call(
        *second_places, second_normed, conv_resid, second_probs, routes_second,
        cotangent, vec(12), vec(13), second_weights,
    )
    slope, dgain_second, dbias_second, drouter_second, dpicked, dinner = second_back_call(
        *second_places, slope, second_probs, routes_second, second_branch, second_inner,
        second_router_full, conv_resid, second_normed, embedding, vec(2), second_weights,
    )
    dshift, dpoint, sums = conv_turn(frames, slope, depth, stats, vec(10), vec(11), point_full)

    def deferred(sums):
        held, _ = tie(dpicked, sums)
        return second_grads_call(
            second_places[0], second_picked, second_inner, held, dinner, gathered_count(devices)
        )

    sums, second_large = total_of(sums, deferred)
    second_large = scatter_second(second_large, devices, width)
    slope, dgated, dtaps, dgain_depth, dbias_depth = conv_back(
        frames, slope, dshift, depth, stats, sums, vec(10), joined, conv_normed,
        attend_resid, vec(8), gated_full, taps, masks,
    )
    slope, dao, dpq, dpk, dpv, drel, attend_vec = attention_backward(
        0, pairs, True, first_resid, slope, attend_full, tables, kept, None, windows
    )
    *first_ddown, first_dpicked, dlogits = first_back_call(
        counts, pos_row, slope, first_probs, routes_first, first_branch, first_inner, first_downs
    )
    first_ddown = scatter_parts(first_ddown, True)
    *first_dup, first_dinner = first_middle_call(
        counts, first_dpicked, first_picked, first_inner, first_ups, first_downs
    )
    first_dup = scatter_parts(first_dup, False)
    (first_dinner,) = first_ddown.step(first_dinner)
    slope, dgain_first, dbias_first, drouter_first = first_leave_call(
        counts, pos_col, first_dinner, dlogits, first_router_full, slope, inputs, first_normed, embedding,
        vec(0), first_ups,
    )
    slope, dgain_first, dbias_first, drouter_first, *matrices = advance(
        [first_ddown, first_dup], slope, dgain_first, dbias_first, drouter_first,
        dpq, dpk, dpv, drel, dao, dgated, dpoint,
    )

    def columns_of(grad):
        return (
            grad[:EXPERTS]
            .reshape(EXPERTS, devices, 2, -1)
            .transpose(1, 3, 2, 0)
            .reshape(width, 2 * EXPERTS)
        )

    small_grad = jnp.concatenate(
        [
            jnp.concatenate(
                [
                    dgain_first,
                    dbias_first,
                    dgain_second,
                    dbias_second,
                    attend_vec[2:4],
                    attend_vec[0:2],
                    dgain_depth,
                    dbias_depth,
                    final_gain_grad,
                    final_bias_grad,
                    dtaps,
                ],
                0,
            ).T,
            columns_of(drouter_first),
            columns_of(drouter_second),
        ],
        1,
    )
    n_small = small_grad.shape[1]
    small_grad = jnp.pad(small_grad, ((0, 0), (0, -n_small % 128))).astype(jnp.bfloat16)
    matrices = jnp.concatenate([*matrices, small_grad], 1)
    matrices = matrices.reshape((devices, -1) + matrices.shape[1:])
    matrices = scatter_parts(halves(matrices), False)
    (slope,) = advance([first_ddown], slope)
    (slope,) = advance([first_dup, matrices], slope)
    (slope,) = advance([first_ddown], slope)
    (slope,) = advance([matrices], slope)
    first_up_grad = first_dup.finish()
    first_down_grad = first_ddown.finish()
    matrices = matrices.finish()
    small_grad = matrices[:, 8 * width : 8 * width + n_small]
    own = small_grad.shape[0]
    start = own * lax.axis_index(AXES)
    own_sums = lax.dynamic_slice_in_dim(sums, start, own, 1)

    def vector(index):
        return small_grad[:, index]

    def router_of(start):
        block = small_grad[:, start : start + 2 * EXPERTS]
        return block.reshape(own, 2, EXPERTS).transpose(1, 0, 2).reshape(2 * own, EXPERTS)

    return (
        result,
        slope,
        vector(0),
        vector(1),
        router_of(12 + KERNEL),
        first_up_grad,
        first_down_grad,
        vector(4),
        vector(5),
        matrices[:, : 3 * width],
        matrices[:, 3 * width : 4 * width],
        vector(6),
        vector(7),
        matrices[:, 4 * width : 5 * width],
        vector(8),
        vector(9),
        matrices[:, 5 * width : 7 * width],
        small_grad[:, 12 : 12 + KERNEL].T,
        own_sums[0],
        own_sums[1],
        matrices[:, 7 * width : 8 * width],
        vector(2),
        vector(3),
        router_of(12 + KERNEL + 2 * EXPERTS),
        second_large[0],
        second_large[1],
        vector(10),
        vector(11),
    )


def solution(mesh):
    placed = (
        P(("dp", "fsdp"), None),
        P(("dp", "fsdp"), None),
        P(("dp", "fsdp"), None),
        P(("dp", "fsdp"), None),
        P(("dp", "fsdp"), None),
        P(("dp", "fsdp"), None),
        P(("dp", "fsdp")),
        P(("dp", "fsdp")),
        P(("dp", "fsdp"), None),
        P(None, ("dp", "fsdp"), None),
        P(None, ("dp", "fsdp"), None),
        P(("dp", "fsdp")),
        P(("dp", "fsdp")),
        P(("dp", "fsdp"), None),
        P(("dp", "fsdp"), None),
        P(("dp", "fsdp")),
        P(("dp", "fsdp")),
        P(("dp", "fsdp"), None),
        P(("dp", "fsdp")),
        P(("dp", "fsdp")),
        P(("dp", "fsdp"), None),
        P(None, ("dp", "fsdp")),
        P(("dp", "fsdp")),
        P(("dp", "fsdp")),
        P(("dp", "fsdp"), None),
        P(("dp", "fsdp")),
        P(("dp", "fsdp")),
        P(("dp", "fsdp"), None),
        P(None, ("dp", "fsdp"), None),
        P(None, ("dp", "fsdp"), None),
        P(("dp", "fsdp")),
        P(("dp", "fsdp")),
    )
    return jax.shard_map(
        on_device,
        mesh=mesh,
        in_specs=placed,
        out_specs=(
            P(("dp", "fsdp"), None),
            P(("dp", "fsdp"), None),
            P(("dp", "fsdp")),
            P(("dp", "fsdp")),
            P(("dp", "fsdp"), None),
            P(None, ("dp", "fsdp"), None),
            P(None, ("dp", "fsdp"), None),
            P(("dp", "fsdp")),
            P(("dp", "fsdp")),
            P(("dp", "fsdp"), None),
            P(("dp", "fsdp"), None),
            P(("dp", "fsdp")),
            P(("dp", "fsdp")),
            P(("dp", "fsdp"), None),
            P(("dp", "fsdp")),
            P(("dp", "fsdp")),
            P(("dp", "fsdp"), None),
            P(None, ("dp", "fsdp")),
            P(("dp", "fsdp")),
            P(("dp", "fsdp")),
            P(("dp", "fsdp"), None),
            P(("dp", "fsdp")),
            P(("dp", "fsdp")),
            P(("dp", "fsdp"), None),
            P(None, ("dp", "fsdp"), None),
            P(None, ("dp", "fsdp"), None),
            P(("dp", "fsdp")),
            P(("dp", "fsdp")),
        ),
        check_vma=False,
    )
```
